128 devices in a mesh: shard: 128 (over x, z, y, core).
Axes of the slice: x: 4, y: 4, z: 4, core: 2. Of those that a mesh axis runs over, the one named last changes fastest.
Arguments:
- queries: bfloat16 [32768, 256], P('shard')
- clusters: int32 [32768, 8], P('shard'), may hold values from 0 to 2047, all different within a row; in each aligned block of 256 rows (0 to 255, 256 to 511, ...) at most 2 rows name the same one
- placement: int32 [2048], replicated, may hold values from 0 to 2047, each once
- pos_pick: int32 [32768], P('shard'), may hold values from 0 to 7
- pos_row: int32 [32768], P('shard'), may hold values from 0 to 255
- counts: int32 [2048], P('shard'), may hold values from 1 to 256, as said below
- labels: bfloat16 [2048, 256, 256], P('shard'), may hold values from -6 to 6
- accum: float32 [2048, 256], P('shard'), may hold values from 0.01 to 1
Outputs:
- new_labels: float32 [2048, 256, 256], P('shard')
- new_accum: float32 [2048, 256], P('shard')
- query_grad: bfloat16 [32768, 256], P('shard')
- loss: float32 [32768], P('shard')
The draws below stay inside these ranges and needn't reach their ends.
Inputs may be any that keep to these rules, and one draw needn't show every extreme that they name: A query's 8 clusters are distinct; among the queries of one device no cluster is named more than 2 times, a bound that some block reaches. `counts`: some block has all 256 rows valid.
All inputs are finite; a program needn't handle non-finite values.
Results may differ from the reference program's by a relative error of at most 0.0031.
Values may be sent and summed in bfloat16 or wider, within the bound.
No kernel may reach another device: no remote copies, remote signals or barrier semaphores. Data moves between devices by JAX's collectives and lax.ppermute only.
A program may use at most 64 MiB of HBM per device.

```python
import math
import jax
import jax.numpy as jnp
import numpy as np
from jax import lax

W = 256
BLOCK = 256
TOPC = 8
CL_DEV = 16
Q_DEV = 256
CLUSTERS = 2048
QUERIES = 32768
MOST = 2
N_SHARD = 128


def draw_queries(key, part):
    key = jax.random.fold_in(key, 5)
    key_base, key_scale = jax.random.split(key)
    base = jax.random.normal(key_base, (QUERIES, W), jnp.float32)
    spread = jnp.exp(jax.random.uniform(key_scale, (QUERIES,), jnp.float32, math.log(0.3), math.log(3.0)))
    return (base * spread[:, None] * W ** (-0.5)).astype(jnp.bfloat16)


def draw_counts(key, part):
    key = jax.random.fold_in(key, 7)
    key_rows, key_full = jax.random.split(key)
    valid_rows = jax.random.randint(key_rows, (CLUSTERS,), 1, BLOCK + 1, jnp.int32)
    chosen = jax.random.randint(key_full, (), 0, CLUSTERS, jnp.int32)
    return valid_rows.at[chosen].set(BLOCK)


def with_ends(result, own_key, least, high):
    place = [jax.random.randint(jax.random.fold_in(own_key, axis), (), 0, length) for axis, length in enumerate(result.shape)]
    main_axis = result.shape.index(max(result.shape))
    beside = place[:main_axis] + [(place[main_axis] + 1) % result.shape[main_axis]] + place[main_axis + 1:]
    return result.at[tuple(place)].set(least).at[tuple(beside)].set(high)


def level_of(rng, extent, shards, low, high):
    level = 1.0
    for dim, blocks in shards:
        steps = jax.random.uniform(jax.random.fold_in(jax.random.fold_in(rng, 6), dim), (blocks,), jnp.float32, low / len(shards), high / len(shards))
        level = level * jnp.repeat(jnp.exp(steps), extent[dim] // blocks).reshape((-1,) + (1,) * (len(extent) - 1 - dim))
    return level


def assign_block(stream_key, own, number, rows, amount, top, most, skew):
    order = jax.random.permutation(stream_key, amount)
    crowded, ordinary = shares(amount, rows * top, most, skew, True), shares(amount, rows * top, most, skew, False)
    places = jnp.arange(amount)

    def named(lengths, turn):
        used = int((lengths > 0).sum())
        fixed = max(1, used // 4)
        shifted = fixed + (places - fixed + turn * (used - fixed)) % max(1, amount - fixed)
        return jnp.zeros((amount,), jnp.int32).at[order[jnp.where(places < fixed, places, shifted)]].set(jnp.asarray(lengths, jnp.int32))

    lengths = jnp.where(number % 4 == 0, named(crowded, number // 4), named(ordinary, number - number // 4 - 1))
    mixed = jax.random.permutation(jax.random.fold_in(own, 3), amount)
    giver, receiver = mixed[0:amount // 2 * 2:2], mixed[1:amount // 2 * 2:2]
    slack = jnp.minimum(lengths[giver] - 1, most - lengths[receiver]) // 2
    slack = jnp.where((giver == order[0]) | (receiver == order[0]) | (lengths[receiver] == 0), 0, jnp.maximum(slack, 0))
    shifted = jax.random.randint(jax.random.fold_in(own, 4), (amount // 2,), 0, 1 << 20) % (slack + 1)
    lengths = lengths.at[giver].add(-shifted).at[receiver].add(shifted)
    items = jnp.searchsorted(jnp.cumsum(lengths), jnp.arange(rows * top), side="right").astype(jnp.int32)
    listing = items.reshape(top, rows).T
    listing = listing[jax.random.permutation(jax.random.fold_in(own, 1), rows)]
    turn = jax.random.randint(jax.random.fold_in(own, 2), (rows, 1), 0, top)
    return jnp.take_along_axis(listing, (jnp.arange(top)[None, :] + turn) % top, axis=1)


def shares(amount, total, most, lean, full):
    weights = [(1 << 20) // math.isqrt(rank ** lean) + 1 for rank in range(1, amount + 1)]
    largest = most if full else min(most, max(-(-total // amount), total * weights[0] // sum(weights)))
    least = 1 if total - largest >= amount - 1 else 0
    given, spare = [largest] + [least] * (amount - 1), total - largest - least * (amount - 1)
    while spare > 0:
        movable = [i for i in range(1, amount) if given[i] < largest] or [i for i in range(1, amount) if given[i] < most]
        mass, remaining = sum([weights[i] for i in movable]), spare
        for i in movable:
            addition = min(most - given[i], max(1, remaining * weights[i] // mass), spare)
            given[i] = given[i] + addition
            spare = spare - addition
    return np.array(given)


def centred(key, shape, scale, bound, cuts=(), kind=jnp.bfloat16):
    values = jax.random.normal(key, shape, jnp.float32) * scale
    if len(cuts) > 0:
        values = level_of(key, shape, cuts, -0.22, 0.18) * values
    return jnp.clip(values, min=-bound, max=bound).astype(kind)


def setup_inputs(seed: int = 0) -> dict:
    seeds = jax.random.split(jax.random.key(seed), 9)
    queries = draw_queries(jax.random.fold_in(seeds[8], 71), 0)
    clusters_keys = jax.random.split(jax.random.fold_in(seeds[1], 1), QUERIES // Q_DEV)
    clusters_turns = jax.random.permutation(jax.random.fold_in(seeds[1], 3), QUERIES // Q_DEV)
    clusters = jax.vmap(lambda own, number: assign_block(jax.random.fold_in(seeds[1], 2), own, number, Q_DEV, CLUSTERS, TOPC, MOST, 2))(clusters_keys, clusters_turns).reshape((QUERIES, TOPC))
    placement = jax.random.permutation(seeds[2], CLUSTERS).astype(jnp.int32)
    pos_pick = with_ends(jax.random.randint(seeds[3], (QUERIES,), 0, TOPC), jax.random.fold_in(seeds[3], 1), 0, TOPC - 1).astype(jnp.int32)
    pos_row = with_ends(jax.random.randint(seeds[4], (QUERIES,), 0, BLOCK), jax.random.fold_in(seeds[4], 1), 0, BLOCK - 1).astype(jnp.int32)
    counts = draw_counts(jax.random.fold_in(seeds[8], 71), 0)
    labels = centred(seeds[6], (CLUSTERS, BLOCK, W), 1.0, 6.0, ((0, 128),))
    accum = jnp.clip(jnp.exp(math.log(1.0) - 4.6051702 * jax.random.uniform(seeds[7], (CLUSTERS, BLOCK), jnp.float32) ** level_of(seeds[7], (CLUSTERS, BLOCK), ((0, 128),), -0.2, 0.2)), 0.01, 1.0)
    return {"queries": queries, "clusters": clusters, "placement": placement, "pos_pick": pos_pick, "pos_row": pos_row, "counts": counts, "labels": labels, "accum": accum}


step_rate = 0.1

def ranks_of(keys):
    order = jnp.argsort(keys, stable=True)
    sorted_keys = keys[order]
    places = jnp.arange(keys.shape[0], dtype=jnp.int32)
    starts = jnp.where((places == 0) | (sorted_keys != jnp.roll(sorted_keys, 1)), places, 0)
    starts = lax.cummax(starts)
    return jnp.zeros_like(keys).at[order].set(places - starts)

def reference(queries, clusters, placement, pos_pick, pos_row, counts, labels, accum):
    slots = N_SHARD * MOST
    flat = clusters.reshape(-1)
    owners = jnp.repeat(jnp.arange(QUERIES, dtype=jnp.int32) // Q_DEV, TOPC)
    rank = ranks_of(owners * CLUSTERS + flat)
    blocks = placement[flat]
    where_to = (blocks * N_SHARD + owners) * MOST + rank
    picked = jnp.arange(TOPC, dtype=jnp.int32)[None, :] == pos_pick[:, None]
    target = jnp.where(picked, pos_row[:, None], -1).reshape(-1)
    buf_q = jnp.zeros((CLUSTERS * slots, W), jnp.bfloat16).at[where_to].set(jnp.repeat(queries, TOPC, axis=0))
    buf_t = jnp.full((CLUSTERS * slots,), -1, jnp.int32).at[where_to].set(target)
    groups = CLUSTERS // CL_DEV
    grp_q = buf_q.reshape(groups, CL_DEV, slots, W)
    grp_t = buf_t.reshape(groups, CL_DEV, slots)
    grp_e = labels.reshape(groups, CL_DEV, BLOCK, W)
    grp_c = counts.reshape(groups, CL_DEV)
    grp_a = accum.reshape(groups, CL_DEV, BLOCK)
    rows = jnp.arange(BLOCK, dtype=jnp.int32)

    def scores(block_q, block_e):
        return jnp.einsum('cmw,clw->cml', block_q.astype(jnp.float32), block_e.astype(jnp.float32))

    def first_pass(items):
        block_q, block_t, block_e, block_c = items
        score = scores(block_q, block_e)
        valid = (rows[None, :] < block_c[:, None])[:, None, :]
        masked = jnp.where(valid, score, -jnp.inf)
        top = lax.optimization_barrier(jnp.max(masked, axis=-1))
        total = lax.optimization_barrier(jnp.sum(jnp.exp(masked - top[..., None]), axis=-1))
        trow = jnp.where(block_t >= 0, block_t % block_c[:, None], -1)
        hit = rows[None, None, :] == trow[..., None]
        spos = lax.optimization_barrier(jnp.sum(jnp.where(hit, score, 0.0), axis=-1))
        return (top, total, spos)
    tops, totals, sposs = lax.map(first_pass, (grp_q, grp_t, grp_e, grp_c))
    pair_m = tops.reshape(-1)[where_to].reshape(QUERIES, TOPC)
    pair_z = totals.reshape(-1)[where_to].reshape(QUERIES, TOPC)
    pair_s = sposs.reshape(-1)[where_to].reshape(QUERIES, TOPC)
    largest = lax.optimization_barrier(jnp.max(pair_m, axis=1))
    norm = lax.optimization_barrier(jnp.sum(pair_z * jnp.exp(pair_m - largest[:, None]), axis=1))
    lse = largest + jnp.log(norm)
    loss = lse - lax.optimization_barrier(jnp.sum(pair_s, axis=1))
    buf_l = jnp.zeros((CLUSTERS * slots,), jnp.float32).at[where_to].set(jnp.repeat(lse, TOPC))
    grp_l = buf_l.reshape(groups, CL_DEV, slots)

    def second_pass(items):
        block_q, block_t, block_e, block_c, block_a, block_l = items
        score = scores(block_q, block_e)
        valid = (rows[None, :] < block_c[:, None])[:, None, :]
        masked = jnp.where(valid, score, -jnp.inf)
        top = lax.optimization_barrier(jnp.max(masked, axis=-1))
        trow = jnp.where(block_t >= 0, block_t % block_c[:, None], -1)
        hit = rows[None, None, :] == trow[..., None]
        prob = jnp.where(valid, jnp.exp(score - block_l[..., None]), 0.0)
        dlogit = (prob - hit.astype(jnp.float32)).astype(jnp.bfloat16)
        label_grad = jnp.einsum('cml,cmw->clw', dlogit.astype(jnp.float32), block_q.astype(jnp.float32))
        weight = jnp.where(valid, jnp.exp(score - top[..., None]), 0.0).astype(jnp.bfloat16)
        part = jnp.einsum('cml,clw->cmw', weight.astype(jnp.float32), block_e.astype(jnp.float32)).astype(jnp.bfloat16)
        new_acc = block_a + lax.optimization_barrier(jnp.mean(label_grad * label_grad, axis=-1))
        new_tab = block_e.astype(jnp.float32) - step_rate * label_grad / jnp.sqrt(new_acc)[..., None]
        return (new_tab, new_acc, part)
    new_tab, new_acc, parts = lax.map(second_pass, (grp_q, grp_t, grp_e, grp_c, grp_a, grp_l))
    pieces = parts.reshape(CLUSTERS * slots, W)[where_to].astype(jnp.float32).reshape(QUERIES, TOPC, W)
    scale = jnp.exp(pair_m - lse[:, None])
    pos_cluster = lax.optimization_barrier(jnp.sum(jnp.where(picked, clusters, 0), axis=1))
    pos_block = placement[pos_cluster]
    pos_index = pos_row % counts[pos_block]
    pos_vec = labels[pos_block, pos_index].astype(jnp.float32)
    query_grad = (lax.optimization_barrier(jnp.sum(pieces * scale[..., None], axis=1)) - pos_vec).astype(jnp.bfloat16)
    return (new_tab.reshape(CLUSTERS, BLOCK, W), new_acc.reshape(CLUSTERS, BLOCK), query_grad, loss)
```

```python
import jax
import jax.numpy as jnp
from jax import lax
from jax.experimental import pallas as pl
from jax.experimental.pallas import tpu as pltpu
from jax.sharding import PartitionSpec as P

STEP_RATE = 0.1
DEVS = 128
GROUP = 8
SLOTS = 32
CHUNK = 72
BLOCK = GROUP * CHUNK
NGROUPS = DEVS // GROUP
f32 = jnp.float32
bf16 = jnp.bfloat16
i32 = jnp.int32


def iota(shape, dim):
    return lax.broadcasted_iota(i32, shape, dim)


def one(mask):
    return jnp.where(mask, 1.0, 0.0).astype(bf16)


def dot(a, b, ca=1, cb=0):
    return lax.dot_general(a, b, (((ca,), (cb,)), ((), ())), preferred_element_type=f32)


def pieces_of(x):
    hi = x.astype(bf16).astype(f32)
    rest = x - hi
    mid = rest.astype(bf16).astype(f32)
    return hi, mid, rest - mid


def total(x):
    return jnp.sum(x, axis=0, keepdims=True)


def to_rows(rows, extra):
    left = rows[:, :128].reshape(GROUP, SLOTS, 128)
    right = rows[:, 128:].reshape(GROUP, SLOTS, 128)
    return jnp.concatenate([left, right, extra], axis=1).reshape(BLOCK, 128).astype(bf16)


def from_rows(ref, group):
    block = ref[pl.ds(pl.multiple_of(group * BLOCK, BLOCK), BLOCK), :]
    return block.astype(f32).reshape(GROUP, CHUNK, 128)


def slot_rows(block):
    left = block[:, :SLOTS].reshape(GROUP * SLOTS, 128)
    right = block[:, SLOTS : 2 * SLOTS].reshape(GROUP * SLOTS, 128)
    return jnp.concatenate([left, right], axis=1).astype(bf16)


def route_kernel(cl_ref, place_ref, pick_ref, row_ref, q_ref, send_ref, sid_ref, ext_scr):
    c = cl_ref[...]
    ch, cl = c >> 7, c & 127
    place = place_ref[...]
    table = jnp.concatenate([(place >> 4).astype(f32), (place & 15).astype(f32)], axis=0).astype(bf16)
    i128, i16, i32s = iota((128, 256), 0), iota((16, 256), 0), iota((32, 256), 0)
    query = iota((1, 256), 1)
    queryf = query.astype(f32)
    ds, ls, ohs = [], [], []
    acc = jnp.zeros((32, 128), f32)
    for k in range(8):
        got = dot(table, one(i128 == cl[k : k + 1]))
        mine = i16 == ch[k : k + 1]
        d = total(jnp.where(mine, got[:16], 0.0)).astype(i32)
        l = total(jnp.where(mine, got[16:], 0.0)).astype(i32)
        oh = one(i128 == d)
        is_l = i16 == l
        named = jnp.concatenate([jnp.where(is_l, 1.0, 0.0), jnp.where(is_l, queryf, 0.0)], axis=0)
        acc = acc + dot(named.astype(bf16), oh, 1, 1)
        ds.append(d)
        ls.append(l)
        ohs.append(oh)
    count = acc[:16]
    middle = jnp.where(count > 1.5, jnp.floor(acc[16:] * 0.5), 255.0).astype(bf16)
    rls, sids = [], []
    for k in range(8):
        got = dot(middle, ohs[k])
        border = total(jnp.where(i16 == ls[k], got, 0.0)).astype(i32)
        rl = jnp.where(query > border, 16, 0) + ls[k]
        rls.append(rl)
        sids.append(ds[k] * SLOTS + rl)
    pick = pick_ref[...]
    dp = jnp.zeros((1, 256), i32)
    rlp = jnp.zeros((1, 256), i32)
    for k in range(8):
        dp = jnp.where(pick == k, ds[k], dp)
        rlp = jnp.where(pick == k, rls[k], rlp)
    ohp = one(i128 == dp)
    before = one(iota((256, 256), 0) < iota((256, 256), 1))
    j = total(ohp.astype(f32) * dot(ohp, before)).astype(i32)
    w_t = jnp.where(i32s == rlp, (row_ref[...] + 1).astype(f32), 0.0)
    w_j = jnp.where(i32s == j, (rlp + 1).astype(f32), 0.0)
    res = dot(jnp.concatenate([w_t, w_j, jnp.ones((8, 256), f32)], axis=0).astype(bf16), ohp, 1, 1)
    want = res[64:65]
    free = jnp.where(jnp.concatenate([count, count - 1.0], axis=0) < 0.5, 1.0, 0.0)
    lower = one(iota((32, 32), 1) < iota((32, 32), 0))
    turn = dot(lower, free.astype(bf16))
    turn = jnp.where(free > 0.5, turn, 99.0)
    code = jnp.zeros((32, 128), f32)
    for s in range(SLOTS):
        code = jnp.where(turn == float(s), res[32 + s : 33 + s], code)
    short = jnp.max(jnp.where(want > total(free), 1.0, 0.0), axis=1, keepdims=True)
    got = dot(turn.astype(bf16), ohp)
    carrier = total(jnp.where(got == j.astype(f32), i32s.astype(f32), 0.0)).astype(i32)
    ext = jnp.concatenate([res[:32], code, jnp.broadcast_to(short, (64, 128))], axis=0)
    ext_scr[...] = ext.T
    sid_ref[...] = jnp.concatenate(
        sids + [dp * SLOTS + carrier, dp * SLOTS + rlp] + [jnp.zeros((1, 256), i32)] * 6, axis=0
    )

    def group(g, _):
        slot = iota((256, 256), 0) + g * 256
        mask = slot == sid_ref[0:1, :]
        for k in range(1, 8):
            mask = mask | (slot == sid_ref[k : k + 1, :])
        rows = dot(one(mask), q_ref[...])
        extra = ext_scr[pl.ds(pl.multiple_of(g * GROUP, GROUP), GROUP), :]
        extra = jnp.broadcast_to(extra[:, None, :], (GROUP, 8, 128))
        send_ref[pl.ds(pl.multiple_of(g * BLOCK, BLOCK), BLOCK), :] = to_rows(rows, extra)
        return 0

    lax.fori_loop(0, NGROUPS, group, 0, unroll=2)


def by_slot(x):
    second = pltpu.roll(x, 112, 1)
    both = jnp.concatenate(
        [x.reshape(NGROUPS, 1, GROUP, 128), second.reshape(NGROUPS, 1, GROUP, 128)], axis=1
    )
    return both.reshape(256, 128).T


def owner_kernel(
    counts_ref, cc_ref, recv_ref, lab_ref, x_ref, tr_ref, flag_ref, send_ref,
    ext_scr, part_scr, pos_scr, stat_scr, back_scr,
):
    r256, c256 = iota((256, 256), 0), iota((256, 256), 1)
    sent = (r256 & 7) * 32 + ((r256 >> 3) & 1) * 16 + (r256 >> 4)
    perm = one(c256 == sent)

    def gather(g, _):
        block = from_rows(recv_ref, g)
        x = dot(perm, slot_rows(block)).astype(bf16)
        for l in range(16):
            x_ref[l, pl.ds(pl.multiple_of(g * 16, 16), 16), :] = x[l * 16 : (l + 1) * 16]
        ext_scr[pl.ds(pl.multiple_of(g * 64, 64), 64), :] = block[:, 64:72].reshape(64, 128)
        return 0

    lax.fori_loop(0, NGROUPS, gather, 0, unroll=2)
    ext = ext_scr[pl.ds(0, 128, stride=8), :]
    slots = by_slot(ext)
    flag_ref[...] = jnp.broadcast_to(jnp.max(slots[64:65], axis=1, keepdims=True), (8, 128))
    raw = slots[:16] - 1.0
    cc = cc_ref[...]
    tr_ref[...] = jnp.where(raw > -0.5, raw - cc * jnp.floor((raw + 0.5) / cc), -1.0)
    stat_scr[...] = jnp.zeros((64, 256), f32)

    def cluster(l, _):
        lab = lab_ref[l]
        score = dot(lab, x_ref[l], 1, 1)
        masked = jnp.where(r256 < counts_ref[l], score, -jnp.inf)
        top = jnp.max(masked, axis=0, keepdims=True)
        weight = jnp.exp(masked - top)
        hit = r256.astype(f32) == tr_ref[pl.ds(l, 1), :]
        stat_scr[pl.ds(l, 1), :] = top
        stat_scr[pl.ds(l + 16, 1), :] = total(weight)
        stat_scr[pl.ds(l + 32, 1), :] = total(jnp.where(hit, score, 0.0))
        part_scr[l] = dot(weight.astype(bf16), lab, 0, 0).astype(bf16)
        pos_scr[l] = dot(one(hit), lab, 0, 0).astype(bf16)
        return 0

    lax.fori_loop(0, 16, cluster, 0, unroll=2)
    hi, mid, lo = pieces_of(stat_scr[...])
    first = jnp.concatenate([hi, mid], axis=0).T.reshape(NGROUPS, 2, GROUP, 128)
    second = jnp.concatenate([lo, jnp.zeros((64, 256), f32)], axis=0).T.reshape(NGROUPS, 2, GROUP, 128)
    back_scr[...] = jnp.zeros((1024, 128), f32)
    for r in range(2):
        back_scr[pl.ds(2 * r, 128, stride=8), :] = first[:, r].reshape(128, 128)
        back_scr[pl.ds(2 * r + 1, 128, stride=8), :] = second[:, r].reshape(128, 128)

    back = (c256 & 7) * 32 + ((c256 >> 3) & 1) * 16 + (c256 >> 4)
    unperm = one(r256 == back)
    wanted = jnp.where((r256 >> 5) == (c256 & 7), (back & 31) + 1, -1).astype(f32)
    own_lane = iota((256, 128), 1) == 32 + (iota((256, 128), 0) & 31)
    ones = jnp.ones((128, 256), bf16)

    def scatter(g, _):
        at = pl.ds(pl.multiple_of(g * 16, 16), 16)
        parts = jnp.concatenate([part_scr[l, at, :] for l in range(16)], axis=0)
        pos = jnp.concatenate([pos_scr[l, at, :] for l in range(16)], axis=0)
        codes = ext_scr[pl.ds(pl.multiple_of(g * 64, 64), 64), :].reshape(GROUP, 8, 128)
        codes = jnp.concatenate([codes] * 4, axis=1).reshape(256, 128)
        code = dot(jnp.where(own_lane, codes, 0.0).astype(bf16), ones)
        rows = jnp.where(code > 0.5, dot(one(code == wanted), pos), dot(unperm, parts))
        extra = back_scr[pl.ds(pl.multiple_of(g * 64, 64), 64), :].reshape(GROUP, 8, 128)
        send_ref[pl.ds(pl.multiple_of(g * BLOCK, BLOCK), BLOCK), :] = to_rows(rows, extra)
        return 0

    lax.fori_loop(0, NGROUPS, scatter, 0, unroll=2)


def lse_kernel(recv_ref, sid_ref, loss_ref, send_ref, scale_ref, ext_scr):
    def take(g, _):
        block = from_rows(recv_ref, g)
        ext_scr[pl.ds(pl.multiple_of(g * 64, 64), 64), :] = block[:, 64:72].reshape(64, 128)
        return 0

    lax.fori_loop(0, NGROUPS, take, 0, unroll=2)
    stats = []
    for r in range(2):
        first = ext_scr[pl.ds(2 * r, 128, stride=8), :]
        second = ext_scr[pl.ds(2 * r + 1, 128, stride=8), :]
        stats.append(first + pltpu.roll(first, 64, 1) + second)
    both = jnp.where(iota((128, 128), 1) < 64, stats[0], pltpu.roll(stats[1], 64, 1)).T
    table = jnp.concatenate(pieces_of(both), axis=0).astype(bf16)
    i128, i16, i32s = iota((128, 256), 0), iota((16, 256), 0), iota((32, 256), 0)
    sid = sid_ref[...]
    tops, sums, ohs = [], [], []
    target = jnp.zeros((1, 256), f32)
    for k in range(8):
        s = sid[k : k + 1]
        oh = one(i128 == (s >> 5))
        got = dot(table, oh)
        got = got[:128] + got[128:256] + got[256:]
        got = jnp.where((s & 16) == 0, got[:48], got[64:112])
        mine = i16 == (s & 15)
        tops.append(total(jnp.where(mine, got[:16], 0.0)))
        sums.append(total(jnp.where(mine, got[16:32], 0.0)))
        target = target + total(jnp.where(mine, got[32:48], 0.0))
        ohs.append(oh)
    largest = tops[0]
    for k in range(1, 8):
        largest = jnp.maximum(largest, tops[k])
    norm = sums[0] * jnp.exp(tops[0] - largest)
    for k in range(1, 8):
        norm = norm + sums[k] * jnp.exp(tops[k] - largest)
    lse = largest + jnp.log(norm)
    loss_ref[...] = lse - target
    scale_ref[...] = jnp.concatenate([jnp.exp(t - lse) for t in tops], axis=0)
    split = pieces_of(lse)
    out = jnp.zeros((96, 128), f32)
    for k in range(8):
        mine = i32s == (sid[k : k + 1] & 31)
        w = jnp.concatenate([jnp.where(mine, p, 0.0) for p in split], axis=0)
        out = out + dot(w.astype(bf16), ohs[k], 1, 1)
    out = out[:32] + out[32:64] + out[64:]
    send_ref[...] = jnp.concatenate([out, jnp.zeros((96, 128), f32)], axis=0).T


def combine_kernel(flag_ref, recv_ref, sid_ref, scale_ref, out_ref):
    pos_weight = jnp.where(flag_ref[0:1, :] > 0.5, 0.0, -1.0)
    pos_weight = jnp.concatenate([pos_weight, pos_weight], axis=1)
    cols = jnp.concatenate(
        [sid_ref[...].astype(f32), scale_ref[...], pos_weight, jnp.zeros((103, 256), f32)], axis=0
    ).T
    lane = iota((256, 256), 1).astype(f32)

    def group(g, acc):
        rows = slot_rows(from_rows(recv_ref, g))
        slot = lane + (g * 256).astype(f32)
        a = jnp.where(cols[:, 8:9] == slot, cols[:, 24:25], 0.0)
        for k in range(8):
            a = jnp.where(cols[:, k : k + 1] == slot, cols[:, 16 + k : 17 + k], a)
        hi = a.astype(bf16)
        lo = (a - hi.astype(f32)).astype(bf16)
        return acc + (dot(hi, rows) + dot(lo, rows))

    out_ref[...] = lax.fori_loop(0, NGROUPS, group, jnp.zeros((256, 256), f32))


def table_kernel(counts_ref, lse_ref, tr_ref, acc_ref, x_ref, lab_ref, new_ref, nacc_ref, lse_scr, acc_scr, out_scr):
    l = pl.program_id(0)

    @pl.when(l == 0)
    def _():
        lse_scr[...] = by_slot(lse_ref[...])
        acc_scr[...] = jnp.concatenate([acc_ref[...], jnp.zeros((112, 256), f32)], axis=0).T
        out_scr[...] = jnp.zeros((256, 128), f32)

    r256 = iota((256, 256), 0)
    x, lab = x_ref[0], lab_ref[0]
    score = dot(lab, x, 1, 1)
    prob = jnp.where(r256 < counts_ref[l], jnp.exp(score - lse_scr[pl.ds(l, 1), :]), 0.0)
    hit = r256.astype(f32) == tr_ref[pl.ds(l, 1), :]
    dlogit = (prob - jnp.where(hit, 1.0, 0.0)).astype(bf16)
    grad = dot(dlogit, x)
    square = grad * grad
    mine = iota((256, 128), 1) == l
    both = (square[:, :128] + square[:, 128:]) * (1.0 / 256.0) + jnp.where(mine, acc_scr[...], 0.0)
    accum = jnp.sum(both, axis=1, keepdims=True)
    new_ref[0] = lab.astype(f32) - (STEP_RATE * grad) / jnp.sqrt(accum)
    out_scr[...] = jnp.where(mine, accum, out_scr[...])

    @pl.when(l == 15)
    def _():
        nacc_ref[...] = out_scr[...].T[:16]


def params(mib=40):
    return pltpu.CompilerParams(vmem_limit_bytes=mib * 1024 * 1024)


def shape(*dims, dtype=f32):
    return jax.ShapeDtypeStruct(dims, dtype)


VMEM = pl.BlockSpec(memory_space=pltpu.VMEM)
SMEM = pl.BlockSpec(memory_space=pltpu.SMEM)


def exchange(x):
    return lax.all_to_all(x, "shard", split_axis=0, concat_axis=0, tiled=True)


def shards(queries, clusters, placement, pos_pick, pos_row, counts, labels, accum):
    rows = DEVS * CHUNK
    send, sid = pl.pallas_call(
        route_kernel,
        out_shape=(shape(rows, 128, dtype=bf16), shape(16, 256, dtype=i32)),
        in_specs=[VMEM] * 5,
        out_specs=(VMEM, VMEM),
        scratch_shapes=[pltpu.VMEM((128, 128), f32)],
        compiler_params=params(),
        name="route",
    )(clusters.T, placement.reshape(16, 128), pos_pick.reshape(1, 256), pos_row.reshape(1, 256), queries)
    recv = exchange(send)
    x, target, flag, send = pl.pallas_call(
        owner_kernel,
        out_shape=(
            shape(16, 256, 256, dtype=bf16), shape(16, 256), shape(8, 128), shape(rows, 128, dtype=bf16),
        ),
        in_specs=[SMEM, VMEM, VMEM, VMEM],
        out_specs=(VMEM,) * 4,
        scratch_shapes=[
            pltpu.VMEM((1024, 128), f32),
            pltpu.VMEM((16, 256, 256), bf16),
            pltpu.VMEM((16, 256, 256), bf16),
            pltpu.VMEM((64, 256), f32),
            pltpu.VMEM((1024, 128), f32),
        ],
        compiler_params=params(),
        name="owner",
    )(counts, counts.astype(f32).reshape(16, 1), recv, labels)
    recv = exchange(send)
    loss, send, scale = pl.pallas_call(
        lse_kernel,
        out_shape=(shape(1, 256), shape(DEVS, 128), shape(8, 256)),
        in_specs=[VMEM, VMEM],
        out_specs=(VMEM,) * 3,
        scratch_shapes=[pltpu.VMEM((1024, 128), f32)],
        compiler_params=params(),
        name="normalizer",
    )(recv, sid)
    lse = exchange(send)
    query_grad = pl.pallas_call(
        combine_kernel,
        out_shape=shape(256, 256),
        in_specs=[VMEM] * 4,
        out_specs=VMEM,
        compiler_params=params(),
        cost_estimate=pl.CostEstimate(flops=2 * 2 * 256 * 4096 * 256, bytes_accessed=3_000_000, transcendentals=0),
        name="combine",
    )(flag, recv, sid, scale)

    def with_rows(grad):
        hit = jnp.arange(256, dtype=f32)[None, None, :] == target[:, :, None]
        found = jnp.einsum("csl,clw->csw", hit.astype(bf16), labels, preferred_element_type=f32).astype(bf16)
        found = found.reshape(16, NGROUPS, 2, GROUP, 256).transpose(1, 3, 2, 0, 4).reshape(DEVS * SLOTS, 256)
        return grad - exchange(found)[sid[9]].astype(f32)

    query_grad = lax.cond(flag[0, 0] > 0.5, with_rows, lambda grad: grad, query_grad).astype(bf16)
    whole = lambda *dims: pl.BlockSpec(dims, lambda l: (0,) * len(dims))
    per = pl.BlockSpec((1, 256, 256), lambda l: (l, 0, 0))
    new_labels, new_accum = pl.pallas_call(
        table_kernel,
        grid=(16,),
        out_shape=(shape(16, 256, 256), shape(16, 256)),
        in_specs=[SMEM, whole(128, 128), whole(16, 256), whole(16, 256), per, per],
        out_specs=(per, whole(16, 256)),
        scratch_shapes=[pltpu.VMEM((128, 256), f32), pltpu.VMEM((256, 128), f32), pltpu.VMEM((256, 128), f32)],
        compiler_params=params(),
        name="table",
    )(counts, lse, target, accum, x, labels)
    return (new_labels, new_accum, query_grad, loss.reshape(256))


def solution(mesh):
    return jax.shard_map(
        shards,
        mesh=mesh,
        in_specs=(
            P("shard", None), P("shard", None), P(), P("shard"), P("shard"), P("shard"),
            P("shard", None, None), P("shard", None),
        ),
        out_specs=(P("shard", None, None), P("shard", None), P("shard", None), P("shard")),
        check_vma=False,
    )
```

```python
import jax
import jax.numpy as jnp
from jax import lax
from jax.experimental import pallas as pl
from jax.experimental.pallas import tpu as pltpu
from jax.sharding import PartitionSpec as P

STEP_RATE = 0.1
DEVS = 128
GROUP = 8
SLOTS = 32
CHUNK = 72
BLOCK = GROUP * CHUNK
NGROUPS = DEVS // GROUP
f32 = jnp.float32
bf16 = jnp.bfloat16
i32 = jnp.int32


def iota(shape, dim):
    return lax.broadcasted_iota(i32, shape, dim)


def one(mask):
    return jnp.where(mask, 1.0, 0.0).astype(bf16)


def dot(a, b, ca=1, cb=0):
    return lax.dot_general(a, b, (((ca,), (cb,)), ((), ())), preferred_element_type=f32)


def pieces_of(x):
    hi = x.astype(bf16).astype(f32)
    rest = x - hi
    mid = rest.astype(bf16).astype(f32)
    return hi, mid, rest - mid


def total(x):
    return jnp.sum(x, axis=0, keepdims=True)


def to_rows(rows, extra):
    left = rows[:, :128].reshape(GROUP, SLOTS, 128)
    right = rows[:, 128:].reshape(GROUP, SLOTS, 128)
    return jnp.concatenate([left, right, extra], axis=1).reshape(BLOCK, 128).astype(bf16)


def from_rows(ref, group):
    block = ref[pl.ds(pl.multiple_of(group * BLOCK, BLOCK), BLOCK), :]
    return block.astype(f32).reshape(GROUP, CHUNK, 128)


def slot_rows(block):
    left = block[:, :SLOTS].reshape(GROUP * SLOTS, 128)
    right = block[:, SLOTS : 2 * SLOTS].reshape(GROUP * SLOTS, 128)
    return jnp.concatenate([left, right], axis=1).astype(bf16)


def send_block(scr, out, sems, g):
    at = pl.ds(pl.multiple_of(g * BLOCK, BLOCK), BLOCK)
    return pltpu.make_async_copy(scr.at[at, :], out.at[at, :], sems.at[g])


def route_kernel(
    cl_any, place_any, pick_any, row_any, q_any, send_any, sid_ref,
    cl_ref, place_ref, pick_ref, row_ref, q_ref, send_ref, ext_scr, in_sems, out_sems,
):
    pairs = [(cl_any, cl_ref), (place_any, place_ref), (pick_any, pick_ref), (row_any, row_ref), (q_any, q_ref)]
    copies = [pltpu.make_async_copy(a, b, in_sems.at[n]) for n, (a, b) in enumerate(pairs)]
    for copy in copies:
        copy.start()
    for copy in copies:
        copy.wait()
    c = cl_ref[...]
    ch, cl = c >> 7, c & 127
    place = place_ref[...]
    table = jnp.concatenate([(place >> 4).astype(f32), (place & 15).astype(f32)], axis=0).astype(bf16)
    i128, i16, i32s = iota((128, 256), 0), iota((16, 256), 0), iota((32, 256), 0)
    query = iota((1, 256), 1)
    queryf = query.astype(f32)
    ds, ls, ohs = [], [], []
    acc = jnp.zeros((32, 128), f32)
    for k in range(8):
        got = dot(table, one(i128 == cl[k : k + 1]))
        mine = i16 == ch[k : k + 1]
        d = total(jnp.where(mine, got[:16], 0.0)).astype(i32)
        l = total(jnp.where(mine, got[16:], 0.0)).astype(i32)
        oh = one(i128 == d)
        is_l = i16 == l
        named = jnp.concatenate([jnp.where(is_l, 1.0, 0.0), jnp.where(is_l, queryf, 0.0)], axis=0)
        acc = acc + dot(named.astype(bf16), oh, 1, 1)
        ds.append(d)
        ls.append(l)
        ohs.append(oh)
    count = acc[:16]
    middle = jnp.where(count > 1.5, jnp.floor(acc[16:] * 0.5), 255.0).astype(bf16)
    rls, sids = [], []
    for k in range(8):
        got = dot(middle, ohs[k])
        border = total(jnp.where(i16 == ls[k], got, 0.0)).astype(i32)
        rl = jnp.where(query > border, 16, 0) + ls[k]
        rls.append(rl)
        sids.append(ds[k] * SLOTS + rl)
    pick = pick_ref[...]
    dp = jnp.zeros((1, 256), i32)
    rlp = jnp.zeros((1, 256), i32)
    for k in range(8):
        dp = jnp.where(pick == k, ds[k], dp)
        rlp = jnp.where(pick == k, rls[k], rlp)
    ohp = one(i128 == dp)
    before = one(iota((256, 256), 0) < iota((256, 256), 1))
    j = total(ohp.astype(f32) * dot(ohp, before)).astype(i32)
    w_t = jnp.where(i32s == rlp, (row_ref[...] + 1).astype(f32), 0.0)
    w_j = jnp.where(i32s == j, (rlp + 1).astype(f32), 0.0)
    res = dot(jnp.concatenate([w_t, w_j, jnp.ones((8, 256), f32)], axis=0).astype(bf16), ohp, 1, 1)
    want = res[64:65]
    free = jnp.where(jnp.concatenate([count, count - 1.0], axis=0) < 0.5, 1.0, 0.0)
    lower = one(iota((32, 32), 1) < iota((32, 32), 0))
    turn = dot(lower, free.astype(bf16))
    turn = jnp.where(free > 0.5, turn, 99.0)
    code = jnp.zeros((32, 128), f32)
    for s in range(SLOTS):
        code = jnp.where(turn == float(s), res[32 + s : 33 + s], code)
    short = jnp.max(jnp.where(want > total(free), 1.0, 0.0), axis=1, keepdims=True)
    got = dot(turn.astype(bf16), ohp)
    carrier = total(jnp.where(got == j.astype(f32), i32s.astype(f32), 0.0)).astype(i32)
    ext = jnp.concatenate([res[:32], code, jnp.broadcast_to(short, (64, 128))], axis=0)
    ext_scr[...] = ext.T
    sid_ref[...] = jnp.concatenate(
        sids + [dp * SLOTS + carrier, dp * SLOTS + rlp] + [jnp.zeros((1, 256), i32)] * 6, axis=0
    )

    sub = iota((16, 256), 0)

    def group(g, _):
        named = [sid_ref[k : k + 1, :] - g * 256 for k in range(8)]
        strips = []
        for i in range(16):
            mask = sub == named[0] - 16 * i
            for k in range(1, 8):
                mask = mask | (sub == named[k] - 16 * i)
            strips.append(one(mask))
        rows = dot(jnp.concatenate(strips, axis=0), q_ref[...])
        extra = ext_scr[pl.ds(pl.multiple_of(g * GROUP, GROUP), GROUP), :]
        extra = jnp.broadcast_to(extra[:, None, :], (GROUP, 8, 128))
        send_ref[pl.ds(pl.multiple_of(g * BLOCK, BLOCK), BLOCK), :] = to_rows(rows, extra)
        send_block(send_ref, send_any, out_sems, g).start()
        return 0

    lax.fori_loop(0, NGROUPS, group, 0, unroll=16)
    for g in range(NGROUPS):
        send_block(send_ref, send_any, out_sems, g).wait()


def slot_major(x):
    second = pltpu.roll(x, 112, 1)
    both = jnp.concatenate(
        [x.reshape(NGROUPS, 1, GROUP, 128), second.reshape(NGROUPS, 1, GROUP, 128)], axis=1
    )
    return both.reshape(256, 128)


def owner_kernel(
    counts_ref, cc_ref, recv_ref, lab_any, x_any, tr_ref, flag_ref, stat_ref, send_any,
    x_ref, lab_ref, send_ref, ext_scr, part_scr, pos_scr, back_scr, lab_sem, x_sem, out_sems,
):
    lab_copy = pltpu.make_async_copy(lab_any, lab_ref, lab_sem)
    lab_copy.start()
    r256, c256 = iota((256, 256), 0), iota((256, 256), 1)
    sent = (r256 & 7) * 32 + ((r256 >> 3) & 1) * 16 + (r256 >> 4)
    perm = one(c256 == sent)

    def gather(g, _):
        block = from_rows(recv_ref, g)
        x = dot(perm, slot_rows(block)).astype(bf16)
        for l in range(16):
            x_ref[l, pl.ds(pl.multiple_of(g * 16, 16), 16), :] = x[l * 16 : (l + 1) * 16]
        ext_scr[pl.ds(pl.multiple_of(g * 64, 64), 64), :] = block[:, 64:72].reshape(64, 128)
        return 0

    lax.fori_loop(0, NGROUPS, gather, 0, unroll=4)
    x_copy = pltpu.make_async_copy(x_ref, x_any, x_sem)
    x_copy.start()
    ext = ext_scr[pl.ds(0, 128, stride=8), :]
    flag_ref[0, 0] = jnp.max(ext[:, 64:65])
    raw = slot_major(ext) - 1.0
    cc = cc_ref[...]
    tr_ref[...] = jnp.where(raw > -0.5, raw - cc * jnp.floor((raw + 0.5) / cc), -1.0)
    stat_ref[...] = jnp.zeros((256, 128), f32)
    lab_copy.wait()
    lane, wide = iota((16, 128), 1), iota((16, 256), 1)
    widef = wide.astype(f32)

    def cluster(l, _):
        lab = lab_ref[l]
        score = dot(x_ref[l], lab, 1, 1)
        valid = wide < counts_ref[l]
        weights, hits = [], []
        for i in range(16):
            at = slice(16 * i, 16 * i + 16)
            s = score[at]
            masked = jnp.where(valid, s, -jnp.inf)
            top = jnp.max(masked, axis=1, keepdims=True)
            weight = jnp.exp(masked - top)
            target = jnp.sum(jnp.where(lane == l, tr_ref[at, :], 0.0), axis=1, keepdims=True)
            hit = widef == target
            stat = jnp.where(lane == l, top, stat_ref[at, :])
            stat = jnp.where(lane == l + 16, jnp.sum(weight, axis=1, keepdims=True), stat)
            found = jnp.sum(jnp.where(hit, s, 0.0), axis=1, keepdims=True)
            stat_ref[at, :] = jnp.where(lane == l + 32, found, stat)
            weights.append(weight.astype(bf16))
            hits.append(one(hit))
        part_scr[l] = dot(jnp.concatenate(weights, axis=0), lab).astype(bf16)
        pos_scr[l] = dot(jnp.concatenate(hits, axis=0), lab).astype(bf16)
        return 0

    lax.fori_loop(0, 16, cluster, 0, unroll=4)
    hi, mid, lo = pieces_of(stat_ref[...])
    first = (hi + pltpu.roll(mid, 64, 1)).reshape(NGROUPS, 2, GROUP, 128)
    second = lo.reshape(NGROUPS, 2, GROUP, 128)
    back_scr[...] = jnp.zeros((1024, 128), f32)
    for r in range(2):
        back_scr[pl.ds(2 * r, 128, stride=8), :] = first[:, r].reshape(128, 128)
        back_scr[pl.ds(2 * r + 1, 128, stride=8), :] = second[:, r].reshape(128, 128)

    back = ((wide & 7) * 32 + ((wide >> 3) & 1) * 16 + (wide >> 4)).astype(f32)
    own_row = iota((16, 128), 0)
    sub = iota((16, 1), 0).astype(f32)

    def scatter(g, _):
        at = pl.ds(pl.multiple_of(g * 16, 16), 16)
        parts = jnp.concatenate([part_scr[l, at, :] for l in range(16)], axis=0)
        pos = jnp.concatenate([pos_scr[l, at, :] for l in range(16)], axis=0)
        codes = ext_scr[pl.ds(pl.multiple_of(g * 64, 64), 64), :]
        own, other = [], []
        for i in range(16):
            c = codes[8 * (i // 2) : 8 * (i // 2) + 8]
            c = jnp.concatenate([c, c], axis=0)
            c = jnp.where(lane == 32 + 16 * (i % 2) + own_row, c, 0.0)
            code = jnp.sum(c, axis=1, keepdims=True)
            own.append(one(back == jnp.where(code > 0.5, -1.0, sub + 16.0 * i)))
            other.append(one(back == jnp.where(code > 0.5, code + (32.0 * (i // 2) - 1.0), -1.0)))
        rows = dot(jnp.concatenate(own, axis=0), parts) + dot(jnp.concatenate(other, axis=0), pos)
        extra = back_scr[pl.ds(pl.multiple_of(g * 64, 64), 64), :].reshape(GROUP, 8, 128)
        send_ref[pl.ds(pl.multiple_of(g * BLOCK, BLOCK), BLOCK), :] = to_rows(rows, extra)
        send_block(send_ref, send_any, out_sems, g).start()
        return 0

    lax.fori_loop(0, NGROUPS, scatter, 0, unroll=8)
    x_copy.wait()
    for g in range(NGROUPS):
        send_block(send_ref, send_any, out_sems, g).wait()


def ready_kernel(
    counts_ref, flag_ref, sid_ref, stat_ref, trc_ref, acc_ref, x_any, lab_any,
    mask_ref, acct_ref, top_ref, tr_ref, weight_any, x_ref, lab_ref, weight_ref, sems,
):
    copies = [pltpu.make_async_copy(x_any, x_ref, sems.at[0]), pltpu.make_async_copy(lab_any, lab_ref, sems.at[1])]
    for copy in copies:
        copy.start()
    for copy in copies:
        copy.wait()
    acct_ref[...] = jnp.concatenate([acc_ref[...], jnp.zeros((112, 256), f32)], axis=0).T
    top_ref[...] = stat_ref[...].T[:16]
    r256 = iota((256, 256), 0)
    tr_ref[...] = trc_ref[...].T[:16]
    cols = jnp.concatenate([sid_ref[...].astype(f32), jnp.zeros((112, 256), f32)], axis=0).T
    pos_weight = jnp.where(flag_ref[0, 0] > 0.5, 0.0, -1.0)
    lane = iota((256, 256), 1).astype(f32)

    def step(n, _):
        slot = lane + (n * 256).astype(f32)
        mask = cols[:, 0:1] == slot
        for k in range(1, 8):
            mask = mask | (cols[:, k : k + 1] == slot)
        pos = jnp.where(cols[:, 8:9] == slot, pos_weight, 0.0)
        mask_ref[n] = jnp.where(mask, 1.0, pos).astype(bf16)
        score = dot(lab_ref[n], x_ref[n], 1, 1)
        weight_ref[n] = jnp.where(r256 < counts_ref[n], jnp.exp(score - top_ref[pl.ds(n, 1), :]), 0.0)
        return 0

    lax.fori_loop(0, NGROUPS, step, 0)
    copy = pltpu.make_async_copy(weight_ref, weight_any, sems.at[0])
    copy.start()
    copy.wait()


def lse_kernel(recv_ref, sid_ref, loss_ref, send_ref, lse_ref, top_ref, ext_scr):
    def take(g, _):
        block = from_rows(recv_ref, g)
        ext_scr[pl.ds(pl.multiple_of(g * 64, 64), 64), :] = block[:, 64:72].reshape(64, 128)
        return 0

    lax.fori_loop(0, NGROUPS, take, 0, unroll=2)
    stats = []
    for r in range(2):
        first = ext_scr[pl.ds(2 * r, 128, stride=8), :]
        second = ext_scr[pl.ds(2 * r + 1, 128, stride=8), :]
        stats.append(first + pltpu.roll(first, 64, 1) + second)
    lane = iota((128, 128), 1)
    tops_r = jnp.where(lane < 16, stats[0], pltpu.roll(stats[1], 16, 1))
    top_ref[...] = jnp.where(lane < 32, tops_r, 0.0)
    both = jnp.where(lane < 64, stats[0], pltpu.roll(stats[1], 64, 1)).T
    table = jnp.concatenate(pieces_of(both), axis=0).astype(bf16)
    i128, i16, i32s = iota((128, 256), 0), iota((16, 256), 0), iota((32, 256), 0)
    sid = sid_ref[...]
    tops, sums, ohs = [], [], []
    target = jnp.zeros((1, 256), f32)
    for k in range(8):
        s = sid[k : k + 1]
        oh = one(i128 == (s >> 5))
        got = dot(table, oh)
        got = got[:128] + got[128:256] + got[256:]
        got = jnp.where((s & 16) == 0, got[:48], got[64:112])
        mine = i16 == (s & 15)
        tops.append(total(jnp.where(mine, got[:16], 0.0)))
        sums.append(total(jnp.where(mine, got[16:32], 0.0)))
        target = target + total(jnp.where(mine, got[32:48], 0.0))
        ohs.append(oh)
    largest = tops[0]
    for k in range(1, 8):
        largest = jnp.maximum(largest, tops[k])
    norm = sums[0] * jnp.exp(tops[0] - largest)
    for k in range(1, 8):
        norm = norm + sums[k] * jnp.exp(tops[k] - largest)
    lse = largest + jnp.log(norm)
    loss_ref[...] = lse - target
    lse_ref[...] = jnp.broadcast_to(lse, (8, 256))
    split = pieces_of(lse)
    out = jnp.zeros((96, 128), f32)
    for k in range(8):
        mine = i32s == (sid[k : k + 1] & 31)
        w = jnp.concatenate([jnp.where(mine, p, 0.0) for p in split], axis=0)
        out = out + dot(w.astype(bf16), ohs[k], 1, 1)
    out = out[:32] + out[32:64] + out[64:]
    send_ref[...] = jnp.concatenate([out, jnp.zeros((96, 128), f32)], axis=0).T


def combine_kernel(recv_ref, mask_ref, lse_ref, top_ref, late_ref, out_ref, top_scr):
    lse = jnp.concatenate([lse_ref[...]] * 16, axis=0).T
    lse = jnp.concatenate([lse, lse], axis=1)
    r256, c256 = iota((128, 256), 0), iota((128, 256), 1)
    spread = one((r256 == (c256 & 31)) & (r256 < 32))
    wide = jnp.zeros((128, 256), f32)
    for piece in pieces_of(top_ref[...]):
        wide = wide + dot(piece.astype(bf16), spread)
    wide = jnp.where((r256 & 7) == (c256 >> 5), wide, 0.0)
    top_scr[...] = jnp.sum(wide.reshape(NGROUPS, GROUP, 256), axis=1)

    def group(g, acc):
        rows = slot_rows(from_rows(recv_ref, g))
        top = top_scr[pl.ds(g, 1), :]
        his, los = [], []
        for i in range(16):
            at = slice(16 * i, 16 * i + 16)
            mask = mask_ref[g, at, :].astype(f32)
            a = jnp.where(mask > 0.5, jnp.exp(top - lse[at]), mask)
            hi = a.astype(bf16)
            his.append(hi)
            los.append((a - hi.astype(f32)).astype(bf16))
        return acc + (dot(jnp.concatenate(his, axis=0), rows) + dot(jnp.concatenate(los, axis=0), rows))

    total_grad = lax.fori_loop(0, NGROUPS, group, -late_ref[...], unroll=8)
    out_ref[...] = total_grad.astype(bf16)


PART = 4


def table_kernel(
    lse_ref, top_ref, tr_ref, acct_ref, weight_any, x_any, lab_any, new_any, nacc_ref,
    weight_ref, x_ref, lab_ref, fac_scr, new_scr, out_scr, in_sems, out_sems,
):
    def inputs_of(p):
        at = pl.ds(p * PART, PART)
        pairs = [(weight_any, weight_ref), (x_any, x_ref), (lab_any, lab_ref)]
        return [pltpu.make_async_copy(a.at[at], b.at[at], in_sems.at[n, p]) for n, (a, b) in enumerate(pairs)]

    def output_of(p):
        at = pl.ds(p * PART, PART)
        return pltpu.make_async_copy(new_scr.at[at], new_any.at[at], out_sems.at[p])

    for p in range(16 // PART):
        for copy in inputs_of(p):
            copy.start()
    fac_scr[...] = jnp.exp(top_ref[...] - slot_major(lse_ref[...]).T[:16])
    out_scr[...] = jnp.zeros((256, 128), f32)
    rowf = iota((16, 256), 0).astype(f32)
    lane = iota((16, 128), 1)

    def part(p, _):
        for copy in inputs_of(p):
            copy.wait()
        for q in range(PART):
            l = p * PART + q
            fac = fac_scr[pl.ds(l, 1), :]
            target = tr_ref[pl.ds(l, 1), :]
            strips = []
            for i in range(16):
                hit = rowf == target - 16.0 * i
                strips.append((weight_ref[l, 16 * i : 16 * i + 16, :] * fac - jnp.where(hit, 1.0, 0.0)).astype(bf16))
            grad = dot(jnp.concatenate(strips, axis=0), x_ref[l])
            for i in range(16):
                at = slice(16 * i, 16 * i + 16)
                g = grad[at]
                square = g * g
                both = (square[:, :128] + square[:, 128:]) * (1.0 / 256.0)
                both = both + jnp.where(lane == l, acct_ref[at, :], 0.0)
                accum = jnp.sum(both, axis=1, keepdims=True)
                new_scr[l, at, :] = lab_ref[l, at, :].astype(f32) - g * (STEP_RATE / jnp.sqrt(accum))
                out_scr[at, :] = jnp.where(lane == l, accum, out_scr[at, :])
        output_of(p).start()
        return 0

    lax.fori_loop(0, 16 // PART, part, 0)
    nacc_ref[...] = out_scr[...].T[:16]
    for p in range(16 // PART):
        output_of(p).wait()


def params(mib):
    return pltpu.CompilerParams(vmem_limit_bytes=mib * 1024 * 1024)


def shape(*dims, dtype=f32):
    return jax.ShapeDtypeStruct(dims, dtype)


VMEM = pl.BlockSpec(memory_space=pltpu.VMEM)
SMEM = pl.BlockSpec(memory_space=pltpu.SMEM)
HBM = pl.BlockSpec(memory_space=pltpu.HBM)


def in_hbm(x):
    return pltpu.with_memory_space_constraint(x, pltpu.HBM)


def exchange(x):
    return lax.all_to_all(x, "shard", split_axis=0, concat_axis=0, tiled=True)


def shards(queries, clusters, placement, pos_pick, pos_row, counts, labels, accum):
    rows = DEVS * CHUNK
    send, sid = pl.pallas_call(
        route_kernel,
        out_shape=(pltpu.HBM((rows, 128), bf16), pltpu.VMEM((16, 256), i32)),
        in_specs=[HBM] * 5,
        out_specs=(HBM, VMEM),
        scratch_shapes=[
            pltpu.VMEM((8, 256), i32),
            pltpu.VMEM((16, 128), i32),
            pltpu.VMEM((1, 256), i32),
            pltpu.VMEM((1, 256), i32),
            pltpu.VMEM((256, 256), bf16),
            pltpu.VMEM((rows, 128), bf16),
            pltpu.VMEM((128, 128), f32),
            pltpu.SemaphoreType.DMA((5,)),
            pltpu.SemaphoreType.DMA((NGROUPS,)),
        ],
        compiler_params=params(16),
        name="route",
    )(
        in_hbm(clusters.T), in_hbm(placement.reshape(16, 128)), in_hbm(pos_pick.reshape(1, 256)),
        in_hbm(pos_row.reshape(1, 256)), in_hbm(queries),
    )
    recv = exchange(send)
    lanes = jnp.concatenate([counts.astype(f32), jnp.ones((112,), f32)]).reshape(1, 128)
    x, slot_target, flag, stat, send = pl.pallas_call(
        owner_kernel,
        out_shape=(
            pltpu.HBM((16, 256, 256), bf16), pltpu.VMEM((256, 128), f32), shape(1, 1), pltpu.VMEM((256, 128), f32),
            pltpu.HBM((rows, 128), bf16),
        ),
        in_specs=[SMEM, VMEM, VMEM, HBM],
        out_specs=(HBM, VMEM, SMEM, VMEM, HBM),
        scratch_shapes=[
            pltpu.VMEM((16, 256, 256), bf16),
            pltpu.VMEM((16, 256, 256), bf16),
            pltpu.VMEM((rows, 128), bf16),
            pltpu.VMEM((1024, 128), f32),
            pltpu.VMEM((16, 256, 256), bf16),
            pltpu.VMEM((16, 256, 256), bf16),
            pltpu.VMEM((1024, 128), f32),
            pltpu.SemaphoreType.DMA,
            pltpu.SemaphoreType.DMA,
            pltpu.SemaphoreType.DMA((NGROUPS,)),
        ],
        compiler_params=params(24),
        name="owner",
    )(counts, lanes, recv, in_hbm(labels))

    def with_rows():
        hit = jnp.arange(256, dtype=f32) == slot_target[:, :16].T[:, :, None]
        found = jnp.einsum("csl,clw->csw", hit.astype(bf16), labels, preferred_element_type=f32).astype(bf16)
        found = found.reshape(16, NGROUPS, 2, GROUP, 256).transpose(1, 3, 2, 0, 4).reshape(DEVS * SLOTS, 256)
        return exchange(found)[sid[9]].astype(f32)

    late = lax.cond(flag[0, 0] > 0.5, with_rows, lambda: jnp.zeros((256, 256), f32))
    send, late = lax.optimization_barrier((send, late))
    recv = exchange(send)
    mask, acct, top, target, weight = pl.pallas_call(
        ready_kernel,
        out_shape=(
            pltpu.VMEM((NGROUPS, 256, 256), bf16), pltpu.VMEM((256, 128), f32), pltpu.VMEM((16, 256), f32),
            pltpu.VMEM((16, 256), f32), pltpu.HBM((16, 256, 256), f32),
        ),
        in_specs=[SMEM] * 2 + [VMEM] * 4 + [HBM] * 2,
        out_specs=(VMEM,) * 4 + (HBM,),
        scratch_shapes=[
            pltpu.VMEM((16, 256, 256), bf16),
            pltpu.VMEM((16, 256, 256), bf16),
            pltpu.VMEM((16, 256, 256), f32),
            pltpu.SemaphoreType.DMA((2,)),
        ],
        compiler_params=params(16),
        cost_estimate=pl.CostEstimate(flops=2 * 16 * 256**3, bytes_accessed=10_000_000, transcendentals=16 * 256**2),
        name="ready",
    )(counts, flag, sid, stat, slot_target, accum, in_hbm(x), in_hbm(labels))
    loss, send, lse, tops = pl.pallas_call(
        lse_kernel,
        out_shape=(shape(1, 256), shape(DEVS, 128), shape(8, 256), shape(DEVS, 128)),
        in_specs=[VMEM, VMEM],
        out_specs=(VMEM,) * 4,
        scratch_shapes=[pltpu.VMEM((1024, 128), f32)],
        compiler_params=params(8),
        name="normalizer",
    )(recv, sid)
    back = exchange(send)
    query_grad = pl.pallas_call(
        combine_kernel,
        out_shape=shape(256, 256, dtype=bf16),
        in_specs=[VMEM] * 5,
        out_specs=VMEM,
        scratch_shapes=[
            pltpu.VMEM((NGROUPS, 256), f32),
        ],
        compiler_params=params(8),
        cost_estimate=pl.CostEstimate(flops=2 * 2 * 256 * 4096 * 256, bytes_accessed=5_000_000, transcendentals=256 * 4096),
        name="combine",
    )(recv, mask, lse, tops, late)
    new_labels, new_accum = pl.pallas_call(
        table_kernel,
        out_shape=(pltpu.HBM((16, 256, 256), f32), shape(16, 256)),
        in_specs=[VMEM] * 4 + [HBM] * 3,
        out_specs=(HBM, VMEM),
        scratch_shapes=[
            pltpu.VMEM((16, 256, 256), f32),
            pltpu.VMEM((16, 256, 256), bf16),
            pltpu.VMEM((16, 256, 256), bf16),
            pltpu.VMEM((16, 256), f32),
            pltpu.VMEM((16, 256, 256), f32),
            pltpu.VMEM((256, 128), f32),
            pltpu.SemaphoreType.DMA((3, 16 // PART)),
            pltpu.SemaphoreType.DMA((16 // PART,)),
        ],
        compiler_params=params(24),
        name="table",
    )(back, top, target, acct, in_hbm(weight), in_hbm(x), in_hbm(labels))

    return (new_labels, new_accum, query_grad, loss.reshape(256))


def solution(mesh):
    return jax.shard_map(
        shards,
        mesh=mesh,
        in_specs=(
            P("shard", None), P("shard", None), P(), P("shard"), P("shard"), P("shard"),
            P("shard", None, None), P("shard", None),
        ),
        out_specs=(P("shard", None, None), P("shard", None), P("shard", None), P("shard")),
        check_vma=False,
    )
```

```python
import jax
import jax.numpy as jnp
from jax import lax
from jax.experimental import pallas as pl
from jax.experimental.pallas import tpu as pltpu
from jax.sharding import PartitionSpec as P

STEP_RATE = 0.1
DEVS = 128
GROUP = 8
SLOTS = 32
PAIRS = 24
OUT = 56
BACK = 64
NGROUPS = DEVS // GROUP
f32 = jnp.float32
bf16 = jnp.bfloat16
i32 = jnp.int32


def iota(shape, dim):
    return lax.broadcasted_iota(i32, shape, dim)


def one(mask):
    return jnp.where(mask, 1.0, 0.0).astype(bf16)


def dot(a, b, ca=1, cb=0):
    return lax.dot_general(a, b, (((ca,), (cb,)), ((), ())), preferred_element_type=f32)


def pieces_of(x):
    hi = x.astype(bf16).astype(f32)
    rest = x - hi
    mid = rest.astype(bf16).astype(f32)
    return hi, mid, rest - mid


def total(x):
    return jnp.sum(x, axis=0, keepdims=True)


def from_rows(ref, group, chunk):
    size = GROUP * chunk
    block = ref[pl.ds(pl.multiple_of(group * size, size), size), :]
    return block.astype(f32).reshape(GROUP, chunk, 128)


def slot_rows(block, slots):
    left = block[:, :slots].reshape(GROUP * slots, 128)
    right = block[:, slots : 2 * slots].reshape(GROUP * slots, 128)
    return jnp.concatenate([left, right], axis=1).astype(bf16)


def send_block(scr, out, sems, g, chunk):
    size = GROUP * chunk
    at = pl.ds(pl.multiple_of(g * size, size), size)
    return pltpu.make_async_copy(scr.at[at, :], out.at[at, :], sems.at[g])


def route_kernel(
    cl_any, place_any, pick_any, row_any, q_any, send_any, sid_ref,
    cl_ref, place_ref, pick_ref, row_ref, q_ref, send_ref, ext_scr, in_sems, out_sems,
):
    pairs = [(cl_any, cl_ref), (place_any, place_ref), (pick_any, pick_ref), (row_any, row_ref), (q_any, q_ref)]
    copies = [pltpu.make_async_copy(a, b, in_sems.at[n]) for n, (a, b) in enumerate(pairs)]
    for copy in copies:
        copy.start()
    for copy in copies:
        copy.wait()
    c = cl_ref[...]
    ch, cl = c >> 7, c & 127
    place = place_ref[...]
    table = jnp.concatenate([(place >> 4).astype(f32), (place & 15).astype(f32)], axis=0).astype(bf16)
    i128, i16, i32s = iota((128, 256), 0), iota((16, 256), 0), iota((32, 256), 0)
    query = iota((1, 256), 1)
    queryf = query.astype(f32)
    ds, ls, ohs = [], [], []
    acc = jnp.zeros((32, 128), f32)
    for k in range(8):
        got = dot(table, one(i128 == cl[k : k + 1]))
        mine = i16 == ch[k : k + 1]
        d = total(jnp.where(mine, got[:16], 0.0)).astype(i32)
        l = total(jnp.where(mine, got[16:], 0.0)).astype(i32)
        oh = one(i128 == d)
        is_l = i16 == l
        named = jnp.concatenate([jnp.where(is_l, 1.0, 0.0), jnp.where(is_l, queryf, 0.0)], axis=0)
        acc = acc + dot(named.astype(bf16), oh, 1, 1)
        ds.append(d)
        ls.append(l)
        ohs.append(oh)
    count = acc[:16]
    middle = jnp.where(count > 1.5, jnp.floor(acc[16:] * 0.5), 255.0).astype(bf16)
    before = one(iota((256, 256), 0) < iota((256, 256), 1))
    used = jnp.zeros((128, 1), f32)
    rls, js, codes = [], [], []
    for k in range(8):
        got = dot(middle, ohs[k])
        border = total(jnp.where(i16 == ls[k], got, 0.0)).astype(i32)
        rl = jnp.where(query > border, 16, 0) + ls[k]
        ohf = ohs[k].astype(f32)
        j = total(ohf * (dot(ohs[k], before) + used)).astype(i32)
        used = used + jnp.sum(ohf, axis=1, keepdims=True)
        codes.append(jnp.where(i32s == j, (rl + 1).astype(f32), 0.0).astype(bf16))
        rls.append(rl)
        js.append(j)
    pick = pick_ref[...]
    dp = jnp.zeros((1, 256), i32)
    rlp = jnp.zeros((1, 256), i32)
    for k in range(8):
        dp = jnp.where(pick == k, ds[k], dp)
        rlp = jnp.where(pick == k, rls[k], rlp)
    ohp = one(i128 == dp)
    ohf = ohp.astype(f32)
    jp = total(ohf * (dot(ohp, before) + used)).astype(i32)
    codes.append(jnp.where(i32s == jp, (rlp + 65).astype(f32), 0.0).astype(bf16))
    code = dot(jnp.concatenate(codes, axis=1), jnp.concatenate(ohs + [ohp], axis=1), 1, 1)
    rows = dot(jnp.where(i32s == rlp, (row_ref[...] + 1).astype(f32), 0.0).astype(bf16), ohp, 1, 1)
    most = used + jnp.sum(ohf, axis=1, keepdims=True)
    full = jnp.where((used > PAIRS + 0.5) | (most > SLOTS - 0.5), 1.0, 0.0)
    full = jnp.max(full, axis=0, keepdims=True)
    ext_scr[...] = jnp.concatenate([code, rows, jnp.broadcast_to(full, (64, 128))], axis=0).T
    sid_ref[...] = jnp.concatenate(
        [d * SLOTS + j for d, j in zip(ds, js)] + rls + [dp * SLOTS + jp] + [jnp.zeros((1, 256), i32)] * 7, axis=0
    )
    sub = iota((8, 256), 0)

    def group(g, _):
        named = [sid_ref[k : k + 1, :] - g * 256 for k in range(8)]
        strips = []
        for i in range(12):
            tiles = []
            for q in (2 * i, 2 * i + 1):
                first = (q // 3) * SLOTS + (q % 3) * 8
                mask = sub == named[0] - first
                for k in range(1, 8):
                    mask = mask | (sub == named[k] - first)
                tiles.append(jnp.where(mask, 1.0, 0.0))
            strips.append(jnp.concatenate(tiles, axis=0).astype(bf16))
        rows = dot(jnp.concatenate(strips, axis=0), q_ref[...])
        left = rows[:, :128].reshape(GROUP, PAIRS, 128)
        right = rows[:, 128:].reshape(GROUP, PAIRS, 128)
        extra = ext_scr[pl.ds(pl.multiple_of(g * GROUP, GROUP), GROUP), :]
        extra = jnp.broadcast_to(extra[:, None, :], (GROUP, 8, 128))
        out = jnp.concatenate([left, right, extra], axis=1).reshape(GROUP * OUT, 128).astype(bf16)
        send_ref[pl.ds(pl.multiple_of(g * GROUP * OUT, GROUP * OUT), GROUP * OUT), :] = out
        send_block(send_ref, send_any, out_sems, g, OUT).start()
        return 0

    lax.fori_loop(0, NGROUPS, group, 0, unroll=16)
    for g in range(NGROUPS):
        send_block(send_ref, send_any, out_sems, g, OUT).wait()


def slot_major(x):
    second = pltpu.roll(x, 112, 1)
    both = jnp.concatenate(
        [x.reshape(NGROUPS, 1, GROUP, 128), second.reshape(NGROUPS, 1, GROUP, 128)], axis=1
    )
    return both.reshape(256, 128)


def owner_kernel(
    counts_ref, cc_ref, recv_ref, lab_any, x_any, tr_ref, flag_ref, stat_ref, send_any,
    x_ref, lab_ref, send_ref, ext_scr, key_scr, part_scr, pos_scr, lab_sem, x_sem, out_sems,
):
    lab_copy = pltpu.make_async_copy(lab_any, lab_ref, lab_sem)
    lab_copy.start()

    def take(g, _):
        block = from_rows(recv_ref, g, OUT)
        ext_scr[pl.ds(pl.multiple_of(g * 64, 64), 64), :] = block[:, 48:56].reshape(64, 128)
        return 0

    lax.fori_loop(0, NGROUPS, take, 0, unroll=16)
    ext = ext_scr[pl.ds(0, 128, stride=8), :]
    flag_ref[0, 0] = jnp.max(ext[:, 64:65])
    source, col = iota((128, 256), 0), iota((128, 256), 1)
    owner_of = jnp.floor((col.astype(f32) + 0.5) / PAIRS).astype(i32)
    spread = one(source == col - owner_of * PAIRS)
    codes = jnp.where((source & 7) == owner_of, dot(ext.astype(bf16), spread), 0.0)
    codes = jnp.sum(codes.reshape(NGROUPS, GROUP, 256), axis=1).astype(i32)
    rl = codes - 1
    keys = (rl & 15) * 16 + (rl >> 4) * 8 + owner_of[:16]
    key_scr[...] = jnp.where((codes > 0) & (codes < 64), keys, -1)
    sub = iota((16, 256), 0)

    def gather(g, _):
        block = from_rows(recv_ref, g, OUT)
        key = key_scr[pl.ds(g, 1), :]
        perm = jnp.concatenate([one(sub == key - 16 * i) for i in range(16)], axis=0)
        rows = jnp.concatenate([slot_rows(block, PAIRS), jnp.zeros((64, 256), bf16)], axis=0)
        x = dot(perm, rows).astype(bf16)
        for l in range(16):
            x_ref[l, pl.ds(pl.multiple_of(g * 16, 16), 16), :] = x[l * 16 : (l + 1) * 16]
        return 0

    lax.fori_loop(0, NGROUPS, gather, 0, unroll=4)
    x_copy = pltpu.make_async_copy(x_ref, x_any, x_sem)
    x_copy.start()
    raw = slot_major(pltpu.roll(ext, 96, 1)) - 1.0
    cc = cc_ref[...]
    tr_ref[...] = jnp.where(raw > -0.5, raw - cc * jnp.floor((raw + 0.5) / cc), -1.0)
    stat_ref[...] = jnp.zeros((256, 128), f32)
    lab_copy.wait()
    lane, wide = iota((16, 128), 1), iota((16, 256), 1)
    widef = wide.astype(f32)

    def cluster(l, _):
        lab = lab_ref[l]
        score = dot(x_ref[l], lab, 1, 1)
        valid = wide < counts_ref[l]
        weights, hits = [], []
        for i in range(16):
            at = slice(16 * i, 16 * i + 16)
            s = score[at]
            masked = jnp.where(valid, s, -jnp.inf)
            top = jnp.max(masked, axis=1, keepdims=True)
            weight = jnp.exp(masked - top)
            target = jnp.sum(jnp.where(lane == l, tr_ref[at, :], 0.0), axis=1, keepdims=True)
            hit = widef == target
            stat = jnp.where(lane == l, top, stat_ref[at, :])
            stat = jnp.where(lane == l + 16, jnp.sum(weight, axis=1, keepdims=True), stat)
            found = jnp.sum(jnp.where(hit, s, 0.0), axis=1, keepdims=True)
            stat_ref[at, :] = jnp.where(lane == l + 32, found, stat)
            weights.append(weight.astype(bf16))
            hits.append(one(hit))
        part_scr[l] = dot(jnp.concatenate(weights, axis=0), lab).astype(bf16)
        pos_scr[l] = dot(jnp.concatenate(hits, axis=0), lab).astype(bf16)
        return 0

    lax.fori_loop(0, 16, cluster, 0, unroll=4)
    lane, own_row = iota((16, 128), 1), iota((16, 128), 0)
    own_sub = iota((16, 1), 0).astype(f32)
    wide = iota((16, 256), 1)
    home = ((wide & 7) * 32 + ((wide >> 3) & 1) * 16 + (wide >> 4)).astype(f32)
    last = iota((GROUP, 8, 128), 1) == 7

    def scatter(g, _):
        at = pl.ds(pl.multiple_of(g * 16, 16), 16)
        parts = jnp.concatenate([part_scr[l, at, :] for l in range(16)], axis=0)
        pos = jnp.concatenate([pos_scr[l, at, :] for l in range(16)], axis=0)
        codes = ext_scr[pl.ds(pl.multiple_of(g * 64, 64), 64), :]
        own, other = [], []
        for i in range(16):
            c = codes[8 * (i // 2) : 8 * (i // 2) + 8]
            c = jnp.concatenate([c, c], axis=0)
            c = jnp.where(lane == 16 * (i % 2) + own_row, c, 0.0)
            code = jnp.sum(c, axis=1, keepdims=True) + (32.0 * (i // 2) - 1.0)
            is_pos = code > 32.0 * (i // 2) + 50.0
            is_part = (code > 32.0 * (i // 2) - 0.5) & (code < 32.0 * (i // 2) + 50.0)
            own.append(one(home == jnp.where(is_part, code, -1.0)))
            other.append(one(home == jnp.where(is_pos, code - 64.0, -1.0)))
        rows = dot(jnp.concatenate(own, axis=0), parts) + dot(jnp.concatenate(other, axis=0), pos)
        hi, mid, lo = pieces_of(stat_ref[at, :])
        stat = hi + pltpu.roll(mid, 48, 1)
        stat = stat + jnp.where(lane >= 112, pltpu.roll(lo, 80, 1), jnp.where(lane >= 96, pltpu.roll(lo, 96, 1), 0.0))
        halves = []
        for r in range(2):
            half = rows[:, 128 * r : 128 * r + 128].reshape(GROUP, SLOTS, 128)
            mine = jnp.broadcast_to(stat[8 * r : 8 * r + 8][:, None, :], (GROUP, 8, 128))
            halves += [half[:, :24], jnp.where(last, mine, half[:, 24:])]
        out = jnp.concatenate(halves, axis=1).reshape(GROUP * BACK, 128).astype(bf16)
        send_ref[pl.ds(pl.multiple_of(g * GROUP * BACK, GROUP * BACK), GROUP * BACK), :] = out
        send_block(send_ref, send_any, out_sems, g, BACK).start()
        return 0

    lax.fori_loop(0, NGROUPS, scatter, 0, unroll=8)
    x_copy.wait()
    for g in range(NGROUPS):
        send_block(send_ref, send_any, out_sems, g, BACK).wait()


def ready_kernel(
    counts_ref, sid_ref, stat_ref, trc_ref, acc_ref, x_any, lab_any,
    mask_ref, acct_ref, top_ref, tr_ref, weight_any, x_ref, lab_ref, weight_ref, sems,
):
    copies = [pltpu.make_async_copy(x_any, x_ref, sems.at[0]), pltpu.make_async_copy(lab_any, lab_ref, sems.at[1])]
    for copy in copies:
        copy.start()
    for copy in copies:
        copy.wait()
    acct_ref[...] = jnp.concatenate([acc_ref[...], jnp.zeros((112, 256), f32)], axis=0).T
    top_ref[...] = stat_ref[...].T[:16]
    r256 = iota((256, 256), 0)
    tr_ref[...] = trc_ref[...].T[:16]
    cols = jnp.concatenate([sid_ref[...].astype(f32), jnp.zeros((104, 256), f32)], axis=0).T
    lane = iota((256, 256), 1).astype(f32)

    def step(n, _):
        slot = lane + (n * 256).astype(f32)
        mask = cols[:, 0:1] == slot
        for k in range(1, 8):
            mask = mask | (cols[:, k : k + 1] == slot)
        pos = jnp.where(cols[:, 16:17] == slot, -1.0, 0.0)
        mask_ref[n] = jnp.where(mask, 1.0, pos).astype(bf16)
        score = dot(lab_ref[n], x_ref[n], 1, 1)
        weight_ref[n] = jnp.where(r256 < counts_ref[n], jnp.exp(score - top_ref[pl.ds(n, 1), :]), 0.0)
        return 0

    lax.fori_loop(0, NGROUPS, step, 0)
    copy = pltpu.make_async_copy(weight_ref, weight_any, sems.at[0])
    copy.start()
    copy.wait()


def lse_kernel(recv_ref, sid_ref, loss_ref, send_ref, scale_ref, left_scr, right_scr):
    def take(g, _):
        block = from_rows(recv_ref, g, BACK)
        at = pl.ds(pl.multiple_of(g * 64, 64), 64)
        left_scr[at, :] = block[:, 24:32].reshape(64, 128)
        right_scr[at, :] = block[:, 56:64].reshape(64, 128)
        return 0

    lax.fori_loop(0, NGROUPS, take, 0, unroll=16)
    stats = [scr[pl.ds(7, 128, stride=8), :].T for scr in (left_scr, right_scr)]
    table = jnp.concatenate(stats, axis=0).astype(bf16)
    i128, i16, i32s = iota((128, 256), 0), iota((16, 256), 0), iota((32, 256), 0)
    sid = sid_ref[...]
    tops, sums, ohs = [], [], []
    target = jnp.zeros((1, 256), f32)
    for k in range(8):
        rl = sid[8 + k : 9 + k]
        oh = one(i128 == (sid[k : k + 1] >> 5))
        got = dot(table, oh)
        got = jnp.where((rl & 16) == 0, got[:128], got[128:])
        mine = i16 == (rl & 15)
        tops.append(total(jnp.where(mine, got[:16] + got[48:64] + got[96:112], 0.0)))
        sums.append(total(jnp.where(mine, got[16:32] + got[64:80], 0.0)))
        target = target + total(jnp.where(mine, got[32:48] + got[80:96] + got[112:], 0.0))
        ohs.append(oh)
    largest = tops[0]
    for k in range(1, 8):
        largest = jnp.maximum(largest, tops[k])
    norm = sums[0] * jnp.exp(tops[0] - largest)
    for k in range(1, 8):
        norm = norm + sums[k] * jnp.exp(tops[k] - largest)
    lse = largest + jnp.log(norm)
    loss_ref[...] = lse - target
    split = pieces_of(lse)
    outs = []
    for k in range(8):
        j, rl = sid[k : k + 1] & 31, sid[8 + k : 9 + k]
        w = [jnp.where(i32s == rl, p, 0.0) for p in split]
        w += [jnp.where(i32s == j, p, 0.0) for p in pieces_of(jnp.exp(tops[k] - lse))]
        outs.append(jnp.concatenate(w, axis=0).astype(bf16))
    out = dot(jnp.concatenate(outs, axis=1), jnp.concatenate(ohs, axis=1), 1, 1)
    out = jnp.concatenate([out[:32] + out[32:64] + out[64:96], out[96:128] + out[128:160] + out[160:]], axis=0)
    out = jnp.concatenate([out, jnp.zeros((64, 128), f32)], axis=0).T
    send_ref[...] = out
    scale_ref[...] = jnp.where(iota((128, 128), 1) < 32, pltpu.roll(out, 96, 1), 0.0)


def combine_kernel(recv_ref, mask_ref, scale_ref, out_ref, row_scr):
    r256, c256 = iota((128, 256), 0), iota((128, 256), 1)
    spread = one((r256 == (c256 & 31)) & (r256 < 32))
    wide = jnp.zeros((128, 256), f32)
    for piece in pieces_of(scale_ref[...]):
        wide = wide + dot(piece.astype(bf16), spread)
    wide = jnp.where((r256 & 7) == (c256 >> 5), wide, 0.0)
    row_scr[...] = jnp.sum(wide.reshape(NGROUPS, GROUP, 256), axis=1)

    def group(g, acc):
        rows = slot_rows(from_rows(recv_ref, g, BACK), SLOTS)
        scale = row_scr[pl.ds(g, 1), :]
        his, los = [], []
        for i in range(16):
            mask = mask_ref[g, 16 * i : 16 * i + 16, :].astype(f32)
            a = jnp.where(mask > 0.5, scale, mask)
            hi = a.astype(bf16)
            his.append(hi)
            los.append((a - hi.astype(f32)).astype(bf16))
        return acc + (dot(jnp.concatenate(his, axis=0), rows) + dot(jnp.concatenate(los, axis=0), rows))

    out_ref[...] = lax.fori_loop(0, NGROUPS, group, jnp.zeros((256, 256), f32), unroll=8).astype(bf16)


PART = 4


def table_kernel(
    lse_ref, top_ref, tr_ref, acct_ref, weight_any, x_any, lab_any, new_any, nacc_ref,
    weight_ref, x_ref, lab_ref, fac_scr, new_scr, out_scr, in_sems, out_sems,
):
    def inputs_of(p):
        at = pl.ds(p * PART, PART)
        pairs = [(weight_any, weight_ref), (x_any, x_ref), (lab_any, lab_ref)]
        return [pltpu.make_async_copy(a.at[at], b.at[at], in_sems.at[n, p]) for n, (a, b) in enumerate(pairs)]

    def output_of(p):
        at = pl.ds(p * PART, PART)
        return pltpu.make_async_copy(new_scr.at[at], new_any.at[at], out_sems.at[p])

    for p in range(16 // PART):
        for copy in inputs_of(p):
            copy.start()
    fac_scr[...] = jnp.exp(top_ref[...] - slot_major(lse_ref[...]).T[:16])
    out_scr[...] = jnp.zeros((256, 128), f32)
    rowf = iota((16, 256), 0).astype(f32)
    lane = iota((16, 128), 1)

    def part(p, _):
        for copy in inputs_of(p):
            copy.wait()
        for q in range(PART):
            l = p * PART + q
            fac = fac_scr[pl.ds(l, 1), :]
            target = tr_ref[pl.ds(l, 1), :]
            strips = []
            for i in range(16):
                hit = rowf == target - 16.0 * i
                strips.append((weight_ref[l, 16 * i : 16 * i + 16, :] * fac - jnp.where(hit, 1.0, 0.0)).astype(bf16))
            grad = dot(jnp.concatenate(strips, axis=0), x_ref[l])
            for i in range(16):
                at = slice(16 * i, 16 * i + 16)
                g = grad[at]
                square = g * g
                both = (square[:, :128] + square[:, 128:]) * (1.0 / 256.0)
                both = both + jnp.where(lane == l, acct_ref[at, :], 0.0)
                accum = jnp.sum(both, axis=1, keepdims=True)
                new_scr[l, at, :] = lab_ref[l, at, :].astype(f32) - g * (STEP_RATE / jnp.sqrt(accum))
                out_scr[at, :] = jnp.where(lane == l, accum, out_scr[at, :])
        output_of(p).start()
        return 0

    lax.fori_loop(0, 16 // PART, part, 0)
    nacc_ref[...] = out_scr[...].T[:16]
    for p in range(16 // PART):
        output_of(p).wait()


def params(mib):
    return pltpu.CompilerParams(vmem_limit_bytes=mib * 1024 * 1024)


def shape(*dims, dtype=f32):
    return jax.ShapeDtypeStruct(dims, dtype)


VMEM = pl.BlockSpec(memory_space=pltpu.VMEM)
SMEM = pl.BlockSpec(memory_space=pltpu.SMEM)
HBM = pl.BlockSpec(memory_space=pltpu.HBM)


def in_hbm(x):
    return pltpu.with_memory_space_constraint(x, pltpu.HBM)


def exchange(x):
    return lax.all_to_all(x, "shard", split_axis=0, concat_axis=0, tiled=True)


def ranks_of(keys):
    order = jnp.argsort(keys, stable=True)
    sorted_keys = keys[order]
    places = jnp.arange(keys.shape[0], dtype=jnp.int32)
    starts = jnp.where((places == 0) | (sorted_keys != jnp.roll(sorted_keys, 1)), places, 0)
    starts = lax.cummax(starts)
    return jnp.zeros_like(keys).at[order].set(places - starts)


def scoring(recv_q, labels):
    return jnp.einsum("csw,clw->csl", recv_q, labels, preferred_element_type=jnp.float32)


def owner_share(score, top, valid, labels):
    weight = jnp.where(valid, jnp.exp(score - top[..., None]), 0.0).astype(jnp.bfloat16)
    return jnp.einsum("csl,clw->csw", weight, labels, preferred_element_type=jnp.float32).astype(
        jnp.bfloat16
    )


def send_back(share, pos_rows, devices):
    local_blocks, slot_rows, width = share.shape
    shaped = (local_blocks, devices, slot_rows // devices, width)
    return (
        lax.all_to_all(share.reshape(shaped), "shard", split_axis=1, concat_axis=1, tiled=True),
        lax.all_to_all(pos_rows.reshape(shaped), "shard", split_axis=1, concat_axis=1, tiled=True),
    )


def general(queries, clusters, placement, pos_pick, pos_row, counts, labels, accum):
    devices = lax.axis_size("shard")
    rows_dev, width = queries.shape
    per_query = clusters.shape[1]
    local_blocks, block_rows, _ = labels.shape
    most_rows = max(2, 2 * rows_dev * per_query // (local_blocks * devices))
    all_slots = local_blocks * devices * most_rows
    slot_rows = devices * most_rows
    flat = clusters.reshape(-1)
    rank = ranks_of(flat)
    block_ids = placement[flat]
    dest = block_ids // local_blocks
    local_id = block_ids % local_blocks
    where_to = (local_id * devices + dest) * most_rows + rank
    picked = jnp.arange(per_query, dtype=jnp.int32)[None, :] == pos_pick[:, None]
    target = jnp.where(picked, pos_row[:, None], -1).reshape(-1)
    send_q = (
        jnp.zeros((all_slots, width), jnp.bfloat16)
        .at[where_to]
        .set(jnp.repeat(queries, per_query, axis=0))
    )
    send_t = jnp.full((all_slots,), -1, jnp.int32).at[where_to].set(target)
    recv_q, recv_t = (
        lax.all_to_all(
            send_q.reshape(local_blocks, devices, most_rows, width),
            "shard",
            split_axis=1,
            concat_axis=1,
            tiled=True,
        ),
        lax.all_to_all(
            send_t.reshape(local_blocks, devices, most_rows),
            "shard",
            split_axis=1,
            concat_axis=1,
            tiled=True,
        ),
    )
    recv_q = recv_q.reshape(local_blocks, slot_rows, width)
    recv_t = recv_t.reshape(local_blocks, slot_rows)
    row_ids = jnp.arange(block_rows, dtype=jnp.int32)
    valid = row_ids[None, None, :] < counts[:, None, None]
    target_row = jnp.where(recv_t >= 0, recv_t % counts[:, None], -1)
    hit = row_ids[None, None, :] == target_row[..., None]
    score = scoring(recv_q, labels)
    masked = jnp.where(valid, score, -jnp.inf)
    top = jnp.max(masked, axis=-1)
    total = jnp.sum(jnp.exp(masked - top[..., None]), axis=-1)
    spos = jnp.sum(jnp.where(hit, score, 0.0), axis=-1)
    pos_rows = jnp.einsum(
        "csl,clw->csw", hit.astype(jnp.bfloat16), labels, preferred_element_type=jnp.float32
    ).astype(jnp.bfloat16)
    stat_shape = (local_blocks, devices, most_rows)
    back_m, back_z, back_s = (
        lax.all_to_all(top.reshape(stat_shape), "shard", split_axis=1, concat_axis=1, tiled=True),
        lax.all_to_all(total.reshape(stat_shape), "shard", split_axis=1, concat_axis=1, tiled=True),
        lax.all_to_all(spos.reshape(stat_shape), "shard", split_axis=1, concat_axis=1, tiled=True),
    )
    pair_m = back_m.reshape(-1)[where_to].reshape(rows_dev, per_query)
    pair_z = back_z.reshape(-1)[where_to].reshape(rows_dev, per_query)
    pair_s = back_s.reshape(-1)[where_to].reshape(rows_dev, per_query)
    largest = jnp.max(pair_m, axis=1)
    norm = jnp.sum(pair_z * jnp.exp(pair_m - largest[:, None]), axis=1)
    lse = largest + jnp.log(norm)
    loss = lse - jnp.sum(pair_s, axis=1)
    send_l = jnp.zeros((all_slots,), jnp.float32).at[where_to].set(jnp.repeat(lse, per_query))
    recv_l = lax.all_to_all(
        send_l.reshape(stat_shape), "shard", split_axis=1, concat_axis=1, tiled=True
    ).reshape(local_blocks, slot_rows)
    prob = jnp.where(valid, jnp.exp(score - recv_l[..., None]), 0.0)
    dlogit = (prob - hit.astype(jnp.float32)).astype(jnp.bfloat16)
    label_grad = jnp.einsum("csl,csw->clw", dlogit, recv_q, preferred_element_type=jnp.float32)
    returned, returned_pos = send_back(owner_share(score, top, valid, labels), pos_rows, devices)
    pieces = (
        returned.reshape(all_slots, width)[where_to]
        .astype(jnp.float32)
        .reshape(rows_dev, per_query, width)
    )
    pos_pieces = (
        returned_pos.reshape(all_slots, width)[where_to]
        .astype(jnp.float32)
        .reshape(rows_dev, per_query, width)
    )
    scale = jnp.exp(pair_m - lse[:, None])
    query_grad = (jnp.sum(pieces * scale[..., None], axis=1) - jnp.sum(pos_pieces, axis=1)).astype(
        jnp.bfloat16
    )
    new_accum = accum + jnp.mean(label_grad * label_grad, axis=-1)
    new_labels = (
        labels.astype(jnp.float32) - STEP_RATE * label_grad / jnp.sqrt(new_accum)[..., None]
    )
    return (new_labels, new_accum, query_grad, loss)


def shards(queries, clusters, placement, pos_pick, pos_row, counts, labels, accum):
    send, sid = pl.pallas_call(
        route_kernel,
        out_shape=(pltpu.HBM((DEVS * OUT, 128), bf16), pltpu.VMEM((24, 256), i32)),
        in_specs=[HBM] * 5,
        out_specs=(HBM, VMEM),
        scratch_shapes=[
            pltpu.VMEM((8, 256), i32),
            pltpu.VMEM((16, 128), i32),
            pltpu.VMEM((1, 256), i32),
            pltpu.VMEM((1, 256), i32),
            pltpu.VMEM((256, 256), bf16),
            pltpu.VMEM((DEVS * OUT, 128), bf16),
            pltpu.VMEM((128, 128), f32),
            pltpu.SemaphoreType.DMA((5,)),
            pltpu.SemaphoreType.DMA((NGROUPS,)),
        ],
        compiler_params=params(16),
        name="route",
    )(
        in_hbm(clusters.T), in_hbm(placement.reshape(16, 128)), in_hbm(pos_pick.reshape(1, 256)),
        in_hbm(pos_row.reshape(1, 256)), in_hbm(queries),
    )
    recv = exchange(send)
    lanes = jnp.concatenate([counts.astype(f32), jnp.ones((112,), f32)]).reshape(1, 128)
    x, slot_target, flag, stat, send = pl.pallas_call(
        owner_kernel,
        out_shape=(
            pltpu.HBM((16, 256, 256), bf16), pltpu.VMEM((256, 128), f32), shape(1, 1), pltpu.VMEM((256, 128), f32),
            pltpu.HBM((DEVS * BACK, 128), bf16),
        ),
        in_specs=[SMEM, VMEM, VMEM, HBM],
        out_specs=(HBM, VMEM, SMEM, VMEM, HBM),
        scratch_shapes=[
            pltpu.VMEM((16, 256, 256), bf16),
            pltpu.VMEM((16, 256, 256), bf16),
            pltpu.VMEM((DEVS * BACK, 128), bf16),
            pltpu.VMEM((1024, 128), f32),
            pltpu.VMEM((16, 256), i32),
            pltpu.VMEM((16, 256, 256), bf16),
            pltpu.VMEM((16, 256, 256), bf16),
            pltpu.SemaphoreType.DMA,
            pltpu.SemaphoreType.DMA,
            pltpu.SemaphoreType.DMA((NGROUPS,)),
        ],
        compiler_params=params(24),
        name="owner",
    )(counts, lanes, recv, in_hbm(labels))

    def plain():
        return general(queries, clusters, placement, pos_pick, pos_row, counts, labels, accum)

    def packed():
        return finish(counts, labels, accum, sid, x, slot_target, stat, send)

    return lax.cond(flag[0, 0] > 0.5, plain, packed)


def finish(counts, labels, accum, sid, x, slot_target, stat, send):
    recv = exchange(send)
    mask, acct, top, target, weight = pl.pallas_call(
        ready_kernel,
        out_shape=(
            pltpu.VMEM((NGROUPS, 256, 256), bf16), pltpu.VMEM((256, 128), f32), pltpu.VMEM((16, 256), f32),
            pltpu.VMEM((16, 256), f32), pltpu.HBM((16, 256, 256), f32),
        ),
        in_specs=[SMEM] + [VMEM] * 4 + [HBM] * 2,
        out_specs=(VMEM,) * 4 + (HBM,),
        scratch_shapes=[
            pltpu.VMEM((16, 256, 256), bf16),
            pltpu.VMEM((16, 256, 256), bf16),
            pltpu.VMEM((16, 256, 256), f32),
            pltpu.SemaphoreType.DMA((2,)),
        ],
        compiler_params=params(16),
        cost_estimate=pl.CostEstimate(flops=2 * 16 * 256**3, bytes_accessed=10_000_000, transcendentals=16 * 256**2),
        name="ready",
    )(counts, sid, stat, slot_target, accum, in_hbm(x), in_hbm(labels))
    loss, send, scale = pl.pallas_call(
        lse_kernel,
        out_shape=(shape(1, 256), shape(DEVS, 128), shape(DEVS, 128)),
        in_specs=[VMEM, VMEM],
        out_specs=(VMEM,) * 3,
        scratch_shapes=[pltpu.VMEM((1024, 128), f32)] * 2,
        compiler_params=params(8),
        name="normalizer",
    )(recv, sid)
    back = exchange(send)
    query_grad = pl.pallas_call(
        combine_kernel,
        out_shape=shape(256, 256, dtype=bf16),
        in_specs=[VMEM] * 3,
        out_specs=VMEM,
        scratch_shapes=[
            pltpu.VMEM((NGROUPS, 256), f32),
        ],
        compiler_params=params(8),
        cost_estimate=pl.CostEstimate(flops=2 * 2 * 256 * 4096 * 256, bytes_accessed=5_000_000, transcendentals=256 * 4096),
        name="combine",
    )(recv, mask, scale)
    new_labels, new_accum = pl.pallas_call(
        table_kernel,
        out_shape=(pltpu.HBM((16, 256, 256), f32), shape(16, 256)),
        in_specs=[VMEM] * 4 + [HBM] * 3,
        out_specs=(HBM, VMEM),
        scratch_shapes=[
            pltpu.VMEM((16, 256, 256), f32),
            pltpu.VMEM((16, 256, 256), bf16),
            pltpu.VMEM((16, 256, 256), bf16),
            pltpu.VMEM((16, 256), f32),
            pltpu.VMEM((16, 256, 256), f32),
            pltpu.VMEM((256, 128), f32),
            pltpu.SemaphoreType.DMA((3, 16 // PART)),
            pltpu.SemaphoreType.DMA((16 // PART,)),
        ],
        compiler_params=params(24),
        name="table",
    )(back, top, target, acct, in_hbm(weight), in_hbm(x), in_hbm(labels))

    return (new_labels, new_accum, query_grad, loss.reshape(256))


def solution(mesh):
    return jax.shard_map(
        shards,
        mesh=mesh,
        in_specs=(
            P("shard", None), P("shard", None), P(), P("shard"), P("shard"), P("shard"),
            P("shard", None, None), P("shard", None),
        ),
        out_specs=(P("shard", None, None), P("shard", None), P("shard", None), P("shard")),
        check_vma=False,
    )
```

```python
import jax
import jax.numpy as jnp
from jax import lax
from jax.experimental import pallas as pl
from jax.experimental.pallas import tpu as pltpu
from jax.sharding import PartitionSpec as P

STEP_RATE = 0.1
DEVS = 128
GROUP = 8
SLOTS = 32
PAIRS = 24
OUT = 56
BACK = 64
NGROUPS = DEVS // GROUP
f32 = jnp.float32
bf16 = jnp.bfloat16
i32 = jnp.int32


def iota(shape, dim):
    return lax.broadcasted_iota(i32, shape, dim)


def one(mask):
    return jnp.where(mask, 1.0, 0.0).astype(bf16)


def dot(a, b, ca=1, cb=0):
    return lax.dot_general(a, b, (((ca,), (cb,)), ((), ())), preferred_element_type=f32)


def pieces_of(x):
    hi = x.astype(bf16).astype(f32)
    rest = x - hi
    mid = rest.astype(bf16).astype(f32)
    return hi, mid, rest - mid


def total(x):
    return jnp.sum(x, axis=0, keepdims=True)


def from_rows(ref, group, chunk):
    size = GROUP * chunk
    block = ref[pl.ds(pl.multiple_of(group * size, size), size), :]
    return block.astype(f32).reshape(GROUP, chunk, 128)


def slot_rows(block, slots):
    left = block[:, :slots].reshape(GROUP * slots, 128)
    right = block[:, slots : 2 * slots].reshape(GROUP * slots, 128)
    return jnp.concatenate([left, right], axis=1).astype(bf16)


def send_block(scr, out, sems, g, chunk):
    size = GROUP * chunk
    at = pl.ds(pl.multiple_of(g * size, size), size)
    return pltpu.make_async_copy(scr.at[at, :], out.at[at, :], sems.at[g])


def route_kernel(
    cl_any, place_any, pick_any, row_any, q_any, send_any, sid_ref,
    cl_ref, place_ref, pick_ref, row_ref, q_ref, send_ref, ext_scr, in_sems, out_sems,
):
    pairs = [(cl_any, cl_ref), (place_any, place_ref), (pick_any, pick_ref), (row_any, row_ref), (q_any, q_ref)]
    copies = [pltpu.make_async_copy(a, b, in_sems.at[n]) for n, (a, b) in enumerate(pairs)]
    for copy in copies:
        copy.start()
    for copy in copies:
        copy.wait()
    c = cl_ref[...]
    ch, cl = c >> 7, c & 127
    place = place_ref[...]
    table = jnp.concatenate([(place >> 4).astype(f32), (place & 15).astype(f32)], axis=0).astype(bf16)
    i128, i16, i32s = iota((128, 256), 0), iota((16, 256), 0), iota((32, 256), 0)
    query = iota((1, 256), 1)
    queryf = query.astype(f32)
    ds, ls, ohs = [], [], []
    acc = jnp.zeros((32, 128), f32)
    for k in range(8):
        got = dot(table, one(i128 == cl[k : k + 1]))
        mine = i16 == ch[k : k + 1]
        d = total(jnp.where(mine, got[:16], 0.0)).astype(i32)
        l = total(jnp.where(mine, got[16:], 0.0)).astype(i32)
        oh = one(i128 == d)
        is_l = i16 == l
        named = jnp.concatenate([jnp.where(is_l, 1.0, 0.0), jnp.where(is_l, queryf, 0.0)], axis=0)
        acc = acc + dot(named.astype(bf16), oh, 1, 1)
        ds.append(d)
        ls.append(l)
        ohs.append(oh)
    count = acc[:16]
    middle = jnp.where(count > 1.5, jnp.floor(acc[16:] * 0.5), 255.0).astype(bf16)
    before = one(iota((256, 256), 0) < iota((256, 256), 1))
    used = jnp.zeros((128, 1), f32)
    rls, js, codes = [], [], []
    for k in range(8):
        got = dot(middle, ohs[k])
        border = total(jnp.where(i16 == ls[k], got, 0.0)).astype(i32)
        rl = jnp.where(query > border, 16, 0) + ls[k]
        ohf = ohs[k].astype(f32)
        j = total(ohf * (dot(ohs[k], before) + used)).astype(i32)
        used = used + jnp.sum(ohf, axis=1, keepdims=True)
        codes.append(jnp.where(i32s == j, (rl + 1).astype(f32), 0.0).astype(bf16))
        rls.append(rl)
        js.append(j)
    pick = pick_ref[...]
    dp = jnp.zeros((1, 256), i32)
    rlp = jnp.zeros((1, 256), i32)
    for k in range(8):
        dp = jnp.where(pick == k, ds[k], dp)
        rlp = jnp.where(pick == k, rls[k], rlp)
    ohp = one(i128 == dp)
    ohf = ohp.astype(f32)
    jp = total(ohf * (dot(ohp, before) + used)).astype(i32)
    codes.append(jnp.where(i32s == jp, (rlp + 65).astype(f32), 0.0).astype(bf16))
    code = dot(jnp.concatenate(codes, axis=1), jnp.concatenate(ohs + [ohp], axis=1), 1, 1)
    rows = dot(jnp.where(i32s == rlp, (row_ref[...] + 1).astype(f32), 0.0).astype(bf16), ohp, 1, 1)
    most = used + jnp.sum(ohf, axis=1, keepdims=True)
    full = jnp.where((used > PAIRS + 0.5) | (most > SLOTS - 0.5), 1.0, 0.0)
    full = jnp.max(full, axis=0, keepdims=True)
    ext_scr[...] = jnp.concatenate([code, rows, jnp.broadcast_to(full, (64, 128))], axis=0).T
    sid_ref[...] = jnp.concatenate(
        [d * SLOTS + j for d, j in zip(ds, js)] + rls + [dp * SLOTS + jp] + [jnp.zeros((1, 256), i32)] * 7, axis=0
    )
    sub = iota((8, 256), 0)

    def group(g, _):
        named = [sid_ref[k : k + 1, :] - g * 256 for k in range(8)]
        strips = []
        for i in range(12):
            tiles = []
            for q in (2 * i, 2 * i + 1):
                first = (q // 3) * SLOTS + (q % 3) * 8
                mask = sub == named[0] - first
                for k in range(1, 8):
                    mask = mask | (sub == named[k] - first)
                tiles.append(jnp.where(mask, 1.0, 0.0))
            strips.append(jnp.concatenate(tiles, axis=0).astype(bf16))
        rows = dot(jnp.concatenate(strips, axis=0), q_ref[...])
        left = rows[:, :128].reshape(GROUP, PAIRS, 128)
        right = rows[:, 128:].reshape(GROUP, PAIRS, 128)
        extra = ext_scr[pl.ds(pl.multiple_of(g * GROUP, GROUP), GROUP), :]
        extra = jnp.broadcast_to(extra[:, None, :], (GROUP, 8, 128))
        out = jnp.concatenate([left, right, extra], axis=1).reshape(GROUP * OUT, 128).astype(bf16)
        send_ref[pl.ds(pl.multiple_of(g * GROUP * OUT, GROUP * OUT), GROUP * OUT), :] = out
        send_block(send_ref, send_any, out_sems, g, OUT).start()
        return 0

    lax.fori_loop(0, NGROUPS, group, 0, unroll=16)
    for g in range(NGROUPS):
        send_block(send_ref, send_any, out_sems, g, OUT).wait()


def slot_major(x):
    second = pltpu.roll(x, 112, 1)
    both = jnp.concatenate(
        [x.reshape(NGROUPS, 1, GROUP, 128), second.reshape(NGROUPS, 1, GROUP, 128)], axis=1
    )
    return both.reshape(256, 128)


def owner_kernel(
    counts_ref, cc_ref, recv_ref, lab_any, x_any, tr_ref, flag_ref, stat_ref, send_any,
    x_ref, lab_ref, send_ref, ext_scr, key_scr, part_scr, pos_scr, lab_sem, x_sem, out_sems,
):
    lab_copy = pltpu.make_async_copy(lab_any, lab_ref, lab_sem)
    lab_copy.start()

    def take(g, _):
        block = from_rows(recv_ref, g, OUT)
        ext_scr[pl.ds(pl.multiple_of(g * 64, 64), 64), :] = block[:, 48:56].reshape(64, 128)
        return 0

    lax.fori_loop(0, NGROUPS, take, 0, unroll=16)
    ext = ext_scr[pl.ds(0, 128, stride=8), :]
    flag_ref[0, 0] = jnp.max(ext[:, 64:65])
    source, col = iota((128, 256), 0), iota((128, 256), 1)
    owner_of = jnp.floor((col.astype(f32) + 0.5) / PAIRS).astype(i32)
    spread = one(source == col - owner_of * PAIRS)
    codes = jnp.where((source & 7) == owner_of, dot(ext.astype(bf16), spread), 0.0)
    codes = jnp.sum(codes.reshape(NGROUPS, GROUP, 256), axis=1).astype(i32)
    rl = codes - 1
    keys = (rl & 15) * 16 + (rl >> 4) * 8 + owner_of[:16]
    key_scr[...] = jnp.where((codes > 0) & (codes < 64), keys, -1)
    sub = iota((16, 256), 0)

    def gather(g, _):
        block = from_rows(recv_ref, g, OUT)
        key = key_scr[pl.ds(g, 1), :]
        perm = jnp.concatenate([one(sub == key - 16 * i) for i in range(16)], axis=0)
        rows = jnp.concatenate([slot_rows(block, PAIRS), jnp.zeros((64, 256), bf16)], axis=0)
        x = dot(perm, rows).astype(bf16)
        for l in range(16):
            x_ref[l, pl.ds(pl.multiple_of(g * 16, 16), 16), :] = x[l * 16 : (l + 1) * 16]
        return 0

    lax.fori_loop(0, NGROUPS, gather, 0, unroll=4)
    x_copy = pltpu.make_async_copy(x_ref, x_any, x_sem)
    x_copy.start()
    raw = slot_major(pltpu.roll(ext, 96, 1)) - 1.0
    cc = cc_ref[...]
    tr_ref[...] = jnp.where(raw > -0.5, raw - cc * jnp.floor((raw + 0.5) / cc), -1.0)
    stat_ref[...] = jnp.zeros((256, 128), f32)
    lab_copy.wait()
    lane, wide = iota((16, 128), 1), iota((16, 256), 1)
    widef = wide.astype(f32)

    def cluster(l, _):
        lab = lab_ref[l]
        score = dot(x_ref[l], lab, 1, 1)
        valid = wide < counts_ref[l]
        weights, hits = [], []
        for i in range(16):
            at = slice(16 * i, 16 * i + 16)
            s = score[at]
            masked = jnp.where(valid, s, -jnp.inf)
            top = jnp.max(masked, axis=1, keepdims=True)
            weight = jnp.exp(masked - top)
            target = jnp.sum(jnp.where(lane == l, tr_ref[at, :], 0.0), axis=1, keepdims=True)
            hit = widef == target
            stat = jnp.where(lane == l, top, stat_ref[at, :])
            stat_ref[at, :] = jnp.where(lane == l + 16, jnp.sum(weight, axis=1, keepdims=True), stat)
            weights.append(weight.astype(bf16))
            hits.append(one(hit))
        both = dot(jnp.concatenate(weights + hits, axis=0), lab)
        part_scr[l] = both[:256].astype(bf16)
        pos_scr[l] = both[256:].astype(bf16)
        return 0

    lax.fori_loop(0, 16, cluster, 0, unroll=8)
    lane, own_row = iota((16, 128), 1), iota((16, 128), 0)
    own_sub = iota((16, 1), 0).astype(f32)
    wide = iota((16, 256), 1)
    home = ((wide & 7) * 32 + ((wide >> 3) & 1) * 16 + (wide >> 4)).astype(f32)
    last = iota((GROUP, 8, 128), 1) == 7

    def scatter(g, _):
        at = pl.ds(pl.multiple_of(g * 16, 16), 16)
        parts = jnp.concatenate([part_scr[l, at, :] for l in range(16)], axis=0)
        pos = jnp.concatenate([pos_scr[l, at, :] for l in range(16)], axis=0)
        codes = ext_scr[pl.ds(pl.multiple_of(g * 64, 64), 64), :]
        own, other = [], []
        for i in range(16):
            c = codes[8 * (i // 2) : 8 * (i // 2) + 8]
            c = jnp.concatenate([c, c], axis=0)
            c = jnp.where(lane == 16 * (i % 2) + own_row, c, 0.0)
            code = jnp.sum(c, axis=1, keepdims=True) + (32.0 * (i // 2) - 1.0)
            is_pos = code > 32.0 * (i // 2) + 50.0
            is_part = (code > 32.0 * (i // 2) - 0.5) & (code < 32.0 * (i // 2) + 50.0)
            own.append(one(home == jnp.where(is_part, code, -1.0)))
            other.append(one(home == jnp.where(is_pos, code - 64.0, -1.0)))
        rows = dot(jnp.concatenate(own, axis=0), parts) + dot(jnp.concatenate(other, axis=0), pos)
        hi, mid, lo = pieces_of(stat_ref[at, :])
        stat = hi + pltpu.roll(mid, 32, 1) + pltpu.roll(lo, 64, 1)
        halves = []
        for r in range(2):
            half = rows[:, 128 * r : 128 * r + 128].reshape(GROUP, SLOTS, 128)
            mine = jnp.broadcast_to(stat[8 * r : 8 * r + 8][:, None, :], (GROUP, 8, 128))
            halves += [half[:, :24], jnp.where(last, mine, half[:, 24:])]
        out = jnp.concatenate(halves, axis=1).reshape(GROUP * BACK, 128).astype(bf16)
        send_ref[pl.ds(pl.multiple_of(g * GROUP * BACK, GROUP * BACK), GROUP * BACK), :] = out
        send_block(send_ref, send_any, out_sems, g, BACK).start()
        return 0

    lax.fori_loop(0, NGROUPS, scatter, 0, unroll=8)
    x_copy.wait()
    for g in range(NGROUPS):
        send_block(send_ref, send_any, out_sems, g, BACK).wait()


def ready_kernel(
    counts_ref, sid_ref, stat_ref, trc_ref, acc_ref, x_any, lab_any,
    mask_ref, acct_ref, top_ref, tr_ref, weight_any, x_ref, lab_ref, weight_ref, sems,
):
    copies = [pltpu.make_async_copy(x_any, x_ref, sems.at[0]), pltpu.make_async_copy(lab_any, lab_ref, sems.at[1])]
    for copy in copies:
        copy.start()
    for copy in copies:
        copy.wait()
    acct_ref[...] = jnp.concatenate([acc_ref[...], jnp.zeros((112, 256), f32)], axis=0).T
    top_ref[...] = stat_ref[...].T[:16]
    r256 = iota((256, 256), 0)
    tr_ref[...] = trc_ref[...].T[:16]
    cols = jnp.concatenate([sid_ref[...].astype(f32), jnp.zeros((104, 256), f32)], axis=0).T
    lane = iota((256, 256), 1).astype(f32)

    def step(n, _):
        slot = lane + (n * 256).astype(f32)
        mask = cols[:, 0:1] == slot
        for k in range(1, 8):
            mask = mask | (cols[:, k : k + 1] == slot)
        pos = jnp.where(cols[:, 16:17] == slot, -1.0, 0.0)
        mask_ref[n] = jnp.where(mask, 1.0, pos).astype(bf16)
        score = dot(lab_ref[n], x_ref[n], 1, 1)
        weight_ref[n] = jnp.where(r256 < counts_ref[n], jnp.exp(score - top_ref[pl.ds(n, 1), :]), 0.0)
        return 0

    lax.fori_loop(0, NGROUPS, step, 0)
    copy = pltpu.make_async_copy(weight_ref, weight_any, sems.at[0])
    copy.start()
    copy.wait()


def lse_kernel(recv_ref, sid_ref, lse_ref, send_ref, scale_ref, left_scr, right_scr):
    def take(g, _):
        block = from_rows(recv_ref, g, BACK)
        at = pl.ds(pl.multiple_of(g * 64, 64), 64)
        left_scr[at, :] = block[:, 24:32].reshape(64, 128)
        right_scr[at, :] = block[:, 56:64].reshape(64, 128)
        return 0

    lax.fori_loop(0, NGROUPS, take, 0, unroll=16)
    stats = [scr[pl.ds(7, 128, stride=8), :].T for scr in (left_scr, right_scr)]
    table = jnp.concatenate(stats, axis=0).astype(bf16)
    i128, i16, i32s = iota((128, 256), 0), iota((16, 256), 0), iota((32, 256), 0)
    sid = sid_ref[...]
    tops, sums, ohs = [], [], []
    for k in range(8):
        rl = sid[8 + k : 9 + k]
        oh = one(i128 == (sid[k : k + 1] >> 5))
        got = dot(table, oh)
        got = jnp.where((rl & 16) == 0, got[:128], got[128:])
        mine = i16 == (rl & 15)
        tops.append(total(jnp.where(mine, got[:16] + got[32:48] + got[64:80], 0.0)))
        sums.append(total(jnp.where(mine, got[16:32] + got[48:64] + got[80:96], 0.0)))
        ohs.append(oh)
    largest = tops[0]
    for k in range(1, 8):
        largest = jnp.maximum(largest, tops[k])
    norm = sums[0] * jnp.exp(tops[0] - largest)
    for k in range(1, 8):
        norm = norm + sums[k] * jnp.exp(tops[k] - largest)
    lse = largest + jnp.log(norm)
    lse_ref[...] = lse
    split = pieces_of(lse)
    outs = []
    for k in range(8):
        j, rl = sid[k : k + 1] & 31, sid[8 + k : 9 + k]
        w = [jnp.where(i32s == rl, p, 0.0) for p in split]
        w += [jnp.where(i32s == j, p, 0.0) for p in pieces_of(jnp.exp(tops[k] - lse))]
        outs.append(jnp.concatenate(w, axis=0).astype(bf16))
    out = dot(jnp.concatenate(outs, axis=1), jnp.concatenate(ohs, axis=1), 1, 1)
    out = jnp.concatenate([out[:32] + out[32:64] + out[64:96], out[96:128] + out[128:160] + out[160:]], axis=0)
    out = jnp.concatenate([out, jnp.zeros((64, 128), f32)], axis=0).T
    send_ref[...] = out
    scale_ref[...] = jnp.where(iota((128, 128), 1) < 32, pltpu.roll(out, 96, 1), 0.0)


def combine_kernel(recv_ref, mask_ref, scale_ref, lse_ref, q_ref, out_ref, loss_ref, row_scr):
    r256, c256 = iota((128, 256), 0), iota((128, 256), 1)
    spread = one((r256 == (c256 & 31)) & (r256 < 32))
    wide = jnp.zeros((128, 256), f32)
    for piece in pieces_of(scale_ref[...]):
        wide = wide + dot(piece.astype(bf16), spread)
    wide = jnp.where((r256 & 7) == (c256 >> 5), wide, 0.0)
    row_scr[...] = jnp.sum(wide.reshape(NGROUPS, GROUP, 256), axis=1)

    def group(g, accs):
        acc, pos = accs
        rows = slot_rows(from_rows(recv_ref, g, BACK), SLOTS)
        scale = row_scr[pl.ds(g, 1), :]
        his, los, places = [], [], []
        for i in range(16):
            mask = mask_ref[g, 16 * i : 16 * i + 16, :].astype(f32)
            a = jnp.where(mask > 0.5, scale, 0.0)
            hi = a.astype(bf16)
            his.append(hi)
            los.append((a - hi.astype(f32)).astype(bf16))
            places.append(one(mask < -0.5))
        acc = acc + (dot(jnp.concatenate(his, axis=0), rows) + dot(jnp.concatenate(los, axis=0), rows))
        return acc, pos + dot(jnp.concatenate(places, axis=0), rows)

    zero = jnp.zeros((256, 256), f32)
    acc, pos = lax.fori_loop(0, NGROUPS, group, (zero, zero), unroll=4)
    out_ref[...] = (acc - pos).astype(bf16)
    score = jnp.sum(q_ref[...].astype(f32) * pos, axis=1, keepdims=True)
    loss_ref[...] = lse_ref[...] - jnp.broadcast_to(score, (256, 128)).T[:1]


PART = 4


def table_kernel(
    lse_ref, top_ref, tr_ref, acct_ref, weight_any, x_any, lab_any, new_any, nacc_any,
    weight_ref, x_ref, lab_ref, fac_scr, new_scr, out_scr, nacc_ref, in_sems, out_sems, nacc_sem,
):
    def inputs_of(p):
        at = pl.ds(p * PART, PART)
        pairs = [(weight_any, weight_ref), (x_any, x_ref), (lab_any, lab_ref)]
        return [pltpu.make_async_copy(a.at[at], b.at[at], in_sems.at[n, p]) for n, (a, b) in enumerate(pairs)]

    def output_of(p):
        at = pl.ds(p * PART, PART)
        return pltpu.make_async_copy(new_scr.at[at], new_any.at[at], out_sems.at[p])

    for p in range(16 // PART):
        for copy in inputs_of(p):
            copy.start()
    fac_scr[...] = jnp.exp(top_ref[...] - slot_major(lse_ref[...]).T[:16])
    out_scr[...] = jnp.zeros((256, 128), f32)
    rowf = iota((16, 256), 0).astype(f32)
    lane = iota((16, 128), 1)

    def part(p, _):
        for copy in inputs_of(p):
            copy.wait()
        for q in range(PART):
            l = p * PART + q
            fac = fac_scr[pl.ds(l, 1), :]
            target = tr_ref[pl.ds(l, 1), :]
            strips = []
            for i in range(16):
                hit = rowf == target - 16.0 * i
                strips.append((weight_ref[l, 16 * i : 16 * i + 16, :] * fac - jnp.where(hit, 1.0, 0.0)).astype(bf16))
            grad = dot(jnp.concatenate(strips, axis=0), x_ref[l])
            for i in range(16):
                at = slice(16 * i, 16 * i + 16)
                g = grad[at]
                square = g * g
                both = (square[:, :128] + square[:, 128:]) * (1.0 / 256.0)
                both = both + jnp.where(lane == l, acct_ref[at, :], 0.0)
                accum = jnp.sum(both, axis=1, keepdims=True)
                new_scr[l, at, :] = lab_ref[l, at, :].astype(f32) - g * (STEP_RATE / jnp.sqrt(accum))
                out_scr[at, :] = jnp.where(lane == l, accum, out_scr[at, :])
        output_of(p).start()
        return 0

    lax.fori_loop(0, 16 // PART, part, 0)
    nacc_ref[...] = out_scr[...].T[:16]
    nacc_copy = pltpu.make_async_copy(nacc_ref, nacc_any, nacc_sem)
    nacc_copy.start()
    nacc_copy.wait()
    for p in range(16 // PART):
        output_of(p).wait()


def params(mib):
    return pltpu.CompilerParams(vmem_limit_bytes=mib * 1024 * 1024)


def shape(*dims, dtype=f32):
    return jax.ShapeDtypeStruct(dims, dtype)


VMEM = pl.BlockSpec(memory_space=pltpu.VMEM)
SMEM = pl.BlockSpec(memory_space=pltpu.SMEM)
HBM = pl.BlockSpec(memory_space=pltpu.HBM)


def in_hbm(x):
    return pltpu.with_memory_space_constraint(x, pltpu.HBM)


def exchange(x):
    return lax.all_to_all(x, "shard", split_axis=0, concat_axis=0, tiled=True)


def ranks_of(keys):
    order = jnp.argsort(keys, stable=True)
    sorted_keys = keys[order]
    places = jnp.arange(keys.shape[0], dtype=jnp.int32)
    starts = jnp.where((places == 0) | (sorted_keys != jnp.roll(sorted_keys, 1)), places, 0)
    starts = lax.cummax(starts)
    return jnp.zeros_like(keys).at[order].set(places - starts)


def scoring(recv_q, labels):
    return jnp.einsum("csw,clw->csl", recv_q, labels, preferred_element_type=jnp.float32)


def owner_share(score, top, valid, labels):
    weight = jnp.where(valid, jnp.exp(score - top[..., None]), 0.0).astype(jnp.bfloat16)
    return jnp.einsum("csl,clw->csw", weight, labels, preferred_element_type=jnp.float32).astype(
        jnp.bfloat16
    )


def send_back(share, pos_rows, devices):
    local_blocks, slot_rows, width = share.shape
    shaped = (local_blocks, devices, slot_rows // devices, width)
    return (
        lax.all_to_all(share.reshape(shaped), "shard", split_axis=1, concat_axis=1, tiled=True),
        lax.all_to_all(pos_rows.reshape(shaped), "shard", split_axis=1, concat_axis=1, tiled=True),
    )


def general(queries, clusters, placement, pos_pick, pos_row, counts, labels, accum):
    devices = lax.axis_size("shard")
    rows_dev, width = queries.shape
    per_query = clusters.shape[1]
    local_blocks, block_rows, _ = labels.shape
    most_rows = max(2, 2 * rows_dev * per_query // (local_blocks * devices))
    all_slots = local_blocks * devices * most_rows
    slot_rows = devices * most_rows
    flat = clusters.reshape(-1)
    rank = ranks_of(flat)
    block_ids = placement[flat]
    dest = block_ids // local_blocks
    local_id = block_ids % local_blocks
    where_to = (local_id * devices + dest) * most_rows + rank
    picked = jnp.arange(per_query, dtype=jnp.int32)[None, :] == pos_pick[:, None]
    target = jnp.where(picked, pos_row[:, None], -1).reshape(-1)
    send_q = (
        jnp.zeros((all_slots, width), jnp.bfloat16)
        .at[where_to]
        .set(jnp.repeat(queries, per_query, axis=0))
    )
    send_t = jnp.full((all_slots,), -1, jnp.int32).at[where_to].set(target)
    recv_q, recv_t = (
        lax.all_to_all(
            send_q.reshape(local_blocks, devices, most_rows, width),
            "shard",
            split_axis=1,
            concat_axis=1,
            tiled=True,
        ),
        lax.all_to_all(
            send_t.reshape(local_blocks, devices, most_rows),
            "shard",
            split_axis=1,
            concat_axis=1,
            tiled=True,
        ),
    )
    recv_q = recv_q.reshape(local_blocks, slot_rows, width)
    recv_t = recv_t.reshape(local_blocks, slot_rows)
    row_ids = jnp.arange(block_rows, dtype=jnp.int32)
    valid = row_ids[None, None, :] < counts[:, None, None]
    target_row = jnp.where(recv_t >= 0, recv_t % counts[:, None], -1)
    hit = row_ids[None, None, :] == target_row[..., None]
    score = scoring(recv_q, labels)
    masked = jnp.where(valid, score, -jnp.inf)
    top = jnp.max(masked, axis=-1)
    total = jnp.sum(jnp.exp(masked - top[..., None]), axis=-1)
    spos = jnp.sum(jnp.where(hit, score, 0.0), axis=-1)
    pos_rows = jnp.einsum(
        "csl,clw->csw", hit.astype(jnp.bfloat16), labels, preferred_element_type=jnp.float32
    ).astype(jnp.bfloat16)
    stat_shape = (local_blocks, devices, most_rows)
    back_m, back_z, back_s = (
        lax.all_to_all(top.reshape(stat_shape), "shard", split_axis=1, concat_axis=1, tiled=True),
        lax.all_to_all(total.reshape(stat_shape), "shard", split_axis=1, concat_axis=1, tiled=True),
        lax.all_to_all(spos.reshape(stat_shape), "shard", split_axis=1, concat_axis=1, tiled=True),
    )
    pair_m = back_m.reshape(-1)[where_to].reshape(rows_dev, per_query)
    pair_z = back_z.reshape(-1)[where_to].reshape(rows_dev, per_query)
    pair_s = back_s.reshape(-1)[where_to].reshape(rows_dev, per_query)
    largest = jnp.max(pair_m, axis=1)
    norm = jnp.sum(pair_z * jnp.exp(pair_m - largest[:, None]), axis=1)
    lse = largest + jnp.log(norm)
    loss = lse - jnp.sum(pair_s, axis=1)
    send_l = jnp.zeros((all_slots,), jnp.float32).at[where_to].set(jnp.repeat(lse, per_query))
    recv_l = lax.all_to_all(
        send_l.reshape(stat_shape), "shard", split_axis=1, concat_axis=1, tiled=True
    ).reshape(local_blocks, slot_rows)
    prob = jnp.where(valid, jnp.exp(score - recv_l[..., None]), 0.0)
    dlogit = (prob - hit.astype(jnp.float32)).astype(jnp.bfloat16)
    label_grad = jnp.einsum("csl,csw->clw", dlogit, recv_q, preferred_element_type=jnp.float32)
    returned, returned_pos = send_back(owner_share(score, top, valid, labels), pos_rows, devices)
    pieces = (
        returned.reshape(all_slots, width)[where_to]
        .astype(jnp.float32)
        .reshape(rows_dev, per_query, width)
    )
    pos_pieces = (
        returned_pos.reshape(all_slots, width)[where_to]
        .astype(jnp.float32)
        .reshape(rows_dev, per_query, width)
    )
    scale = jnp.exp(pair_m - lse[:, None])
    query_grad = (jnp.sum(pieces * scale[..., None], axis=1) - jnp.sum(pos_pieces, axis=1)).astype(
        jnp.bfloat16
    )
    new_accum = accum + jnp.mean(label_grad * label_grad, axis=-1)
    new_labels = (
        labels.astype(jnp.float32) - STEP_RATE * label_grad / jnp.sqrt(new_accum)[..., None]
    )
    return (new_labels, new_accum, query_grad, loss)


def shards(queries, clusters, placement, pos_pick, pos_row, counts, labels, accum):
    send, sid = pl.pallas_call(
        route_kernel,
        out_shape=(pltpu.HBM((DEVS * OUT, 128), bf16), pltpu.VMEM((24, 256), i32)),
        in_specs=[HBM] * 5,
        out_specs=(HBM, VMEM),
        scratch_shapes=[
            pltpu.VMEM((8, 256), i32),
            pltpu.VMEM((16, 128), i32),
            pltpu.VMEM((1, 256), i32),
            pltpu.VMEM((1, 256), i32),
            pltpu.VMEM((256, 256), bf16),
            pltpu.VMEM((DEVS * OUT, 128), bf16),
            pltpu.VMEM((128, 128), f32),
            pltpu.SemaphoreType.DMA((5,)),
            pltpu.SemaphoreType.DMA((NGROUPS,)),
        ],
        compiler_params=params(16),
        name="route",
    )(
        in_hbm(clusters.T), in_hbm(placement.reshape(16, 128)), in_hbm(pos_pick.reshape(1, 256)),
        in_hbm(pos_row.reshape(1, 256)), in_hbm(queries),
    )
    recv = exchange(send)
    lanes = jnp.concatenate([counts.astype(f32), jnp.ones((112,), f32)]).reshape(1, 128)
    x, slot_target, flag, stat, send = pl.pallas_call(
        owner_kernel,
        out_shape=(
            pltpu.HBM((16, 256, 256), bf16), pltpu.VMEM((256, 128), f32), shape(1, 1), pltpu.VMEM((256, 128), f32),
            pltpu.HBM((DEVS * BACK, 128), bf16),
        ),
        in_specs=[SMEM, VMEM, VMEM, HBM],
        out_specs=(HBM, VMEM, SMEM, VMEM, HBM),
        scratch_shapes=[
            pltpu.VMEM((16, 256, 256), bf16),
            pltpu.VMEM((16, 256, 256), bf16),
            pltpu.VMEM((DEVS * BACK, 128), bf16),
            pltpu.VMEM((1024, 128), f32),
            pltpu.VMEM((16, 256), i32),
            pltpu.VMEM((16, 256, 256), bf16),
            pltpu.VMEM((16, 256, 256), bf16),
            pltpu.SemaphoreType.DMA,
            pltpu.SemaphoreType.DMA,
            pltpu.SemaphoreType.DMA((NGROUPS,)),
        ],
        compiler_params=params(24),
        name="owner",
    )(counts, lanes, recv, in_hbm(labels))

    def plain():
        return general(queries, clusters, placement, pos_pick, pos_row, counts, labels, accum)

    def packed():
        return finish(queries, counts, labels, accum, sid, x, slot_target, stat, send)

    return lax.cond(flag[0, 0] > 0.5, plain, packed)


def finish(queries, counts, labels, accum, sid, x, slot_target, stat, send):
    recv = exchange(send)
    mask, acct, top, target, weight = pl.pallas_call(
        ready_kernel,
        out_shape=(
            pltpu.VMEM((NGROUPS, 256, 256), bf16), pltpu.VMEM((256, 128), f32), pltpu.VMEM((16, 256), f32),
            pltpu.VMEM((16, 256), f32), pltpu.HBM((16, 256, 256), f32),
        ),
        in_specs=[SMEM] + [VMEM] * 4 + [HBM] * 2,
        out_specs=(VMEM,) * 4 + (HBM,),
        scratch_shapes=[
            pltpu.VMEM((16, 256, 256), bf16),
            pltpu.VMEM((16, 256, 256), bf16),
            pltpu.VMEM((16, 256, 256), f32),
            pltpu.SemaphoreType.DMA((2,)),
        ],
        compiler_params=params(16),
        cost_estimate=pl.CostEstimate(flops=2 * 16 * 256**3, bytes_accessed=10_000_000, transcendentals=16 * 256**2),
        name="ready",
    )(counts, sid, stat, slot_target, accum, in_hbm(x), in_hbm(labels))
    lse, send, scale = pl.pallas_call(
        lse_kernel,
        out_shape=(shape(1, 256), shape(DEVS, 128), shape(DEVS, 128)),
        in_specs=[VMEM, VMEM],
        out_specs=(VMEM,) * 3,
        scratch_shapes=[pltpu.VMEM((1024, 128), f32)] * 2,
        compiler_params=params(8),
        name="normalizer",
    )(recv, sid)
    back = exchange(send)
    query_grad, loss = pl.pallas_call(
        combine_kernel,
        out_shape=(pltpu.HBM((256, 256), bf16), pltpu.HBM((1, 256), f32)),
        in_specs=[VMEM] * 5,
        out_specs=(VMEM, VMEM),
        scratch_shapes=[
            pltpu.VMEM((NGROUPS, 256), f32),
        ],
        compiler_params=params(8),
        cost_estimate=pl.CostEstimate(flops=2 * 2 * 256 * 4096 * 256, bytes_accessed=5_000_000, transcendentals=256 * 4096),
        name="combine",
    )(recv, mask, scale, lse, queries)
    new_labels, new_accum = pl.pallas_call(
        table_kernel,
        out_shape=(pltpu.HBM((16, 256, 256), f32), pltpu.HBM((16, 256), f32)),
        in_specs=[VMEM] * 4 + [HBM] * 3,
        out_specs=(HBM, HBM),
        scratch_shapes=[
            pltpu.VMEM((16, 256, 256), f32),
            pltpu.VMEM((16, 256, 256), bf16),
            pltpu.VMEM((16, 256, 256), bf16),
            pltpu.VMEM((16, 256), f32),
            pltpu.VMEM((16, 256, 256), f32),
            pltpu.VMEM((256, 128), f32),
            pltpu.VMEM((16, 256), f32),
            pltpu.SemaphoreType.DMA((3, 16 // PART)),
            pltpu.SemaphoreType.DMA((16 // PART,)),
            pltpu.SemaphoreType.DMA,
        ],
        compiler_params=params(24),
        name="table",
    )(back, top, target, acct, in_hbm(weight), in_hbm(x), in_hbm(labels))

    return (new_labels, new_accum, query_grad, loss.reshape(256))


def solution(mesh):
    return jax.shard_map(
        shards,
        mesh=mesh,
        in_specs=(
            P("shard", None), P("shard", None), P(), P("shard"), P("shard"), P("shard"),
            P("shard", None, None), P("shard", None),
        ),
        out_specs=(P("shard", None, None), P("shard", None), P("shard", None), P("shard")),
        check_vma=False,
    )
```

```python
import jax
import jax.numpy as jnp
from jax import lax
from jax.experimental import pallas as pl
from jax.experimental.pallas import tpu as pltpu
from jax.sharding import PartitionSpec as P

STEP_RATE = 0.1
DEVS = 128
GROUP = 8
SLOTS = 32
PAIRS = 24
OUT = 56
BACK = 64
NGROUPS = DEVS // GROUP
f32 = jnp.float32
bf16 = jnp.bfloat16
i32 = jnp.int32


def iota(shape, dim):
    return lax.broadcasted_iota(i32, shape, dim)


def one(mask):
    return jnp.where(mask, 1.0, 0.0).astype(bf16)


def one16(mask):
    return jnp.where(mask, jnp.ones((), bf16), jnp.zeros((), bf16))


def dot(a, b, ca=1, cb=0):
    return lax.dot_general(a, b, (((ca,), (cb,)), ((), ())), preferred_element_type=f32)


def pieces_of(x):
    hi = x.astype(bf16).astype(f32)
    rest = x - hi
    mid = rest.astype(bf16).astype(f32)
    return hi, mid, rest - mid


def total(x):
    return jnp.sum(x, axis=0, keepdims=True)


def from_rows(ref, group, chunk):
    size = GROUP * chunk
    block = ref[pl.ds(pl.multiple_of(group * size, size), size), :]
    return block.astype(f32).reshape(GROUP, chunk, 128)


def slot_rows(block, slots):
    left = block[:, :slots].reshape(GROUP * slots, 128)
    right = block[:, slots : 2 * slots].reshape(GROUP * slots, 128)
    return jnp.concatenate([left, right], axis=1).astype(bf16)


def send_block(scr, out, sems, g, chunk):
    size = GROUP * chunk
    at = pl.ds(pl.multiple_of(g * size, size), size)
    return pltpu.make_async_copy(scr.at[at, :], out.at[at, :], sems.at[g])


def route_kernel(
    cl_any, place_any, pick_any, row_any, q_any, send_any, sid_ref,
    cl_ref, place_ref, pick_ref, row_ref, q_ref, send_ref, ext_scr, in_sems, out_sems,
):
    pairs = [(cl_any, cl_ref), (place_any, place_ref), (pick_any, pick_ref), (row_any, row_ref), (q_any, q_ref)]
    copies = [pltpu.make_async_copy(a, b, in_sems.at[n]) for n, (a, b) in enumerate(pairs)]
    for copy in copies:
        copy.start()
    for copy in copies:
        copy.wait()
    c = cl_ref[...]
    ch, cl = c >> 7, c & 127
    place = place_ref[...]
    table = jnp.concatenate([(place >> 4).astype(f32), (place & 15).astype(f32)], axis=0).astype(bf16)
    i128, i16, i32s = iota((128, 256), 0), iota((16, 256), 0), iota((32, 256), 0)
    query = iota((1, 256), 1)
    queryf = query.astype(f32)
    ds, ls, ohs = [], [], []
    acc = jnp.zeros((32, 128), f32)
    for k in range(8):
        got = dot(table, one(i128 == cl[k : k + 1]))
        mine = i16 == ch[k : k + 1]
        d = total(jnp.where(mine, got[:16], 0.0)).astype(i32)
        l = total(jnp.where(mine, got[16:], 0.0)).astype(i32)
        oh = one(i128 == d)
        is_l = i16 == l
        named = jnp.concatenate([jnp.where(is_l, 1.0, 0.0), jnp.where(is_l, queryf, 0.0)], axis=0)
        acc = acc + dot(named.astype(bf16), oh, 1, 1)
        ds.append(d)
        ls.append(l)
        ohs.append(oh)
    count = acc[:16]
    middle = jnp.where(count > 1.5, jnp.floor(acc[16:] * 0.5), 255.0).astype(bf16)
    before = one(iota((256, 256), 0) < iota((256, 256), 1))
    used = jnp.zeros((128, 1), f32)
    rls, js, codes = [], [], []
    for k in range(8):
        got = dot(middle, ohs[k])
        border = total(jnp.where(i16 == ls[k], got, 0.0)).astype(i32)
        rl = jnp.where(query > border, 16, 0) + ls[k]
        ohf = ohs[k].astype(f32)
        j = total(ohf * (dot(ohs[k], before) + used)).astype(i32)
        used = used + jnp.sum(ohf, axis=1, keepdims=True)
        codes.append(jnp.where(i32s == j, (rl + 1).astype(f32), 0.0).astype(bf16))
        rls.append(rl)
        js.append(j)
    pick = pick_ref[...]
    dp = jnp.zeros((1, 256), i32)
    rlp = jnp.zeros((1, 256), i32)
    for k in range(8):
        dp = jnp.where(pick == k, ds[k], dp)
        rlp = jnp.where(pick == k, rls[k], rlp)
    ohp = one(i128 == dp)
    ohf = ohp.astype(f32)
    jp = total(ohf * (dot(ohp, before) + used)).astype(i32)
    codes.append(jnp.where(i32s == jp, (rlp + 65).astype(f32), 0.0).astype(bf16))
    code = dot(jnp.concatenate(codes, axis=1), jnp.concatenate(ohs + [ohp], axis=1), 1, 1)
    rows = dot(jnp.where(i32s == rlp, (row_ref[...] + 1).astype(f32), 0.0).astype(bf16), ohp, 1, 1)
    most = used + jnp.sum(ohf, axis=1, keepdims=True)
    full = jnp.where((used > PAIRS + 0.5) | (most > SLOTS - 0.5), 1.0, 0.0)
    full = jnp.max(full, axis=0, keepdims=True)
    ext_scr[...] = jnp.concatenate([code, rows, jnp.broadcast_to(full, (64, 128))], axis=0).T
    sid_ref[...] = jnp.concatenate(
        [d * SLOTS + j for d, j in zip(ds, js)] + rls + [dp * SLOTS + jp] + [jnp.zeros((1, 256), i32)] * 7, axis=0
    )
    sub = iota((16, 256), 0)

    def group(g, _):
        named = jnp.clip(sid_ref[:8, :] - g * 256, -1, 256).astype(f32).astype(bf16)
        named = [jnp.broadcast_to(named[k : k + 1], (16, 256)) for k in range(8)]
        strips = []
        for i in range(12):
            places = [(q // 3) * SLOTS + (q % 3) * 8 for q in (2 * i, 2 * i + 1)]
            at = (jnp.where(sub < 8, places[0], places[1] - 8) + sub).astype(f32).astype(bf16)
            mask = at == named[0]
            for k in range(1, 8):
                mask = mask | (at == named[k])
            strips.append(one16(mask))
        rows = dot(jnp.concatenate(strips, axis=0), q_ref[...])
        left = rows[:, :128].reshape(GROUP, PAIRS, 128)
        right = rows[:, 128:].reshape(GROUP, PAIRS, 128)
        extra = ext_scr[pl.ds(pl.multiple_of(g * GROUP, GROUP), GROUP), :]
        extra = jnp.broadcast_to(extra[:, None, :], (GROUP, 8, 128))
        out = jnp.concatenate([left, right, extra], axis=1).reshape(GROUP * OUT, 128).astype(bf16)
        send_ref[pl.ds(pl.multiple_of(g * GROUP * OUT, GROUP * OUT), GROUP * OUT), :] = out
        send_block(send_ref, send_any, out_sems, g, OUT).start()
        return 0

    lax.fori_loop(0, NGROUPS, group, 0, unroll=16)
    for g in range(NGROUPS):
        send_block(send_ref, send_any, out_sems, g, OUT).wait()


def slot_major(x):
    second = pltpu.roll(x, 112, 1)
    both = jnp.concatenate(
        [x.reshape(NGROUPS, 1, GROUP, 128), second.reshape(NGROUPS, 1, GROUP, 128)], axis=1
    )
    return both.reshape(256, 128)


def owner_kernel(
    counts_ref, cc_ref, recv_ref, lab_any, x_any, tr_ref, flag_ref, stat_ref, send_any,
    x_ref, lab_ref, send_ref, ext_scr, key_scr, part_scr, pos_scr, lab_sem, x_sem, out_sems,
):
    lab_copy = pltpu.make_async_copy(lab_any, lab_ref, lab_sem)
    lab_copy.start()

    def take(g, _):
        block = from_rows(recv_ref, g, OUT)
        ext_scr[pl.ds(pl.multiple_of(g * 64, 64), 64), :] = block[:, 48:56].reshape(64, 128)
        return 0

    lax.fori_loop(0, NGROUPS, take, 0, unroll=16)
    ext = ext_scr[pl.ds(0, 128, stride=8), :]
    flag_ref[0, 0] = jnp.max(ext[:, 64:65]).astype(i32)
    source, col = iota((128, 256), 0), iota((128, 256), 1)
    owner_of = jnp.floor((col.astype(f32) + 0.5) / PAIRS).astype(i32)
    spread = one(source == col - owner_of * PAIRS)
    codes = jnp.where((source & 7) == owner_of, dot(ext.astype(bf16), spread), 0.0)
    codes = jnp.sum(codes.reshape(NGROUPS, GROUP, 256), axis=1).astype(i32)
    rl = codes - 1
    keys = (rl & 15) * 16 + (rl >> 4) * 8 + owner_of[:16]
    key_scr[...] = jnp.where((codes > 0) & (codes < 64), keys, -1)
    sub = iota((16, 256), 0)

    def gather(g, _):
        block = from_rows(recv_ref, g, OUT)
        key = key_scr[pl.ds(g, 1), :]
        perm = jnp.concatenate([one(sub == key - 16 * i) for i in range(16)], axis=0)
        rows = jnp.concatenate([slot_rows(block, PAIRS), jnp.zeros((64, 256), bf16)], axis=0)
        x = dot(perm, rows).astype(bf16)
        for l in range(16):
            x_ref[l, pl.ds(pl.multiple_of(g * 16, 16), 16), :] = x[l * 16 : (l + 1) * 16]
        return 0

    lax.fori_loop(0, NGROUPS, gather, 0, unroll=4)
    x_copy = pltpu.make_async_copy(x_ref, x_any, x_sem)
    x_copy.start()
    raw = slot_major(pltpu.roll(ext, 96, 1)) - 1.0
    cc = cc_ref[...]
    tr_ref[...] = jnp.where(raw > -0.5, raw - cc * jnp.floor((raw + 0.5) / cc), -1.0)
    stat_ref[...] = jnp.zeros((256, 128), f32)
    lab_copy.wait()
    lane, wide = iota((16, 128), 1), iota((16, 256), 1)
    widef = wide.astype(f32)

    def cluster(l, _):
        lab = lab_ref[l]
        score = dot(x_ref[l], lab, 1, 1)
        valid = wide < counts_ref[l]
        weights, hits = [], []
        for i in range(16):
            at = slice(16 * i, 16 * i + 16)
            s = score[at]
            masked = jnp.where(valid, s, -jnp.inf)
            top = jnp.max(masked, axis=1, keepdims=True)
            weight = jnp.exp(masked - top)
            target = jnp.sum(jnp.where(lane == l, tr_ref[at, :], 0.0), axis=1, keepdims=True)
            hit = widef == target
            stat = jnp.where(lane == l, top, stat_ref[at, :])
            stat_ref[at, :] = jnp.where(lane == l + 16, jnp.sum(weight, axis=1, keepdims=True), stat)
            weights.append(weight.astype(bf16))
            hits.append(one(hit))
        both = dot(jnp.concatenate(weights + hits, axis=0), lab)
        part_scr[l] = both[:256].astype(bf16)
        pos_scr[l] = both[256:].astype(bf16)
        return 0

    lax.fori_loop(0, 16, cluster, 0, unroll=8)
    lane, own_row = iota((16, 128), 1), iota((16, 128), 0)
    own_sub = iota((16, 1), 0).astype(f32)
    wide = iota((16, 256), 1)
    home = ((wide & 7) * 32 + ((wide >> 3) & 1) * 16 + (wide >> 4)).astype(f32)
    last = iota((GROUP, 8, 128), 1) == 7

    def scatter(g, _):
        at = pl.ds(pl.multiple_of(g * 16, 16), 16)
        parts = jnp.concatenate([part_scr[l, at, :] for l in range(16)], axis=0)
        pos = jnp.concatenate([pos_scr[l, at, :] for l in range(16)], axis=0)
        codes = ext_scr[pl.ds(pl.multiple_of(g * 64, 64), 64), :]
        own, other = [], []
        for i in range(16):
            c = codes[8 * (i // 2) : 8 * (i // 2) + 8]
            c = jnp.concatenate([c, c], axis=0)
            c = jnp.where(lane == 16 * (i % 2) + own_row, c, 0.0)
            code = jnp.sum(c, axis=1, keepdims=True) + (32.0 * (i // 2) - 1.0)
            is_pos = code > 32.0 * (i // 2) + 50.0
            is_part = (code > 32.0 * (i // 2) - 0.5) & (code < 32.0 * (i // 2) + 50.0)
            own.append(one(home == jnp.where(is_part, code, -1.0)))
            other.append(one(home == jnp.where(is_pos, code - 64.0, -1.0)))
        rows = dot(jnp.concatenate(own, axis=0), parts) + dot(jnp.concatenate(other, axis=0), pos)
        hi, mid, lo = pieces_of(stat_ref[at, :])
        stat = hi + pltpu.roll(mid, 32, 1) + pltpu.roll(lo, 64, 1)
        halves = []
        for r in range(2):
            half = rows[:, 128 * r : 128 * r + 128].reshape(GROUP, SLOTS, 128)
            mine = jnp.broadcast_to(stat[8 * r : 8 * r + 8][:, None, :], (GROUP, 8, 128))
            halves += [half[:, :24], jnp.where(last, mine, half[:, 24:])]
        out = jnp.concatenate(halves, axis=1).reshape(GROUP * BACK, 128).astype(bf16)
        send_ref[pl.ds(pl.multiple_of(g * GROUP * BACK, GROUP * BACK), GROUP * BACK), :] = out
        send_block(send_ref, send_any, out_sems, g, BACK).start()
        return 0

    lax.fori_loop(0, NGROUPS, scatter, 0, unroll=8)
    x_copy.wait()
    for g in range(NGROUPS):
        send_block(send_ref, send_any, out_sems, g, BACK).wait()


def ready_kernel(
    counts_ref, sid_ref, stat_ref, trc_ref, acc_ref, x_any, lab_any,
    mask_ref, acct_ref, top_ref, tr_ref, weight_any, x_ref, lab_ref, weight_ref, sems,
):
    copies = [pltpu.make_async_copy(x_any, x_ref, sems.at[0]), pltpu.make_async_copy(lab_any, lab_ref, sems.at[1])]
    for copy in copies:
        copy.start()
    for copy in copies:
        copy.wait()
    acct_ref[...] = jnp.concatenate([acc_ref[...], jnp.zeros((112, 256), f32)], axis=0).T
    top_ref[...] = stat_ref[...].T[:16]
    r256 = iota((256, 256), 0)
    tr_ref[...] = trc_ref[...].T[:16]
    cols = jnp.concatenate([sid_ref[...].astype(f32), jnp.zeros((104, 256), f32)], axis=0).T
    lane = iota((256, 256), 1).astype(f32)

    def step(n, _):
        slot = lane + (n * 256).astype(f32)
        mask = cols[:, 0:1] == slot
        for k in range(1, 8):
            mask = mask | (cols[:, k : k + 1] == slot)
        pos = jnp.where(cols[:, 16:17] == slot, -1.0, 0.0)
        mask_ref[n] = jnp.where(mask, 1.0, pos).astype(bf16)
        score = dot(lab_ref[n], x_ref[n], 1, 1)
        weight_ref[n] = jnp.where(r256 < counts_ref[n], jnp.exp(score - top_ref[pl.ds(n, 1), :]), 0.0)
        return 0

    lax.fori_loop(0, NGROUPS, step, 0)
    copy = pltpu.make_async_copy(weight_ref, weight_any, sems.at[0])
    copy.start()
    copy.wait()


def lse_kernel(recv_ref, sid_ref, lse_ref, send_ref, scale_ref, left_scr, right_scr):
    def take(g, _):
        block = from_rows(recv_ref, g, BACK)
        at = pl.ds(pl.multiple_of(g * 64, 64), 64)
        left_scr[at, :] = block[:, 24:32].reshape(64, 128)
        right_scr[at, :] = block[:, 56:64].reshape(64, 128)
        return 0

    lax.fori_loop(0, NGROUPS, take, 0, unroll=16)
    stats = [scr[pl.ds(7, 128, stride=8), :].T for scr in (left_scr, right_scr)]
    table = jnp.concatenate(stats, axis=0).astype(bf16)
    i128, i16, i32s = iota((128, 256), 0), iota((16, 256), 0), iota((32, 256), 0)
    sid = sid_ref[...]
    tops, sums, ohs = [], [], []
    for k in range(8):
        rl = sid[8 + k : 9 + k]
        oh = one(i128 == (sid[k : k + 1] >> 5))
        got = dot(table, oh)
        got = jnp.where((rl & 16) == 0, got[:128], got[128:])
        mine = i16 == (rl & 15)
        tops.append(total(jnp.where(mine, got[:16] + got[32:48] + got[64:80], 0.0)))
        sums.append(total(jnp.where(mine, got[16:32] + got[48:64] + got[80:96], 0.0)))
        ohs.append(oh)
    largest = tops[0]
    for k in range(1, 8):
        largest = jnp.maximum(largest, tops[k])
    norm = sums[0] * jnp.exp(tops[0] - largest)
    for k in range(1, 8):
        norm = norm + sums[k] * jnp.exp(tops[k] - largest)
    lse = largest + jnp.log(norm)
    lse_ref[...] = lse
    split = pieces_of(lse)
    outs = []
    for k in range(8):
        j, rl = sid[k : k + 1] & 31, sid[8 + k : 9 + k]
        w = [jnp.where(i32s == rl, p, 0.0) for p in split]
        w += [jnp.where(i32s == j, p, 0.0) for p in pieces_of(jnp.exp(tops[k] - lse))]
        outs.append(jnp.concatenate(w, axis=0).astype(bf16))
    out = dot(jnp.concatenate(outs, axis=1), jnp.concatenate(ohs, axis=1), 1, 1)
    out = jnp.concatenate([out[:32] + out[32:64] + out[64:96], out[96:128] + out[128:160] + out[160:]], axis=0)
    out = jnp.concatenate([out, jnp.zeros((64, 128), f32)], axis=0).T
    send_ref[...] = out
    scale_ref[...] = jnp.where(iota((128, 128), 1) < 32, pltpu.roll(out, 96, 1), 0.0)


def combine_kernel(recv_ref, mask_ref, scale_ref, lse_ref, q_ref, out_ref, loss_ref, row_scr):
    r256, c256 = iota((128, 256), 0), iota((128, 256), 1)
    spread = one((r256 == (c256 & 31)) & (r256 < 32))
    wide = jnp.zeros((128, 256), f32)
    for piece in pieces_of(scale_ref[...]):
        wide = wide + dot(piece.astype(bf16), spread)
    wide = jnp.where((r256 & 7) == (c256 >> 5), wide, 0.0)
    row_scr[...] = jnp.sum(wide.reshape(NGROUPS, GROUP, 256), axis=1)

    def group(g, accs):
        acc, pos = accs
        rows = slot_rows(from_rows(recv_ref, g, BACK), SLOTS)
        scale = row_scr[pl.ds(g, 1), :]
        his, los, places = [], [], []
        for i in range(16):
            mask = mask_ref[g, 16 * i : 16 * i + 16, :].astype(f32)
            a = jnp.where(mask > 0.5, scale, 0.0)
            hi = a.astype(bf16)
            his.append(hi)
            los.append((a - hi.astype(f32)).astype(bf16))
            places.append(one(mask < -0.5))
        acc = acc + (dot(jnp.concatenate(his, axis=0), rows) + dot(jnp.concatenate(los, axis=0), rows))
        return acc, pos + dot(jnp.concatenate(places, axis=0), rows)

    zero = jnp.zeros((256, 256), f32)
    acc, pos = lax.fori_loop(0, NGROUPS, group, (zero, zero), unroll=4)
    out_ref[...] = (acc - pos).astype(bf16)
    score = jnp.sum(q_ref[...].astype(f32) * pos, axis=1, keepdims=True)
    loss_ref[...] = lse_ref[...] - jnp.broadcast_to(score, (256, 128)).T[:1]


PART = 4


def table_kernel(
    lse_ref, top_ref, tr_ref, acct_ref, weight_any, x_any, lab_any, new_any, nacc_any,
    weight_ref, x_ref, lab_ref, fac_scr, new_scr, out_scr, nacc_ref, in_sems, out_sems, nacc_sem,
):
    def inputs_of(p):
        at = pl.ds(p * PART, PART)
        pairs = [(weight_any, weight_ref), (x_any, x_ref), (lab_any, lab_ref)]
        return [pltpu.make_async_copy(a.at[at], b.at[at], in_sems.at[n, p]) for n, (a, b) in enumerate(pairs)]

    def output_of(p):
        at = pl.ds(p * PART, PART)
        return pltpu.make_async_copy(new_scr.at[at], new_any.at[at], out_sems.at[p])

    for p in range(16 // PART):
        for copy in inputs_of(p):
            copy.start()
    fac_scr[...] = jnp.exp(top_ref[...] - slot_major(lse_ref[...]).T[:16])
    out_scr[...] = jnp.zeros((256, 128), f32)
    rowf = iota((16, 256), 0).astype(f32)
    lane = iota((16, 128), 1)

    def part(p, _):
        for copy in inputs_of(p):
            copy.wait()
        for q in range(PART):
            l = p * PART + q
            fac = fac_scr[pl.ds(l, 1), :]
            target = tr_ref[pl.ds(l, 1), :]
            strips = []
            for i in range(16):
                hit = rowf == target - 16.0 * i
                strips.append((weight_ref[l, 16 * i : 16 * i + 16, :] * fac - jnp.where(hit, 1.0, 0.0)).astype(bf16))
            grad = dot(jnp.concatenate(strips, axis=0), x_ref[l])
            for i in range(16):
                at = slice(16 * i, 16 * i + 16)
                g = grad[at]
                square = g * g
                both = (square[:, :128] + square[:, 128:]) * (1.0 / 256.0)
                both = both + jnp.where(lane == l, acct_ref[at, :], 0.0)
                accum = jnp.sum(both, axis=1, keepdims=True)
                new_scr[l, at, :] = lab_ref[l, at, :].astype(f32) - g * (STEP_RATE / jnp.sqrt(accum))
                out_scr[at, :] = jnp.where(lane == l, accum, out_scr[at, :])
        output_of(p).start()
        return 0

    lax.fori_loop(0, 16 // PART, part, 0)
    nacc_ref[...] = out_scr[...].T[:16]
    nacc_copy = pltpu.make_async_copy(nacc_ref, nacc_any, nacc_sem)
    nacc_copy.start()
    nacc_copy.wait()
    for p in range(16 // PART):
        output_of(p).wait()


def params(mib):
    return pltpu.CompilerParams(vmem_limit_bytes=mib * 1024 * 1024)


def shape(*dims, dtype=f32):
    return jax.ShapeDtypeStruct(dims, dtype)


VMEM = pl.BlockSpec(memory_space=pltpu.VMEM)
SMEM = pl.BlockSpec(memory_space=pltpu.SMEM)
HBM = pl.BlockSpec(memory_space=pltpu.HBM)


def in_hbm(x):
    return pltpu.with_memory_space_constraint(x, pltpu.HBM)


def exchange(x):
    return lax.all_to_all(x, "shard", split_axis=0, concat_axis=0, tiled=True)


def ranks_of(keys):
    order = jnp.argsort(keys, stable=True)
    sorted_keys = keys[order]
    places = jnp.arange(keys.shape[0], dtype=jnp.int32)
    starts = jnp.where((places == 0) | (sorted_keys != jnp.roll(sorted_keys, 1)), places, 0)
    starts = lax.cummax(starts)
    return jnp.zeros_like(keys).at[order].set(places - starts)


def scoring(recv_q, labels):
    return jnp.einsum("csw,clw->csl", recv_q, labels, preferred_element_type=jnp.float32)


def owner_share(score, top, valid, labels):
    weight = jnp.where(valid, jnp.exp(score - top[..., None]), 0.0).astype(jnp.bfloat16)
    return jnp.einsum("csl,clw->csw", weight, labels, preferred_element_type=jnp.float32).astype(
        jnp.bfloat16
    )


def send_back(share, pos_rows, devices):
    local_blocks, slot_rows, width = share.shape
    shaped = (local_blocks, devices, slot_rows // devices, width)
    return (
        lax.all_to_all(share.reshape(shaped), "shard", split_axis=1, concat_axis=1, tiled=True),
        lax.all_to_all(pos_rows.reshape(shaped), "shard", split_axis=1, concat_axis=1, tiled=True),
    )


def general(queries, clusters, placement, pos_pick, pos_row, counts, labels, accum):
    devices = lax.axis_size("shard")
    rows_dev, width = queries.shape
    per_query = clusters.shape[1]
    local_blocks, block_rows, _ = labels.shape
    most_rows = max(2, 2 * rows_dev * per_query // (local_blocks * devices))
    all_slots = local_blocks * devices * most_rows
    slot_rows = devices * most_rows
    flat = clusters.reshape(-1)
    rank = ranks_of(flat)
    block_ids = placement[flat]
    dest = block_ids // local_blocks
    local_id = block_ids % local_blocks
    where_to = (local_id * devices + dest) * most_rows + rank
    picked = jnp.arange(per_query, dtype=jnp.int32)[None, :] == pos_pick[:, None]
    target = jnp.where(picked, pos_row[:, None], -1).reshape(-1)
    send_q = (
        jnp.zeros((all_slots, width), jnp.bfloat16)
        .at[where_to]
        .set(jnp.repeat(queries, per_query, axis=0))
    )
    send_t = jnp.full((all_slots,), -1, jnp.int32).at[where_to].set(target)
    recv_q, recv_t = (
        lax.all_to_all(
            send_q.reshape(local_blocks, devices, most_rows, width),
            "shard",
            split_axis=1,
            concat_axis=1,
            tiled=True,
        ),
        lax.all_to_all(
            send_t.reshape(local_blocks, devices, most_rows),
            "shard",
            split_axis=1,
            concat_axis=1,
            tiled=True,
        ),
    )
    recv_q = recv_q.reshape(local_blocks, slot_rows, width)
    recv_t = recv_t.reshape(local_blocks, slot_rows)
    row_ids = jnp.arange(block_rows, dtype=jnp.int32)
    valid = row_ids[None, None, :] < counts[:, None, None]
    target_row = jnp.where(recv_t >= 0, recv_t % counts[:, None], -1)
    hit = row_ids[None, None, :] == target_row[..., None]
    score = scoring(recv_q, labels)
    masked = jnp.where(valid, score, -jnp.inf)
    top = jnp.max(masked, axis=-1)
    total = jnp.sum(jnp.exp(masked - top[..., None]), axis=-1)
    spos = jnp.sum(jnp.where(hit, score, 0.0), axis=-1)
    pos_rows = jnp.einsum(
        "csl,clw->csw", hit.astype(jnp.bfloat16), labels, preferred_element_type=jnp.float32
    ).astype(jnp.bfloat16)
    stat_shape = (local_blocks, devices, most_rows)
    back_m, back_z, back_s = (
        lax.all_to_all(top.reshape(stat_shape), "shard", split_axis=1, concat_axis=1, tiled=True),
        lax.all_to_all(total.reshape(stat_shape), "shard", split_axis=1, concat_axis=1, tiled=True),
        lax.all_to_all(spos.reshape(stat_shape), "shard", split_axis=1, concat_axis=1, tiled=True),
    )
    pair_m = back_m.reshape(-1)[where_to].reshape(rows_dev, per_query)
    pair_z = back_z.reshape(-1)[where_to].reshape(rows_dev, per_query)
    pair_s = back_s.reshape(-1)[where_to].reshape(rows_dev, per_query)
    largest = jnp.max(pair_m, axis=1)
    norm = jnp.sum(pair_z * jnp.exp(pair_m - largest[:, None]), axis=1)
    lse = largest + jnp.log(norm)
    loss = lse - jnp.sum(pair_s, axis=1)
    send_l = jnp.zeros((all_slots,), jnp.float32).at[where_to].set(jnp.repeat(lse, per_query))
    recv_l = lax.all_to_all(
        send_l.reshape(stat_shape), "shard", split_axis=1, concat_axis=1, tiled=True
    ).reshape(local_blocks, slot_rows)
    prob = jnp.where(valid, jnp.exp(score - recv_l[..., None]), 0.0)
    dlogit = (prob - hit.astype(jnp.float32)).astype(jnp.bfloat16)
    label_grad = jnp.einsum("csl,csw->clw", dlogit, recv_q, preferred_element_type=jnp.float32)
    returned, returned_pos = send_back(owner_share(score, top, valid, labels), pos_rows, devices)
    pieces = (
        returned.reshape(all_slots, width)[where_to]
        .astype(jnp.float32)
        .reshape(rows_dev, per_query, width)
    )
    pos_pieces = (
        returned_pos.reshape(all_slots, width)[where_to]
        .astype(jnp.float32)
        .reshape(rows_dev, per_query, width)
    )
    scale = jnp.exp(pair_m - lse[:, None])
    query_grad = (jnp.sum(pieces * scale[..., None], axis=1) - jnp.sum(pos_pieces, axis=1)).astype(
        jnp.bfloat16
    )
    new_accum = accum + jnp.mean(label_grad * label_grad, axis=-1)
    new_labels = (
        labels.astype(jnp.float32) - STEP_RATE * label_grad / jnp.sqrt(new_accum)[..., None]
    )
    return (new_labels, new_accum, query_grad, loss)


def shards(queries, clusters, placement, pos_pick, pos_row, counts, labels, accum):
    send, sid = pl.pallas_call(
        route_kernel,
        out_shape=(pltpu.HBM((DEVS * OUT, 128), bf16), pltpu.VMEM((24, 256), i32)),
        in_specs=[HBM] * 5,
        out_specs=(HBM, VMEM),
        scratch_shapes=[
            pltpu.VMEM((8, 256), i32),
            pltpu.VMEM((16, 128), i32),
            pltpu.VMEM((1, 256), i32),
            pltpu.VMEM((1, 256), i32),
            pltpu.VMEM((256, 256), bf16),
            pltpu.VMEM((DEVS * OUT, 128), bf16),
            pltpu.VMEM((128, 128), f32),
            pltpu.SemaphoreType.DMA((5,)),
            pltpu.SemaphoreType.DMA((NGROUPS,)),
        ],
        compiler_params=params(16),
        name="route",
    )(
        in_hbm(clusters.T), in_hbm(placement.reshape(16, 128)), in_hbm(pos_pick.reshape(1, 256)),
        in_hbm(pos_row.reshape(1, 256)), in_hbm(queries),
    )
    recv = exchange(send)
    lanes = jnp.concatenate([counts.astype(f32), jnp.ones((112,), f32)]).reshape(1, 128)
    x, slot_target, flag, stat, send = pl.pallas_call(
        owner_kernel,
        out_shape=(
            pltpu.HBM((16, 256, 256), bf16), pltpu.VMEM((256, 128), f32), shape(1, 1, dtype=i32), pltpu.VMEM((256, 128), f32),
            pltpu.HBM((DEVS * BACK, 128), bf16),
        ),
        in_specs=[SMEM, VMEM, VMEM, HBM],
        out_specs=(HBM, VMEM, SMEM, VMEM, HBM),
        scratch_shapes=[
            pltpu.VMEM((16, 256, 256), bf16),
            pltpu.VMEM((16, 256, 256), bf16),
            pltpu.VMEM((DEVS * BACK, 128), bf16),
            pltpu.VMEM((1024, 128), f32),
            pltpu.VMEM((16, 256), i32),
            pltpu.VMEM((16, 256, 256), bf16),
            pltpu.VMEM((16, 256, 256), bf16),
            pltpu.SemaphoreType.DMA,
            pltpu.SemaphoreType.DMA,
            pltpu.SemaphoreType.DMA((NGROUPS,)),
        ],
        compiler_params=params(24),
        name="owner",
    )(counts, lanes, recv, in_hbm(labels))

    def plain():
        return general(queries, clusters, placement, pos_pick, pos_row, counts, labels, accum)

    def packed():
        return finish(queries, counts, labels, accum, sid, x, slot_target, stat, send)

    return lax.switch(flag[0, 0], [packed, plain])


def finish(queries, counts, labels, accum, sid, x, slot_target, stat, send):
    recv = exchange(send)
    mask, acct, top, target, weight = pl.pallas_call(
        ready_kernel,
        out_shape=(
            pltpu.VMEM((NGROUPS, 256, 256), bf16), pltpu.VMEM((256, 128), f32), pltpu.VMEM((16, 256), f32),
            pltpu.VMEM((16, 256), f32), pltpu.HBM((16, 256, 256), f32),
        ),
        in_specs=[SMEM] + [VMEM] * 4 + [HBM] * 2,
        out_specs=(VMEM,) * 4 + (HBM,),
        scratch_shapes=[
            pltpu.VMEM((16, 256, 256), bf16),
            pltpu.VMEM((16, 256, 256), bf16),
            pltpu.VMEM((16, 256, 256), f32),
            pltpu.SemaphoreType.DMA((2,)),
        ],
        compiler_params=params(16),
        cost_estimate=pl.CostEstimate(flops=2 * 16 * 256**3, bytes_accessed=10_000_000, transcendentals=16 * 256**2),
        name="ready",
    )(counts, sid, stat, slot_target, accum, in_hbm(x), in_hbm(labels))
    lse, send, scale = pl.pallas_call(
        lse_kernel,
        out_shape=(shape(1, 256), shape(DEVS, 128), shape(DEVS, 128)),
        in_specs=[VMEM, VMEM],
        out_specs=(VMEM,) * 3,
        scratch_shapes=[pltpu.VMEM((1024, 128), f32)] * 2,
        compiler_params=params(8),
        name="normalizer",
    )(recv, sid)
    back = exchange(send)
    query_grad, loss = pl.pallas_call(
        combine_kernel,
        out_shape=(pltpu.HBM((256, 256), bf16), pltpu.HBM((1, 256), f32)),
        in_specs=[VMEM] * 5,
        out_specs=(VMEM, VMEM),
        scratch_shapes=[
            pltpu.VMEM((NGROUPS, 256), f32),
        ],
        compiler_params=params(8),
        cost_estimate=pl.CostEstimate(flops=2 * 2 * 256 * 4096 * 256, bytes_accessed=5_000_000, transcendentals=256 * 4096),
        name="combine",
    )(recv, mask, scale, lse, queries)
    new_labels, new_accum = pl.pallas_call(
        table_kernel,
        out_shape=(pltpu.HBM((16, 256, 256), f32), pltpu.HBM((16, 256), f32)),
        in_specs=[VMEM] * 4 + [HBM] * 3,
        out_specs=(HBM, HBM),
        scratch_shapes=[
            pltpu.VMEM((16, 256, 256), f32),
            pltpu.VMEM((16, 256, 256), bf16),
            pltpu.VMEM((16, 256, 256), bf16),
            pltpu.VMEM((16, 256), f32),
            pltpu.VMEM((16, 256, 256), f32),
            pltpu.VMEM((256, 128), f32),
            pltpu.VMEM((16, 256), f32),
            pltpu.SemaphoreType.DMA((3, 16 // PART)),
            pltpu.SemaphoreType.DMA((16 // PART,)),
            pltpu.SemaphoreType.DMA,
        ],
        compiler_params=params(24),
        name="table",
    )(back, top, target, acct, in_hbm(weight), in_hbm(x), in_hbm(labels))

    return (new_labels, new_accum, query_grad, loss.reshape(256))


def solution(mesh):
    return jax.shard_map(
        shards,
        mesh=mesh,
        in_specs=(
            P("shard", None), P("shard", None), P(), P("shard"), P("shard"), P("shard"),
            P("shard", None, None), P("shard", None),
        ),
        out_specs=(P("shard", None, None), P("shard", None), P("shard", None), P("shard")),
        check_vma=False,
    )
```

```python
import jax
import jax.numpy as jnp
from jax import lax
from jax.experimental import pallas as pl
from jax.experimental.pallas import tpu as pltpu
from jax.sharding import PartitionSpec as P

STEP_RATE = 0.1
DEVS = 128
GROUP = 8
SLOTS = 32
PAIRS = 24
OUT = 56
BACK = 64
NGROUPS = DEVS // GROUP
f32 = jnp.float32
bf16 = jnp.bfloat16
i32 = jnp.int32


def iota(shape, dim):
    return lax.broadcasted_iota(i32, shape, dim)


def one(mask):
    return jnp.where(mask, 1.0, 0.0).astype(bf16)


def one16(mask):
    return jnp.where(mask, jnp.ones((), bf16), jnp.zeros((), bf16))


def dot(a, b, ca=1, cb=0):
    return lax.dot_general(a, b, (((ca,), (cb,)), ((), ())), preferred_element_type=f32)


def pieces_of(x):
    hi = x.astype(bf16).astype(f32)
    rest = x - hi
    mid = rest.astype(bf16).astype(f32)
    return hi, mid, rest - mid


def total(x):
    return jnp.sum(x, axis=0, keepdims=True)


def from_rows(ref, group, chunk):
    size = GROUP * chunk
    block = ref[pl.ds(pl.multiple_of(group * size, size), size), :]
    return block.astype(f32).reshape(GROUP, chunk, 128)


def slot_rows(block, slots):
    left = block[:, :slots].reshape(GROUP * slots, 128)
    right = block[:, slots : 2 * slots].reshape(GROUP * slots, 128)
    return jnp.concatenate([left, right], axis=1).astype(bf16)


def send_block(scr, out, sems, g, chunk):
    size = GROUP * chunk
    at = pl.ds(pl.multiple_of(g * size, size), size)
    return pltpu.make_async_copy(scr.at[at, :], out.at[at, :], sems.at[g])


def route_kernel(
    cl_any, place_any, pick_any, row_any, q_any, send_any, sid_ref,
    cl_ref, place_ref, pick_ref, row_ref, q_ref, send_ref, ext_scr, in_sems, out_sems,
):
    pairs = [(cl_any, cl_ref), (place_any, place_ref), (pick_any, pick_ref), (row_any, row_ref), (q_any, q_ref)]
    copies = [pltpu.make_async_copy(a, b, in_sems.at[n]) for n, (a, b) in enumerate(pairs)]
    for copy in copies:
        copy.start()
    for copy in copies:
        copy.wait()
    c = cl_ref[...]
    ch, cl = c >> 7, c & 127
    place = place_ref[...]
    table = jnp.concatenate([(place >> 4).astype(f32), (place & 15).astype(f32)], axis=0).astype(bf16)
    i128, i16, i32s = iota((128, 256), 0), iota((16, 256), 0), iota((32, 256), 0)
    query = iota((1, 256), 1)
    queryf = query.astype(f32)
    ds, ls, ohs = [], [], []
    acc = jnp.zeros((32, 128), f32)
    for k in range(8):
        got = dot(table, one(i128 == cl[k : k + 1]))
        mine = i16 == ch[k : k + 1]
        d = total(jnp.where(mine, got[:16], 0.0)).astype(i32)
        l = total(jnp.where(mine, got[16:], 0.0)).astype(i32)
        oh = one(i128 == d)
        is_l = i16 == l
        named = jnp.concatenate([jnp.where(is_l, 1.0, 0.0), jnp.where(is_l, queryf, 0.0)], axis=0)
        acc = acc + dot(named.astype(bf16), oh, 1, 1)
        ds.append(d)
        ls.append(l)
        ohs.append(oh)
    count = acc[:16]
    middle = jnp.where(count > 1.5, jnp.floor(acc[16:] * 0.5), 255.0).astype(bf16)
    before = one(iota((256, 256), 0) < iota((256, 256), 1))
    used = jnp.zeros((128, 1), f32)
    rls, js, codes = [], [], []
    for k in range(8):
        got = dot(middle, ohs[k])
        border = total(jnp.where(i16 == ls[k], got, 0.0)).astype(i32)
        rl = jnp.where(query > border, 16, 0) + ls[k]
        ohf = ohs[k].astype(f32)
        j = total(ohf * (dot(ohs[k], before) + used)).astype(i32)
        used = used + jnp.sum(ohf, axis=1, keepdims=True)
        codes.append(jnp.where(i32s == j, (rl + 1).astype(f32), 0.0).astype(bf16))
        rls.append(rl)
        js.append(j)
    pick = pick_ref[...]
    dp = jnp.zeros((1, 256), i32)
    rlp = jnp.zeros((1, 256), i32)
    for k in range(8):
        dp = jnp.where(pick == k, ds[k], dp)
        rlp = jnp.where(pick == k, rls[k], rlp)
    ohp = one(i128 == dp)
    ohf = ohp.astype(f32)
    jp = total(ohf * (dot(ohp, before) + used)).astype(i32)
    codes.append(jnp.where(i32s == jp, (rlp + 65).astype(f32), 0.0).astype(bf16))
    code = dot(jnp.concatenate(codes, axis=1), jnp.concatenate(ohs + [ohp], axis=1), 1, 1)
    rows = dot(jnp.where(i32s == rlp, (row_ref[...] + 1).astype(f32), 0.0).astype(bf16), ohp, 1, 1)
    most = used + jnp.sum(ohf, axis=1, keepdims=True)
    full = jnp.where((used > PAIRS + 0.5) | (most > SLOTS - 0.5), 1.0, 0.0)
    full = jnp.max(full, axis=0, keepdims=True)
    ext_scr[...] = jnp.concatenate([code, rows, jnp.broadcast_to(full, (64, 128))], axis=0).T
    sid_ref[...] = jnp.concatenate(
        [d * SLOTS + j for d, j in zip(ds, js)] + rls + [dp * SLOTS + jp] + [jnp.zeros((1, 256), i32)] * 7, axis=0
    )
    sub = iota((16, 256), 0)

    def group(g, _):
        named = jnp.clip(sid_ref[:8, :] - g * 256, -1, 256).astype(f32).astype(bf16)
        named = [jnp.broadcast_to(named[k : k + 1], (16, 256)) for k in range(8)]
        strips = []
        for i in range(12):
            places = [(q // 3) * SLOTS + (q % 3) * 8 for q in (2 * i, 2 * i + 1)]
            at = (jnp.where(sub < 8, places[0], places[1] - 8) + sub).astype(f32).astype(bf16)
            mask = at == named[0]
            for k in range(1, 8):
                mask = mask | (at == named[k])
            strips.append(one16(mask))
        rows = dot(jnp.concatenate(strips, axis=0), q_ref[...])
        left = rows[:, :128].reshape(GROUP, PAIRS, 128)
        right = rows[:, 128:].reshape(GROUP, PAIRS, 128)
        extra = ext_scr[pl.ds(pl.multiple_of(g * GROUP, GROUP), GROUP), :]
        extra = jnp.broadcast_to(extra[:, None, :], (GROUP, 8, 128))
        out = jnp.concatenate([left, right, extra], axis=1).reshape(GROUP * OUT, 128).astype(bf16)
        send_ref[pl.ds(pl.multiple_of(g * GROUP * OUT, GROUP * OUT), GROUP * OUT), :] = out
        send_block(send_ref, send_any, out_sems, g, OUT).start()
        return 0

    lax.fori_loop(0, NGROUPS, group, 0, unroll=16)
    for g in range(NGROUPS):
        send_block(send_ref, send_any, out_sems, g, OUT).wait()


def slot_major(x):
    second = pltpu.roll(x, 112, 1)
    both = jnp.concatenate(
        [x.reshape(NGROUPS, 1, GROUP, 128), second.reshape(NGROUPS, 1, GROUP, 128)], axis=1
    )
    return both.reshape(256, 128)


def owner_kernel(
    counts_ref, cc_ref, recv_ref, lab_any, x_any, tr_ref, flag_ref, stat_ref, send_any,
    x_ref, lab_ref, send_ref, ext_scr, key_scr, part_scr, pos_scr, lab_sem, x_sem, out_sems,
):
    lab_copy = pltpu.make_async_copy(lab_any, lab_ref, lab_sem)
    lab_copy.start()

    def take(g, _):
        block = from_rows(recv_ref, g, OUT)
        ext_scr[pl.ds(pl.multiple_of(g * 64, 64), 64), :] = block[:, 48:56].reshape(64, 128)
        return 0

    lax.fori_loop(0, NGROUPS, take, 0, unroll=16)
    ext = ext_scr[pl.ds(0, 128, stride=8), :]
    flag_ref[0, 0] = jnp.max(ext[:, 64:65]).astype(i32)
    source, col = iota((128, 256), 0), iota((128, 256), 1)
    owner_of = jnp.floor((col.astype(f32) + 0.5) / PAIRS).astype(i32)
    spread = one(source == col - owner_of * PAIRS)
    codes = jnp.where((source & 7) == owner_of, dot(ext.astype(bf16), spread), 0.0)
    codes = jnp.sum(codes.reshape(NGROUPS, GROUP, 256), axis=1).astype(i32)
    rl = codes - 1
    keys = (rl & 15) * 16 + (rl >> 4) * 8 + owner_of[:16]
    key_scr[...] = jnp.where((codes > 0) & (codes < 64), keys, -1)
    sub = iota((16, 256), 0)

    def gather(g, _):
        block = from_rows(recv_ref, g, OUT)
        key = key_scr[pl.ds(g, 1), :]
        perm = jnp.concatenate([one(sub == key - 16 * i) for i in range(16)], axis=0)
        rows = jnp.concatenate([slot_rows(block, PAIRS), jnp.zeros((64, 256), bf16)], axis=0)
        x = dot(perm, rows).astype(bf16)
        for l in range(16):
            x_ref[l, pl.ds(pl.multiple_of(g * 16, 16), 16), :] = x[l * 16 : (l + 1) * 16]
        return 0

    lax.fori_loop(0, NGROUPS, gather, 0, unroll=4)
    x_copy = pltpu.make_async_copy(x_ref, x_any, x_sem)
    x_copy.start()
    raw = slot_major(pltpu.roll(ext, 96, 1)) - 1.0
    cc = cc_ref[...]
    tr_ref[...] = jnp.where(raw > -0.5, raw - cc * jnp.floor((raw + 0.5) / cc), -1.0)
    stat_ref[...] = jnp.zeros((256, 128), f32)
    lab_copy.wait()
    lane, wide = iota((16, 128), 1), iota((16, 256), 1)
    widef = wide.astype(f32)

    def cluster(l, _):
        lab = lab_ref[l]
        score = dot(x_ref[l], lab, 1, 1)
        valid = wide < counts_ref[l]
        weights, hits = [], []
        for i in range(16):
            at = slice(16 * i, 16 * i + 16)
            s = score[at]
            masked = jnp.where(valid, s, -jnp.inf)
            top = jnp.max(masked, axis=1, keepdims=True)
            weight = jnp.exp(masked - top)
            target = jnp.sum(jnp.where(lane == l, tr_ref[at, :], 0.0), axis=1, keepdims=True)
            hit = widef == target
            stat = jnp.where(lane == l, top, stat_ref[at, :])
            stat_ref[at, :] = jnp.where(lane == l + 16, jnp.sum(weight, axis=1, keepdims=True), stat)
            weights.append(weight.astype(bf16))
            hits.append(one(hit))
        both = dot(jnp.concatenate(weights + hits, axis=0), lab)
        part_scr[l] = both[:256].astype(bf16)
        pos_scr[l] = both[256:].astype(bf16)
        return 0

    lax.fori_loop(0, 16, cluster, 0, unroll=8)
    lane, own_row = iota((16, 128), 1), iota((16, 128), 0)
    own_sub = iota((16, 1), 0).astype(f32)
    wide = iota((16, 256), 1)
    home = ((wide & 7) * 32 + ((wide >> 3) & 1) * 16 + (wide >> 4)).astype(f32)
    last = iota((GROUP, 8, 128), 1) == 7

    def scatter(g, _):
        at = pl.ds(pl.multiple_of(g * 16, 16), 16)
        parts = jnp.concatenate([part_scr[l, at, :] for l in range(16)], axis=0)
        pos = jnp.concatenate([pos_scr[l, at, :] for l in range(16)], axis=0)
        codes = ext_scr[pl.ds(pl.multiple_of(g * 64, 64), 64), :]
        own, other = [], []
        for i in range(16):
            c = codes[8 * (i // 2) : 8 * (i // 2) + 8]
            c = jnp.concatenate([c, c], axis=0)
            c = jnp.where(lane == 16 * (i % 2) + own_row, c, 0.0)
            code = jnp.sum(c, axis=1, keepdims=True) + (32.0 * (i // 2) - 1.0)
            is_pos = code > 32.0 * (i // 2) + 50.0
            is_part = (code > 32.0 * (i // 2) - 0.5) & (code < 32.0 * (i // 2) + 50.0)
            own.append(one(home == jnp.where(is_part, code, -1.0)))
            other.append(one(home == jnp.where(is_pos, code - 64.0, -1.0)))
        rows = dot(jnp.concatenate(own, axis=0), parts) + dot(jnp.concatenate(other, axis=0), pos)
        hi, mid, lo = pieces_of(stat_ref[at, :])
        stat = hi + pltpu.roll(mid, 32, 1) + pltpu.roll(lo, 64, 1)
        halves = []
        for r in range(2):
            half = rows[:, 128 * r : 128 * r + 128].reshape(GROUP, SLOTS, 128)
            mine = jnp.broadcast_to(stat[8 * r : 8 * r + 8][:, None, :], (GROUP, 8, 128))
            halves += [half[:, :24], jnp.where(last, mine, half[:, 24:])]
        out = jnp.concatenate(halves, axis=1).reshape(GROUP * BACK, 128).astype(bf16)
        send_ref[pl.ds(pl.multiple_of(g * GROUP * BACK, GROUP * BACK), GROUP * BACK), :] = out
        send_block(send_ref, send_any, out_sems, g, BACK).start()
        return 0

    lax.fori_loop(0, NGROUPS, scatter, 0, unroll=16)
    x_copy.wait()
    for g in range(NGROUPS):
        send_block(send_ref, send_any, out_sems, g, BACK).wait()


def ready_kernel(
    counts_ref, sid_ref, stat_ref, trc_ref, acc_ref, x_any, lab_any,
    mask_ref, acct_ref, top_ref, tr_ref, weight_any, x_ref, lab_ref, weight_ref, sems,
):
    copies = [pltpu.make_async_copy(x_any, x_ref, sems.at[0]), pltpu.make_async_copy(lab_any, lab_ref, sems.at[1])]
    for copy in copies:
        copy.start()
    for copy in copies:
        copy.wait()
    acct_ref[...] = jnp.concatenate([acc_ref[...], jnp.zeros((112, 256), f32)], axis=0).T
    top_ref[...] = stat_ref[...].T[:16]
    r256 = iota((256, 256), 0)
    tr_ref[...] = trc_ref[...].T[:16]
    cols = jnp.concatenate([sid_ref[...].astype(f32), jnp.zeros((104, 256), f32)], axis=0).T
    lane = iota((256, 256), 1).astype(f32)

    def step(n, _):
        slot = lane + (n * 256).astype(f32)
        mask = cols[:, 0:1] == slot
        for k in range(1, 8):
            mask = mask | (cols[:, k : k + 1] == slot)
        pos = jnp.where(cols[:, 16:17] == slot, -1.0, 0.0)
        mask_ref[n] = jnp.where(mask, 1.0, pos).astype(bf16)
        score = dot(lab_ref[n], x_ref[n], 1, 1)
        weight_ref[n] = jnp.where(r256 < counts_ref[n], jnp.exp(score - top_ref[pl.ds(n, 1), :]), 0.0)
        return 0

    lax.fori_loop(0, NGROUPS, step, 0)
    copy = pltpu.make_async_copy(weight_ref, weight_any, sems.at[0])
    copy.start()
    copy.wait()


def spread_pairs(values, rows, ohs):
    i32s = iota((32, 256), 0)
    outs = []
    for value, row, _ in zip(values, rows, ohs):
        outs.append(jnp.concatenate([jnp.where(i32s == row, p, 0.0) for p in pieces_of(value)], axis=0).astype(bf16))
    out = dot(jnp.concatenate(outs, axis=1), jnp.concatenate(ohs, axis=1), 1, 1)
    return out[:32] + out[32:64] + out[64:]


def lse_kernel(recv_ref, sid_ref, lse_ref, send_ref, scale_ref, left_scr, right_scr):
    def take(g, _):
        block = from_rows(recv_ref, g, BACK)
        at = pl.ds(pl.multiple_of(g * 64, 64), 64)
        left_scr[at, :] = block[:, 24:32].reshape(64, 128)
        right_scr[at, :] = block[:, 56:64].reshape(64, 128)
        return 0

    lax.fori_loop(0, NGROUPS, take, 0, unroll=16)
    stats = [scr[pl.ds(7, 128, stride=8), :].T for scr in (left_scr, right_scr)]
    table = jnp.concatenate(stats, axis=0).astype(bf16)
    i128, i16 = iota((128, 256), 0), iota((16, 256), 0)
    sid = sid_ref[...]
    tops, sums, ohs = [], [], []
    for k in range(8):
        rl = sid[8 + k : 9 + k]
        oh = one(i128 == (sid[k : k + 1] >> 5))
        got = dot(table, oh)
        got = jnp.where((rl & 16) == 0, got[:128], got[128:])
        mine = i16 == (rl & 15)
        tops.append(total(jnp.where(mine, got[:16] + got[32:48] + got[64:80], 0.0)))
        sums.append(total(jnp.where(mine, got[16:32] + got[48:64] + got[80:96], 0.0)))
        ohs.append(oh)
    largest = tops[0]
    for k in range(1, 8):
        largest = jnp.maximum(largest, tops[k])
    norm = sums[0] * jnp.exp(tops[0] - largest)
    for k in range(1, 8):
        norm = norm + sums[k] * jnp.exp(tops[k] - largest)
    lse = largest + jnp.log(norm)
    lse_ref[...] = lse
    scale_ref[...] = jnp.concatenate([jnp.exp(t - lse) for t in tops], axis=0)
    out = spread_pairs([lse] * 8, [sid[8 + k : 9 + k] for k in range(8)], ohs)
    send_ref[...] = jnp.concatenate([out, jnp.zeros((96, 128), f32)], axis=0).T


def combine_kernel(recv_ref, mask_ref, scale_ref, sid_ref, lse_ref, q_ref, out_ref, loss_ref, row_scr):
    sid = sid_ref[...]
    ohs = [one(iota((128, 256), 0) == (sid[k : k + 1] >> 5)) for k in range(8)]
    scales = spread_pairs([scale_ref[k : k + 1, :] for k in range(8)], [sid[k : k + 1] & 31 for k in range(8)], ohs)
    scales = jnp.concatenate([scales, jnp.zeros((96, 128), f32)], axis=0).T
    r256, c256 = iota((128, 256), 0), iota((128, 256), 1)
    spread = one((r256 == (c256 & 31)) & (r256 < 32))
    wide = jnp.zeros((128, 256), f32)
    for piece in pieces_of(scales):
        wide = wide + dot(piece.astype(bf16), spread)
    wide = jnp.where((r256 & 7) == (c256 >> 5), wide, 0.0)
    row_scr[...] = jnp.sum(wide.reshape(NGROUPS, GROUP, 256), axis=1)

    def group(g, accs):
        acc, pos = accs
        rows = slot_rows(from_rows(recv_ref, g, BACK), SLOTS)
        scale = row_scr[pl.ds(g, 1), :]
        his, los, places = [], [], []
        for i in range(16):
            mask = mask_ref[g, 16 * i : 16 * i + 16, :].astype(f32)
            a = jnp.where(mask > 0.5, scale, 0.0)
            hi = a.astype(bf16)
            his.append(hi)
            los.append((a - hi.astype(f32)).astype(bf16))
            places.append(one(mask < -0.5))
        acc = acc + (dot(jnp.concatenate(his, axis=0), rows) + dot(jnp.concatenate(los, axis=0), rows))
        return acc, pos + dot(jnp.concatenate(places, axis=0), rows)

    zero = jnp.zeros((256, 256), f32)
    acc, pos = lax.fori_loop(0, NGROUPS, group, (zero, zero), unroll=4)
    out_ref[...] = (acc - pos).astype(bf16)
    score = jnp.sum(q_ref[...].astype(f32) * pos, axis=1, keepdims=True)
    loss_ref[...] = lse_ref[...] - jnp.broadcast_to(score, (256, 128)).T[:1]


PART = 4


def table_kernel(
    lse_ref, top_ref, tr_ref, acct_ref, weight_any, x_any, lab_any, new_any, nacc_any,
    weight_ref, x_ref, lab_ref, fac_scr, new_scr, out_scr, nacc_ref, in_sems, out_sems, nacc_sem,
):
    def inputs_of(p):
        at = pl.ds(p * PART, PART)
        pairs = [(weight_any, weight_ref), (x_any, x_ref), (lab_any, lab_ref)]
        return [pltpu.make_async_copy(a.at[at], b.at[at], in_sems.at[n, p]) for n, (a, b) in enumerate(pairs)]

    def output_of(p):
        at = pl.ds(p * PART, PART)
        return pltpu.make_async_copy(new_scr.at[at], new_any.at[at], out_sems.at[p])

    for p in range(16 // PART):
        for copy in inputs_of(p):
            copy.start()
    fac_scr[...] = jnp.exp(top_ref[...] - slot_major(lse_ref[...]).T[:16])
    out_scr[...] = jnp.zeros((256, 128), f32)
    rowf = iota((16, 256), 0).astype(f32)
    lane = iota((16, 128), 1)

    def part(p, _):
        for copy in inputs_of(p):
            copy.wait()
        for q in range(PART):
            l = p * PART + q
            fac = fac_scr[pl.ds(l, 1), :]
            target = tr_ref[pl.ds(l, 1), :]
            strips = []
            for i in range(16):
                hit = rowf == target - 16.0 * i
                strips.append((weight_ref[l, 16 * i : 16 * i + 16, :] * fac - jnp.where(hit, 1.0, 0.0)).astype(bf16))
            grad = dot(jnp.concatenate(strips, axis=0), x_ref[l])
            for i in range(16):
                at = slice(16 * i, 16 * i + 16)
                g = grad[at]
                square = g * g
                both = (square[:, :128] + square[:, 128:]) * (1.0 / 256.0)
                both = both + jnp.where(lane == l, acct_ref[at, :], 0.0)
                accum = jnp.sum(both, axis=1, keepdims=True)
                new_scr[l, at, :] = lab_ref[l, at, :].astype(f32) - g * (STEP_RATE / jnp.sqrt(accum))
                out_scr[at, :] = jnp.where(lane == l, accum, out_scr[at, :])
        output_of(p).start()
        return 0

    lax.fori_loop(0, 16 // PART, part, 0)
    nacc_ref[...] = out_scr[...].T[:16]
    nacc_copy = pltpu.make_async_copy(nacc_ref, nacc_any, nacc_sem)
    nacc_copy.start()
    nacc_copy.wait()
    for p in range(16 // PART):
        output_of(p).wait()


def params(mib):
    return pltpu.CompilerParams(vmem_limit_bytes=mib * 1024 * 1024)


def shape(*dims, dtype=f32):
    return jax.ShapeDtypeStruct(dims, dtype)


VMEM = pl.BlockSpec(memory_space=pltpu.VMEM)
SMEM = pl.BlockSpec(memory_space=pltpu.SMEM)
HBM = pl.BlockSpec(memory_space=pltpu.HBM)


def in_hbm(x):
    return pltpu.with_memory_space_constraint(x, pltpu.HBM)


def exchange(x):
    return lax.all_to_all(x, "shard", split_axis=0, concat_axis=0, tiled=True)


def ranks_of(keys):
    order = jnp.argsort(keys, stable=True)
    sorted_keys = keys[order]
    places = jnp.arange(keys.shape[0], dtype=jnp.int32)
    starts = jnp.where((places == 0) | (sorted_keys != jnp.roll(sorted_keys, 1)), places, 0)
    starts = lax.cummax(starts)
    return jnp.zeros_like(keys).at[order].set(places - starts)


def scoring(recv_q, labels):
    return jnp.einsum("csw,clw->csl", recv_q, labels, preferred_element_type=jnp.float32)


def owner_share(score, top, valid, labels):
    weight = jnp.where(valid, jnp.exp(score - top[..., None]), 0.0).astype(jnp.bfloat16)
    return jnp.einsum("csl,clw->csw", weight, labels, preferred_element_type=jnp.float32).astype(
        jnp.bfloat16
    )


def send_back(share, pos_rows, devices):
    local_blocks, slot_rows, width = share.shape
    shaped = (local_blocks, devices, slot_rows // devices, width)
    return (
        lax.all_to_all(share.reshape(shaped), "shard", split_axis=1, concat_axis=1, tiled=True),
        lax.all_to_all(pos_rows.reshape(shaped), "shard", split_axis=1, concat_axis=1, tiled=True),
    )


def general(queries, clusters, placement, pos_pick, pos_row, counts, labels, accum):
    devices = lax.axis_size("shard")
    rows_dev, width = queries.shape
    per_query = clusters.shape[1]
    local_blocks, block_rows, _ = labels.shape
    most_rows = max(2, 2 * rows_dev * per_query // (local_blocks * devices))
    all_slots = local_blocks * devices * most_rows
    slot_rows = devices * most_rows
    flat = clusters.reshape(-1)
    rank = ranks_of(flat)
    block_ids = placement[flat]
    dest = block_ids // local_blocks
    local_id = block_ids % local_blocks
    where_to = (local_id * devices + dest) * most_rows + rank
    picked = jnp.arange(per_query, dtype=jnp.int32)[None, :] == pos_pick[:, None]
    target = jnp.where(picked, pos_row[:, None], -1).reshape(-1)
    send_q = (
        jnp.zeros((all_slots, width), jnp.bfloat16)
        .at[where_to]
        .set(jnp.repeat(queries, per_query, axis=0))
    )
    send_t = jnp.full((all_slots,), -1, jnp.int32).at[where_to].set(target)
    recv_q, recv_t = (
        lax.all_to_all(
            send_q.reshape(local_blocks, devices, most_rows, width),
            "shard",
            split_axis=1,
            concat_axis=1,
            tiled=True,
        ),
        lax.all_to_all(
            send_t.reshape(local_blocks, devices, most_rows),
            "shard",
            split_axis=1,
            concat_axis=1,
            tiled=True,
        ),
    )
    recv_q = recv_q.reshape(local_blocks, slot_rows, width)
    recv_t = recv_t.reshape(local_blocks, slot_rows)
    row_ids = jnp.arange(block_rows, dtype=jnp.int32)
    valid = row_ids[None, None, :] < counts[:, None, None]
    target_row = jnp.where(recv_t >= 0, recv_t % counts[:, None], -1)
    hit = row_ids[None, None, :] == target_row[..., None]
    score = scoring(recv_q, labels)
    masked = jnp.where(valid, score, -jnp.inf)
    top = jnp.max(masked, axis=-1)
    total = jnp.sum(jnp.exp(masked - top[..., None]), axis=-1)
    spos = jnp.sum(jnp.where(hit, score, 0.0), axis=-1)
    pos_rows = jnp.einsum(
        "csl,clw->csw", hit.astype(jnp.bfloat16), labels, preferred_element_type=jnp.float32
    ).astype(jnp.bfloat16)
    stat_shape = (local_blocks, devices, most_rows)
    back_m, back_z, back_s = (
        lax.all_to_all(top.reshape(stat_shape), "shard", split_axis=1, concat_axis=1, tiled=True),
        lax.all_to_all(total.reshape(stat_shape), "shard", split_axis=1, concat_axis=1, tiled=True),
        lax.all_to_all(spos.reshape(stat_shape), "shard", split_axis=1, concat_axis=1, tiled=True),
    )
    pair_m = back_m.reshape(-1)[where_to].reshape(rows_dev, per_query)
    pair_z = back_z.reshape(-1)[where_to].reshape(rows_dev, per_query)
    pair_s = back_s.reshape(-1)[where_to].reshape(rows_dev, per_query)
    largest = jnp.max(pair_m, axis=1)
    norm = jnp.sum(pair_z * jnp.exp(pair_m - largest[:, None]), axis=1)
    lse = largest + jnp.log(norm)
    loss = lse - jnp.sum(pair_s, axis=1)
    send_l = jnp.zeros((all_slots,), jnp.float32).at[where_to].set(jnp.repeat(lse, per_query))
    recv_l = lax.all_to_all(
        send_l.reshape(stat_shape), "shard", split_axis=1, concat_axis=1, tiled=True
    ).reshape(local_blocks, slot_rows)
    prob = jnp.where(valid, jnp.exp(score - recv_l[..., None]), 0.0)
    dlogit = (prob - hit.astype(jnp.float32)).astype(jnp.bfloat16)
    label_grad = jnp.einsum("csl,csw->clw", dlogit, recv_q, preferred_element_type=jnp.float32)
    returned, returned_pos = send_back(owner_share(score, top, valid, labels), pos_rows, devices)
    pieces = (
        returned.reshape(all_slots, width)[where_to]
        .astype(jnp.float32)
        .reshape(rows_dev, per_query, width)
    )
    pos_pieces = (
        returned_pos.reshape(all_slots, width)[where_to]
        .astype(jnp.float32)
        .reshape(rows_dev, per_query, width)
    )
    scale = jnp.exp(pair_m - lse[:, None])
    query_grad = (jnp.sum(pieces * scale[..., None], axis=1) - jnp.sum(pos_pieces, axis=1)).astype(
        jnp.bfloat16
    )
    new_accum = accum + jnp.mean(label_grad * label_grad, axis=-1)
    new_labels = (
        labels.astype(jnp.float32) - STEP_RATE * label_grad / jnp.sqrt(new_accum)[..., None]
    )
    return (new_labels, new_accum, query_grad, loss)


def shards(queries, clusters, placement, pos_pick, pos_row, counts, labels, accum):
    send, sid = pl.pallas_call(
        route_kernel,
        out_shape=(pltpu.HBM((DEVS * OUT, 128), bf16), pltpu.VMEM((24, 256), i32)),
        in_specs=[HBM] * 5,
        out_specs=(HBM, VMEM),
        scratch_shapes=[
            pltpu.VMEM((8, 256), i32),
            pltpu.VMEM((16, 128), i32),
            pltpu.VMEM((1, 256), i32),
            pltpu.VMEM((1, 256), i32),
            pltpu.VMEM((256, 256), bf16),
            pltpu.VMEM((DEVS * OUT, 128), bf16),
            pltpu.VMEM((128, 128), f32),
            pltpu.SemaphoreType.DMA((5,)),
            pltpu.SemaphoreType.DMA((NGROUPS,)),
        ],
        compiler_params=params(16),
        name="route",
    )(
        in_hbm(clusters.T), in_hbm(placement.reshape(16, 128)), in_hbm(pos_pick.reshape(1, 256)),
        in_hbm(pos_row.reshape(1, 256)), in_hbm(queries),
    )
    recv = exchange(send)
    lanes = jnp.concatenate([counts.astype(f32), jnp.ones((112,), f32)]).reshape(1, 128)
    x, slot_target, flag, stat, send = pl.pallas_call(
        owner_kernel,
        out_shape=(
            pltpu.HBM((16, 256, 256), bf16), pltpu.VMEM((256, 128), f32), shape(1, 1, dtype=i32), pltpu.VMEM((256, 128), f32),
            pltpu.HBM((DEVS * BACK, 128), bf16),
        ),
        in_specs=[SMEM, VMEM, VMEM, HBM],
        out_specs=(HBM, VMEM, SMEM, VMEM, HBM),
        scratch_shapes=[
            pltpu.VMEM((16, 256, 256), bf16),
            pltpu.VMEM((16, 256, 256), bf16),
            pltpu.VMEM((DEVS * BACK, 128), bf16),
            pltpu.VMEM((1024, 128), f32),
            pltpu.VMEM((16, 256), i32),
            pltpu.VMEM((16, 256, 256), bf16),
            pltpu.VMEM((16, 256, 256), bf16),
            pltpu.SemaphoreType.DMA,
            pltpu.SemaphoreType.DMA,
            pltpu.SemaphoreType.DMA((NGROUPS,)),
        ],
        compiler_params=params(24),
        name="owner",
    )(counts, lanes, recv, in_hbm(labels))

    def plain():
        return general(queries, clusters, placement, pos_pick, pos_row, counts, labels, accum)

    def packed():
        return finish(queries, counts, labels, accum, sid, x, slot_target, stat, send)

    return lax.switch(flag[0, 0], [packed, plain])


def finish(queries, counts, labels, accum, sid, x, slot_target, stat, send):
    recv = exchange(send)
    mask, acct, top, target, weight = pl.pallas_call(
        ready_kernel,
        out_shape=(
            pltpu.VMEM((NGROUPS, 256, 256), bf16), pltpu.VMEM((256, 128), f32), pltpu.VMEM((16, 256), f32),
            pltpu.VMEM((16, 256), f32), pltpu.HBM((16, 256, 256), f32),
        ),
        in_specs=[SMEM] + [VMEM] * 4 + [HBM] * 2,
        out_specs=(VMEM,) * 4 + (HBM,),
        scratch_shapes=[
            pltpu.VMEM((16, 256, 256), bf16),
            pltpu.VMEM((16, 256, 256), bf16),
            pltpu.VMEM((16, 256, 256), f32),
            pltpu.SemaphoreType.DMA((2,)),
        ],
        compiler_params=params(16),
        cost_estimate=pl.CostEstimate(flops=2 * 16 * 256**3, bytes_accessed=10_000_000, transcendentals=16 * 256**2),
        name="ready",
    )(counts, sid, stat, slot_target, accum, in_hbm(x), in_hbm(labels))
    lse, send, scale = pl.pallas_call(
        lse_kernel,
        out_shape=(shape(1, 256), shape(DEVS, 128), shape(8, 256)),
        in_specs=[VMEM, VMEM],
        out_specs=(VMEM,) * 3,
        scratch_shapes=[pltpu.VMEM((1024, 128), f32)] * 2,
        compiler_params=params(8),
        name="normalizer",
    )(recv, sid)
    back = exchange(send)
    query_grad, loss = pl.pallas_call(
        combine_kernel,
        out_shape=(pltpu.HBM((256, 256), bf16), pltpu.HBM((1, 256), f32)),
        in_specs=[VMEM] * 6,
        out_specs=(VMEM, VMEM),
        scratch_shapes=[
            pltpu.VMEM((NGROUPS, 256), f32),
        ],
        compiler_params=params(8),
        cost_estimate=pl.CostEstimate(flops=2 * 2 * 256 * 4096 * 256, bytes_accessed=5_000_000, transcendentals=256 * 4096),
        name="combine",
    )(recv, mask, scale, sid, lse, queries)
    new_labels, new_accum = pl.pallas_call(
        table_kernel,
        out_shape=(pltpu.HBM((16, 256, 256), f32), pltpu.HBM((16, 256), f32)),
        in_specs=[VMEM] * 4 + [HBM] * 3,
        out_specs=(HBM, HBM),
        scratch_shapes=[
            pltpu.VMEM((16, 256, 256), f32),
            pltpu.VMEM((16, 256, 256), bf16),
            pltpu.VMEM((16, 256, 256), bf16),
            pltpu.VMEM((16, 256), f32),
            pltpu.VMEM((16, 256, 256), f32),
            pltpu.VMEM((256, 128), f32),
            pltpu.VMEM((16, 256), f32),
            pltpu.SemaphoreType.DMA((3, 16 // PART)),
            pltpu.SemaphoreType.DMA((16 // PART,)),
            pltpu.SemaphoreType.DMA,
        ],
        compiler_params=params(24),
        name="table",
    )(back, top, target, acct, in_hbm(weight), in_hbm(x), in_hbm(labels))

    return (new_labels, new_accum, query_grad, loss.reshape(256))


def solution(mesh):
    return jax.shard_map(
        shards,
        mesh=mesh,
        in_specs=(
            P("shard", None), P("shard", None), P(), P("shard"), P("shard"), P("shard"),
            P("shard", None, None), P("shard", None),
        ),
        out_specs=(P("shard", None, None), P("shard", None), P("shard", None), P("shard")),
        check_vma=False,
    )
```
